512 devices in a mesh: rows: 128 (over y, z, core), rep: 4 (over x).
Axes of the slice: x: 4, y: 4, z: 16, core: 2. Of those that a mesh axis runs over, the one named last changes fastest.
Arguments:
- feats: bfloat16 [32768, 128], P('rows'), may hold values from -6 to 6
- edge_w: bfloat16 [32768, 8192], P('rows', 'rep'), may hold values from -0.09375 to 0.09375
- send_rows: int32 [128, 128, 64], P('rows', None, 'rep'), may hold values from 0 to 255
- counts: int32 [128, 128], P('rows'), may hold values from 0 to 64, as said below
- w_one: bfloat16 [128, 256], replicated, may hold values from -0.5 to 0.5
- w_two: bfloat16 [256, 256], replicated, may hold values from -0.375 to 0.375
- cotangent: bfloat16 [32768, 256], P('rows'), may hold values from -0.03125 to 0.03125
Outputs:
- output: bfloat16 [32768, 256], P('rows')
- grad_w1: float32 [128, 256], replicated
- grad_w2: float32 [256, 256], replicated
The draws below stay inside these ranges and needn't reach their ends.
Inputs may be any that keep to these rules, and one draw needn't show every extreme that they name: `counts`: every receiving block has a source block with all 64 slots live.
All inputs are finite; a program needn't handle non-finite values.
Results may differ from the reference program's by a relative error of at most 0.02.
Values may be sent and summed in bfloat16 or wider, within the bound.
A program may use at most 64 MiB of HBM per device.

```python
import jax
import jax.numpy as jnp
from jax import lax

F = 128
HID = 256
BLK = 256
SUB = 64
NB = 128
NODES = 32768


def draw_counts(key, part):
    key = jax.random.fold_in(key, 7)
    key_base, key_top, key_low = jax.random.split(key, 3)
    base = jax.random.randint(key_base, (NB, NB), 0, SUB + 1)
    top_column = jax.random.randint(key_top, (NB, 1), 0, NB)
    low_column = jax.random.randint(key_low, (NB, 1), 0, NB)
    columns = jnp.arange(NB, dtype=jnp.int32)[None, :]
    base = jnp.where(columns == low_column, 0, base)
    base = jnp.where(columns == top_column, SUB, base)
    return base.astype(jnp.int32)


def plant(entries, rng, smallest, largest):
    index_at = [jax.random.randint(jax.random.fold_in(rng, axis), (), 0, length) for axis, length in enumerate(entries.shape)]
    main_axis = entries.shape.index(max(entries.shape))
    beside = index_at[:main_axis] + [(index_at[main_axis] + 1) % entries.shape[main_axis]] + index_at[main_axis + 1:]
    return entries.at[tuple(index_at)].set(smallest).at[tuple(beside)].set(largest)


def block_levels(key, dims, cuts, low, largest):
    loudness = 1.0
    for dim, blocks in cuts:
        steps = jax.random.uniform(jax.random.fold_in(jax.random.fold_in(key, 6), dim), (blocks,), jnp.float32, low / len(cuts), largest / len(cuts))
        loudness = loudness * jnp.repeat(jnp.exp(steps), dims[dim] // blocks).reshape((-1,) + (1,) * (len(dims) - 1 - dim))
    return loudness


def centred(key, shape, scale, limit, cuts=(), kind=jnp.bfloat16):
    result = scale * jax.random.normal(key, shape, jnp.float32)
    if cuts:
        result = result * block_levels(key, shape, cuts, -0.22, 0.18)
    return jnp.clip(result, -limit, limit).astype(kind)


def setup_inputs(seed: int = 0) -> dict:
    splits = jax.random.split(jax.random.key(seed), 8)
    return {
        "feats": centred(splits[0], (NODES, F), 1.0, 6.0, ((0, 128),)),
        "edge_w": centred(splits[1], (NODES, SUB * NB), (NB * SUB // 2) ** -0.5, 0.09375, ((0, 128), (1, 4))),
        "send_rows": plant(jax.random.randint(splits[2], (NB, NB, SUB), 0, BLK), jax.random.fold_in(splits[2], 1), 0, BLK - 1).astype(jnp.int32),
        "counts": draw_counts(jax.random.fold_in(splits[7], 71), 0),
        "w_one": centred(splits[4], (F, HID), F ** -0.5, 0.5),
        "w_two": centred(splits[5], (HID, HID), HID ** -0.5, 0.375),
        "cotangent": centred(splits[6], (NODES, HID), NODES ** -0.5, 0.03125, ((0, 128),)),
    }


def slot_mask(counts):
    slot_ids = jnp.arange(SUB, dtype=jnp.int32)
    return (slot_ids[None, None, :] < counts[:, :, None]).astype(jnp.bfloat16)


def silu_slope(values):
    sigma = jax.nn.sigmoid(values)
    return sigma * (1.0 + values * (1.0 - sigma))


def aggregate(values, edge_w, send_rows, live_slots):
    feature_width = values.shape[1]
    blocks = values.reshape(NB, BLK, feature_width)
    sources = jnp.arange(NB, dtype=jnp.int32)

    def one_block(block_id):
        source_rows = send_rows[:, block_id, :]
        picked = blocks[sources[:, None], source_rows]
        edge_rows = lax.dynamic_slice_in_dim(edge_w, block_id * BLK, BLK, 0).reshape(BLK, SUB, NB)
        weights = jnp.transpose(edge_rows, (0, 2, 1)) * live_slots[block_id][None, :, :]
        return jnp.dot(weights.reshape(BLK, NB * SUB), picked.reshape(NB * SUB, feature_width),
                       preferred_element_type=jnp.float32)

    return lax.map(one_block, sources).reshape(NB * BLK, feature_width)


def transpose_aggregate(grads, edge_w, send_rows, live_slots):
    feature_width = grads.shape[1]
    blocks = grads.reshape(NB, BLK, feature_width).astype(jnp.float32)
    edge_grid = edge_w.reshape(NB, BLK, SUB, NB)

    def one_source(block_id):
        picked = lax.dynamic_index_in_dim(edge_grid, block_id, 3, keepdims=False)
        weights = (picked * live_slots[:, block_id, :][:, None, :]).astype(jnp.float32)
        slot_terms = jnp.einsum("ips,iph->ish", weights, blocks)
        return jax.ops.segment_sum(slot_terms.reshape(NB * SUB, feature_width),
                                   send_rows[block_id].reshape(NB * SUB), num_segments=BLK)

    return lax.map(one_source, jnp.arange(NB, dtype=jnp.int32)).reshape(NB * BLK, feature_width)


def reference(feats, edge_w, send_rows, counts, w_one, w_two, cotangent):
    live_slots = slot_mask(counts)
    agg_one = aggregate(feats, edge_w, send_rows, live_slots).astype(jnp.bfloat16)
    z_one = jnp.dot(agg_one, w_one, preferred_element_type=jnp.float32)
    hidden = jax.nn.silu(z_one).astype(jnp.bfloat16)
    agg_two = aggregate(hidden, edge_w, send_rows, live_slots).astype(jnp.bfloat16)
    z_two = jnp.dot(agg_two, w_two, preferred_element_type=jnp.float32)
    output = jax.nn.silu(z_two).astype(jnp.bfloat16)
    dz_two = (cotangent.astype(jnp.float32) * silu_slope(z_two)).astype(jnp.bfloat16)
    grad_w2 = jnp.dot(agg_two.T, dz_two, preferred_element_type=jnp.float32)
    back_two = jnp.dot(dz_two, w_two.T, preferred_element_type=jnp.float32).astype(jnp.bfloat16)
    d_hidden = transpose_aggregate(back_two, edge_w, send_rows, live_slots)
    dz_one = (d_hidden * silu_slope(z_one)).astype(jnp.bfloat16)
    grad_w1 = jnp.dot(agg_one.T, dz_one, preferred_element_type=jnp.float32)
    return (output, grad_w1, grad_w2)
```

```python
import functools

import jax
import jax.numpy as jnp
from jax import lax
from jax.experimental import pallas as pl
from jax.experimental.pallas import tpu as pltpu
from jax.sharding import PartitionSpec as P

MESH = pl.DeviceIdType.MESH
BF = jnp.bfloat16
F32 = jnp.float32


def dot(a, b, ca=1, cb=0):
    return lax.dot_general(a, b, (((ca,), (cb,)), ((), ())), preferred_element_type=F32)


def silu_slope(values):
    sigma = jax.nn.sigmoid(values)
    return sigma * (1.0 + values * (1.0 - sigma))


def kernel(
    feats, idxt, cnt, w, w1, w2, cot,
    out, gr1, gr2,
    wtf, wtb, wr, stage, g1, acc1, rb1, sw, g2, acc2, rb2, dd, dt, bk, st0, rsb, ys, yb,
    ga, gb, gy, gz, gt, gq,
    sw_s, sw_r, wx_s, wx_r, y1_s, y1_r, z1_s, z1_r, r1_s, r1_r, sx_s, sx_r, y2_s, y2_r, z2_s, z2_r,
    r2_s, r2_r, ox_s, ox_r, bx_s, bx_r, rs_s, rs_r, ry_s, ry_r,
    ga_s, ga_r, gy_s, gy_r, gz_s, gz_r, gt_s, gt_r, gq_s, gq_r,
):
    r = lax.axis_index("rows")
    x = lax.axis_index("rep")
    core = lax.rem(r, 2)
    z = lax.rem(lax.div(r, 2), 16)
    y = lax.div(r, 32)
    zh = lax.div(z, 8)
    zl = lax.rem(z, 8)
    q = core * 4 + x

    def rid(yy, zz, cc):
        return (yy * 16 + zz) * 2 + cc

    def peer8(m):
        pq = lax.rem(q + m, 8)
        pc, px = lax.div(pq, 4), lax.rem(pq, 4)
        return pq, rid(y, z, pc), px

    def zpeer(m):
        return rid(y, lax.rem(z + m, 16), core)

    def ypeer(m):
        return rid(lax.rem(y + m, 4), z, core)

    def copy(src, dst, ssem, rsem, rows, rep):
        return pltpu.make_async_remote_copy(
            src_ref=src, dst_ref=dst, send_sem=ssem, recv_sem=rsem,
            device_id={"rows": rows, "rep": rep}, device_id_type=MESH,
        )

    alone = jnp.logical_and(x == y, core == zh)
    part_r, part_x = rid(x, core * 8 + zl, zh), y

    barrier = pltpu.get_barrier_semaphore()

    def greet(rows, rep):
        pl.semaphore_signal(barrier, inc=1, device_id={"rows": rows, "rep": rep}, device_id_type=MESH)

    for m in range(1, 8):
        _, pr, px = peer8(m)
        greet(pr, px)
    for m in range(1, 4):
        greet(ypeer(m), x)
    for m in range(1, 16):
        greet(zpeer(m), x)

    @pl.when(jnp.logical_not(alone))
    def _():
        greet(part_r, part_x)

    stage[0:64, :] = feats[pl.ds(pl.multiple_of(x * 64, 64), 64), :]
    stage[64:80, :] = idxt[...].astype(F32).astype(BF)

    pl.semaphore_wait(barrier, 26 - alone.astype(jnp.int32))

    def swap(src, dst, ssem, rsem):
        @pl.when(alone)
        def _():
            dst[...] = src[...]

        c = copy(src, dst, ssem, rsem, part_r, part_x)

        @pl.when(jnp.logical_not(alone))
        def _():
            c.start()

        def finish():
            @pl.when(jnp.logical_not(alone))
            def _():
                c.wait()

        return finish

    swap_done = swap(stage, g1.at[core * 8 + zl, x], sw_s, sw_r)

    for s in range(16):
        t = jnp.where(cnt[...] > x * 16 + s, w[:, s * 128:(s + 1) * 128].astype(F32), 0.0)
        tt = t.T
        for half in range(2):
            wtf[half, pl.ds(s, 128, stride=16), :] = tt[:, half * 128:(half + 1) * 128]
    for half in range(2):
        wtb[:, :, half * 128:(half + 1) * 128] = wtf[half].astype(BF).reshape(128, 16, 128)

    wcopies = []
    for m in range(1, 8):
        pq, pr, px = peer8(m)
        group = px * 2 + lax.div(pq, 4)
        c = copy(wtb.at[pl.ds(group * 16, 16)], wr.at[core, :, x], wx_s.at[m], wx_r.at[m], pr, px)
        c.start()
        wcopies.append(c)
    wr[core, :, x] = wtb[pl.ds((x * 2 + core) * 16, 16)]

    swap_done()

    def gather_y(g, ssem, rsem):
        cs = []
        for m in range(1, 4):
            c = copy(g.at[z, y], g.at[z, y], ssem.at[m], rsem.at[m], ypeer(m), x)
            c.start()
            cs.append(c)
        for c in cs:
            c.wait()

    def zslot(m):
        return lax.rem(z + m + 16, 16)

    def gather_z(g, ssem, rsem, process):
        def hop(d, s, chunk):
            slot = zslot(-s) if d == 0 else zslot(s)
            return copy(g.at[slot, chunk], g.at[slot, chunk], ssem.at[d, s, chunk], rsem.at[d, s, chunk],
                        zpeer(1 if d == 0 else 15), x)

        for chunk in range(4):
            for d in range(2):
                hop(d, 0, chunk).start()
        process(z)

        def body(s, _):
            for chunk in range(4):
                for d in range(2):
                    hop(d, s, chunk).wait_recv()
                    hop(d, s + 1, chunk).start()
            process(zslot(-1 - s))
            process(zslot(1 + s))
            return 0

        lax.fori_loop(0, 6, body, 0)
        for chunk in range(4):
            for d in range(2):
                hop(d, 6, chunk).wait_recv()
                if chunk // 2 == d:
                    hop(d, 7, chunk).start()
        process(zslot(-7))
        process(zslot(7))
        for chunk in range(4):
            hop(chunk // 2, 7, chunk).wait_recv()
        process(zslot(8))

        def sent(s, _):
            for chunk in range(4):
                for d in range(2):
                    hop(d, s, chunk).wait_send()
            return 0

        lax.fori_loop(0, 7, sent, 0)
        for chunk in range(4):
            hop(chunk // 2, 7, chunk).wait_send()

    gather_y(g1, y1_s, y1_r)

    for c in wcopies:
        c.wait()

    i0 = r - core
    lane = lax.broadcasted_iota(jnp.int32, (64, 256), 1).astype(F32)
    row_i = lax.broadcasted_iota(jnp.int32, (128, 256), 0)
    acc1[...] = jnp.zeros_like(acc1)

    def process1(slot):
        c16 = lax.rem(slot, 8) * 2 + lax.div(slot, 8)
        rows = g1[slot, :, 64:80, :].reshape(64, 128)
        vals = g1[slot, :, 0:64, :].reshape(256, 128)
        for g in range(2):
            pick = (row_i == i0 + g).astype(F32).astype(BF)
            oh = (dot(rows, pick) == lane).astype(F32).astype(BF)
            ww = wr[g, c16].reshape(64, 256)
            d = dot(ww, oh, 0, 0).astype(BF)
            dd[slot, g * 256:(g + 1) * 256, :] = d
            dt[slot, :, g * 256:(g + 1) * 256] = dot(oh, ww, 0, 0).astype(BF)
            acc1[g * 256:(g + 1) * 256, :] += dot(d, vals)

    gather_z(g1, z1_s, z1_r, process1)

    def reduce8(acc, rb, ssem, rsem):
        cs = []
        for m in range(1, 8):
            pq, pr, px = peer8(m)
            c = copy(acc.at[pl.ds(pl.multiple_of(pq * 64, 64), 64)], rb.at[m], ssem.at[m], rsem.at[m], pr, px)
            c.start()
            cs.append(c)
        total = acc[pl.ds(pl.multiple_of(q * 64, 64), 64), :]
        for m in range(1, 8):
            cs[m - 1].wait_recv()
            total = total + rb[m]
        for c in cs:
            c.wait_send()
        return total

    sw[0] = reduce8(acc1, rb1, r1_s, r1_r).astype(BF)
    swap(sw.at[0], sw.at[1], sx_s, sx_r)()
    agg1 = sw[1]
    z_one = dot(agg1, w1[...])
    g2[z, y] = (z_one * jax.nn.sigmoid(z_one)).astype(BF)

    acc2[...] = jnp.zeros_like(acc2)

    def process2(slot):
        acc2[...] += dot(dd[slot], g2[slot].reshape(256, 256))

    gather_y(g2, y2_s, y2_r)
    gather_z(g2, z2_s, z2_r, process2)

    agg2 = reduce8(acc2, rb2, r2_s, r2_r).astype(BF)
    z_two = dot(agg2, w2[...])
    mine = pl.ds(pl.multiple_of(x * 64, 64), 64)
    dz2 = (cot[mine, :].astype(F32) * silu_slope(z_two)).astype(BF)
    own = pl.ds(pl.multiple_of(q * 64, 64), 64)
    bk[own, :] = dot(dz2, w2[...], 1, 1).astype(BF)
    bcopies = []
    for m in range(1, 8):
        _, pr, px = peer8(m)
        c = copy(bk.at[own], bk.at[own], bx_s.at[m], bx_r.at[m], pr, px)
        c.start()
        bcopies.append(c)
    out[mine, :] = (z_two * jax.nn.sigmoid(z_two)).astype(BF)
    ocopies = []
    for m in range(1, 4):
        c = copy(out.at[mine], out.at[mine], ox_s.at[m], ox_r.at[m], r, lax.rem(x + m, 4))
        c.start()
        ocopies.append(c)
    grad2 = dot(agg2, dz2, 0, 0)
    ga[:, :, :, 0:256] = grad2.reshape(8, 4, 8, 256)

    rsb[0, 0, 2:4] = jnp.zeros((2, 64, 256), BF)
    rsb[1, 0, 0:2] = jnp.zeros((2, 64, 256), BF)
    for c in bcopies:
        c.wait()

    def terms(slot):
        return dot(dt[slot], bk[...]).reshape(4, 64, 256)

    def hop(d, s, chunk):
        src = st0.at[chunk] if isinstance(s, int) and s == 0 else rsb.at[d, s - 1, chunk]
        return copy(src, rsb.at[d, s, chunk], rs_s.at[d, s, chunk], rs_r.at[d, s, chunk],
                    zpeer(1 if d == 0 else 15), x)

    st0[...] = terms(zslot(8)).astype(BF)
    for chunk in range(4):
        hop(chunk // 2, 0, chunk).start()

    def rs_step(s, first):
        for d in range(2):
            val = terms(zslot(8 - s) if d == 0 else zslot(s - 8))
            for chunk in range(4):
                if not first or chunk // 2 == d:
                    hop(d, s - 1, chunk).wait_recv()
                rsb[d, s - 1, chunk] = (rsb[d, s - 1, chunk].astype(F32) + val[chunk]).astype(BF)
                hop(d, s, chunk).start()

    rs_step(1, True)

    def rs_body(s, _):
        rs_step(s, False)
        return 0

    lax.fori_loop(2, 8, rs_body, 0)
    val = terms(z)
    for chunk in range(4):
        for d in range(2):
            hop(d, 7, chunk).wait_recv()
    ys[...] = val + rsb[0, 7].astype(F32) + rsb[1, 7].astype(F32)
    ycopies = []
    for m in range(1, 4):
        c = copy(ys.at[lax.rem(y + m, 4)], yb.at[m], ry_s.at[m], ry_r.at[m], ypeer(m), x)
        c.start()
        ycopies.append(c)
    dh = ys[y]
    for m in range(1, 4):
        ycopies[m - 1].wait_recv()
        dh = dh + yb[m]
    dz1 = (dh * silu_slope(z_one)).astype(BF)
    grad1 = dot(agg1, dz1, 0, 0).reshape(8, 2, 8, 256)
    for a in range(2):
        for b in range(2):
            ga[:, a * 2 + b, :, 256:384] = grad1[:, a, :, b * 128:(b + 1) * 128]

    cs = []
    for m in range(1, 8):
        pq, pr, px = peer8(m)
        c = copy(ga.at[pq], gb.at[m], ga_s.at[m], ga_r.at[m], pr, px)
        c.start()
        cs.append(c)
    total = ga[q]
    for m in range(1, 8):
        cs[m - 1].wait_recv()
        total = total + gb[m]
    gy[0] = total
    c2 = []
    for m in range(1, 4):
        c = copy(gy.at[0, lax.rem(y + m, 4)], gy.at[m, 0], gy_s.at[m], gy_r.at[m], ypeer(m), x)
        c.start()
        c2.append(c)
    tot = gy[0, y]
    for m in range(1, 4):
        c2[m - 1].wait_recv()
        tot = tot + gy[m, 0]
    gz[0] = tot
    c3 = []
    for m in range(1, 16):
        c = copy(gz.at[0], gz.at[m], gz_s.at[m], gz_r.at[m], zpeer(m), x)
        c.start()
        c3.append(c)
    for c in c3:
        c.wait_recv()
    tot = jnp.zeros((8, 384), F32)
    for k in range(16):
        tot = tot + gz[lax.rem(z - k + 16, 16)]
    gt[y] = tot
    c4 = []
    for m in range(1, 4):
        c = copy(gt.at[y], gt.at[y], gt_s.at[m], gt_r.at[m], ypeer(m), x)
        c.start()
        c4.append(c)
    for c in c4:
        c.wait()
    gq[q] = gt[...]
    c5 = []
    for m in range(1, 8):
        _, pr, px = peer8(m)
        c = copy(gq.at[q], gq.at[q], gq_s.at[m], gq_r.at[m], pr, px)
        c.start()
        c5.append(c)
    for c in c5:
        c.wait()
    gr2[...] = gq[:, :, :, 0:256].reshape(256, 256)
    for a in range(2):
        for b in range(2):
            gr1[:, a, :, b * 128:(b + 1) * 128] = gq[:, a * 2 + b, :, 256:384]

    for c in cs + c2 + c3 + ycopies:
        c.wait_send()
    for c in ocopies:
        c.wait()
    for chunk in range(4):
        hop(chunk // 2, 0, chunk).wait_send()

    def rs_sent(s, _):
        for chunk in range(4):
            for d in range(2):
                hop(d, s, chunk).wait_send()
        return 0

    lax.fori_loop(1, 8, rs_sent, 0)


def local(feats, edge_w, send_rows, counts, w_one, w_two, cotangent):
    idxt = jnp.transpose(send_rows[0])
    vm = pl.BlockSpec(memory_space=pltpu.VMEM)
    dma = pltpu.SemaphoreType.DMA
    scratch = [
        pltpu.VMEM((2, 2048, 128), F32),
        pltpu.VMEM((128, 16, 256), BF),
        pltpu.VMEM((2, 16, 4, 16, 256), BF),
        pltpu.VMEM((80, 128), BF),
        pltpu.VMEM((16, 4, 80, 128), BF),
        pltpu.VMEM((512, 128), F32),
        pltpu.VMEM((8, 64, 128), F32),
        pltpu.VMEM((2, 64, 128), BF),
        pltpu.VMEM((16, 4, 64, 256), BF),
        pltpu.VMEM((512, 256), F32),
        pltpu.VMEM((8, 64, 256), F32),
        pltpu.VMEM((16, 512, 256), BF),
        pltpu.VMEM((16, 256, 512), BF),
        pltpu.VMEM((512, 256), BF),
        pltpu.VMEM((4, 64, 256), BF),
        pltpu.VMEM((2, 8, 4, 64, 256), BF),
        pltpu.VMEM((4, 64, 256), F32),
        pltpu.VMEM((4, 64, 256), F32),
        pltpu.VMEM((8, 4, 8, 384), F32),
        pltpu.VMEM((8, 4, 8, 384), F32),
        pltpu.VMEM((4, 4, 8, 384), F32),
        pltpu.VMEM((16, 8, 384), F32),
        pltpu.VMEM((4, 8, 384), F32),
        pltpu.VMEM((8, 4, 8, 384), F32),
    ]
    one = dma(())
    sems = [
        one, one, dma((8,)), dma((8,)), dma((4,)), dma((4,)), dma((2, 8, 4)), dma((2, 8, 4)),
        dma((8,)), dma((8,)), one, one, dma((4,)), dma((4,)), dma((2, 8, 4)), dma((2, 8, 4)),
        dma((8,)), dma((8,)), dma((4,)), dma((4,)), dma((8,)), dma((8,)),
        dma((2, 8, 4)), dma((2, 8, 4)), dma((4,)), dma((4,)),
        dma((8,)), dma((8,)), dma((4,)), dma((4,)), dma((16,)), dma((16,)), dma((4,)), dma((4,)), dma((8,)), dma((8,)),
    ]
    out, gr1, gr2 = pl.pallas_call(
        kernel,
        out_shape=(
            jax.ShapeDtypeStruct((256, 256), BF),
            jax.ShapeDtypeStruct((8, 2, 8, 256), F32),
            jax.ShapeDtypeStruct((256, 256), F32),
        ),
        in_specs=[vm] * 7,
        out_specs=(vm, vm, vm),
        scratch_shapes=scratch + sems,
        compiler_params=pltpu.CompilerParams(
            collective_id=0, has_side_effects=True, vmem_limit_bytes=48 * 1024 * 1024
        ),
    )(feats, idxt, counts, edge_w, w_one, w_two, cotangent)
    return out, gr1.reshape(128, 256), gr2


def solution(mesh):
    in_specs = (
        P("rows", None),
        P("rows", "rep"),
        P("rows", None, "rep"),
        P("rows", None),
        P(),
        P(),
        P("rows", None),
    )
    out_specs = (P("rows", None), P(), P())
    return jax.shard_map(local, mesh=mesh, in_specs=in_specs, out_specs=out_specs, check_vma=False)
```

```python
import jax
import jax.numpy as jnp
from jax import lax
from jax.experimental import pallas as pl
from jax.experimental.pallas import tpu as pltpu
from jax.sharding import PartitionSpec as P

MESH = pl.DeviceIdType.MESH
BF = jnp.bfloat16
F32 = jnp.float32


def dot(a, b, ca=1, cb=0):
    return lax.dot_general(a, b, (((ca,), (cb,)), ((), ())), preferred_element_type=F32)


def silu_slope(values):
    sigma = jax.nn.sigmoid(values)
    return sigma * (1.0 + values * (1.0 - sigma))


def iota(shape, dim):
    return lax.broadcasted_iota(jnp.int32, shape, dim)


def one_hot(hit):
    return jnp.where(hit, 1.0, 0.0).astype(BF)


def body(
    pending,
    feats_h, idxt_h, cnt_h, w_h, w1_h, w2_h, cot_h,
    out, gr1, gr2,
    feats, idxt, cnt, w, w1, w2, cot,
    wtb, wr, wb, wf, stage, g1, oh, oht, pk, mine1, sum1, rc1, ab1, rp1, sw, g2,
    mine2, sum2, rc2, ab2, rp2, bk, tt, pb, fr, nr, cb,
    in_s, sw_s, sw_r, wx_s, wx_r, z1_s, z1_r, c1_s, c1_r, p1_s, p1_r, sx_s, sx_r, z2_s, z2_r,
    c2_s, c2_r, p2_s, p2_r, ox_s, ox_r, bp_s, bp_r, bc_s, bc_r, fr_s, fr_r, nr_s, nr_r,
    *sums,
):
    r = lax.axis_index("rows")
    x = lax.axis_index("rep")
    core = lax.rem(r, 2)
    z = lax.rem(lax.div(r, 2), 16)
    y = lax.div(r, 32)
    za = lax.div(z, 4)
    zb = lax.rem(z, 4)
    q = y * 4 + x
    other = 1 - core

    def rid(yy, zz, cc):
        return (yy * 16 + zz) * 2 + cc

    def peer(m):
        pq = lax.rem(q + m, 16)
        py, px = lax.div(pq, 4), lax.rem(pq, 4)
        return py, px, rid(py, z, core)

    def zat(m):
        return lax.rem(z + m + 16, 16)

    def zpeer(m):
        return rid(y, zat(m), core)

    def copy(src, dst, ssem, rsem, rows, rep):
        return pltpu.make_async_remote_copy(
            src_ref=src, dst_ref=dst, send_sem=ssem, recv_sem=rsem,
            device_id={"rows": rows, "rep": rep}, device_id_type=MESH,
        )

    def send(src, dst, ssem, rsem, rows, rep):
        c = copy(src, dst, ssem, rsem, rows, rep)
        c.start()
        pending.append(c.wait_send)
        return c

    def to_core(src, dst, ssem, rsem):
        return send(src, dst, ssem, rsem, rid(y, z, other), x)

    barrier = pltpu.get_barrier_semaphore()

    def greet(rows, rep):
        pl.semaphore_signal(barrier, inc=1, device_id={"rows": rows, "rep": rep}, device_id_type=MESH)

    ins = []
    for n, (a, b) in enumerate(
        [(feats_h, feats), (idxt_h, idxt), (cnt_h, cnt), (w_h, w), (w1_h, w1), (w2_h, w2), (cot_h, cot)]
    ):
        c = pltpu.make_async_copy(a, b, in_s.at[n])
        c.start()
        ins.append(c)

    alone = x == zb
    swap_r, swap_x = rid(y, za * 4 + x, core), zb
    for m in range(1, 16):
        greet(zpeer(m), x)
    for m in range(1, 16):
        py, px, pr = peer(m)
        greet(pr, px)
        greet(rid(py, z, other), px)
    greet(rid(y, z, other), x)

    @pl.when(jnp.logical_not(alone))
    def _():
        greet(swap_r, swap_x)

    mine = pl.ds(pl.multiple_of(x * 64, 64), 64)
    ins[0].wait()
    ins[1].wait()
    stage[0:64, :] = feats[mine, :]
    stage[64:80, :] = idxt[...].astype(F32).astype(BF)

    ins[2].wait()
    ins[3].wait()
    row = iota((512, 512), 0)
    plane, rest = row // 16, row % 16
    source = (plane // 8) * 32 + (rest % 4) * 8 + plane % 8
    order = one_hot((rest // 4) * 128 + source == iota((512, 512), 1))
    for sq in range(4):
        parts = []
        for s4 in range(4):
            s = sq * 4 + s4
            parts.append(jnp.where(cnt[...] > x * 16 + s, w[:, s * 128:(s + 1) * 128].astype(F32), 0.0).astype(BF))
        live = jnp.concatenate(parts, axis=1)
        wtb[sq] = dot(order, live, 1, 1).astype(BF).reshape(32, 16, 256)

    pl.semaphore_wait(barrier, 47 - alone.astype(jnp.int32))

    def swap(src, dst, ssem, rsem):
        c = copy(src, dst, ssem, rsem, swap_r, swap_x)

        @pl.when(alone)
        def _():
            dst[...] = src[...]

        @pl.when(jnp.logical_not(alone))
        def _():
            c.start()

        def finish():
            @pl.when(jnp.logical_not(alone))
            def _():
                c.wait_recv()

        def sent():
            @pl.when(jnp.logical_not(alone))
            def _():
                c.wait_send()

        pending.append(sent)
        return finish

    swap_done = swap(stage, g1.at[za * 4 + x], sw_s, sw_r)

    wcopies = []
    me8 = y * 2 + core
    for m in range(1, 16):
        py, px, pr = peer(m)
        for h, hr in ((core, pr), (other, rid(py, z, other))):
            n = 2 * m + (0 if h is core else 1)
            wcopies.append(send(wtb.at[:, (py * 4 + px) * 2 + h], wr.at[me8, x], wx_s.at[n], wx_r.at[n], hr, px))
    wcopies.append(to_core(wtb.at[:, q * 2 + other], wr.at[me8, x], wx_s.at[1], wx_r.at[1]))
    wr[me8, x] = wtb[:, q * 2 + core]
    yield "prep"

    swap_done()
    yield "swap1"

    def gather_z(g, rows, cut, ssem, rsem):
        full, parts = pl.ds(0, rows), (pl.ds(0, cut), pl.ds(cut, rows - cut))

        def move(d, dist):
            sign = 1 if d == 0 else -1
            far = dist > 4
            part = parts[d] if dist == 8 else full
            slot = zat(-sign * 4) if far else z
            return copy(g.at[slot, part], g.at[slot, part], ssem.at[d, dist], rsem.at[d, dist],
                        zpeer(sign * (dist - 4 if far else dist)), x)

        moves = {}
        for dist in (4, 3, 2, 1):
            for d in range(2):
                moves[d, dist] = move(d, dist)
                moves[d, dist].start()
                pending.append(moves[d, dist].wait_send)
        for d in range(2):
            moves[d, 4].wait_recv()
            for dist in (8, 7, 6, 5):
                moves[d, dist] = move(d, dist)
                moves[d, dist].start()
                pending.append(moves[d, dist].wait_send)
        for dist in (1, 2, 3, 5, 6, 7, 8):
            for d in range(2):
                moves[d, dist].wait_recv()

    gather_z(g1, 80, 48, z1_s, z1_r)
    yield "gz1"

    ids = g1[:, 64:80, :].reshape(256, 128)
    lane = iota((256, 256), 1).astype(F32)
    for k in range(8):
        at = ((k // 2) * 16 + z) * 2 + k % 2
        rows = dot(ids, one_hot(iota((128, 256), 0) == at))
        oh[:, k * 64:(k + 1) * 64, :] = one_hot(rows == lane).reshape(4, 64, 256)
    for a in range(4):
        pk[a, :, 0:128] = dot(oh[a], g1[4 * a:4 * a + 4, 0:64, :].reshape(256, 128)).astype(BF)

    yield "picks1"
    for c in wcopies:
        c.wait_recv()
    yield "wwait"

    row, col = iota((256, 256), 0), iota((256, 256), 1)
    regroup = one_hot((row % 64) * 4 + row // 64 == col)
    eye = one_hot(row == col)

    def weights(k):
        wb[k] = dot(regroup, wr[k].reshape(256, 256)).astype(BF)
        wf[k] = dot(eye, wb[k], 1, 1).astype(BF)

    def reduce_planes(width, prepare, own, total, rc, ab, rp, csem_s, csem_r, psem_s, psem_r):
        def partial(k):
            prepare(k)
            picked = pk[:, pl.ds(pl.multiple_of(k * 64, 64), 64), 0:width].reshape(256, width)
            return dot(wf[k], picked)

        cs = []
        for j in range(4):
            own[1, j] = partial(j * 2 + other).astype(BF)
            cs.append(to_core(own.at[1, j], rc.at[j], csem_s.at[j], csem_r.at[j]))
        for j in range(4):
            total[j] = partial(j * 2 + core)
        for j in range(4):
            cs[j].wait_recv()
            ab[j] = (total[j] + rc[j].astype(F32)).astype(BF).reshape(4, 64, width)
        ps = []
        for m in range(1, 16):
            py, px, pr = peer(m)
            ps.append(send(ab.at[py, px], rp.at[m], psem_s.at[m], psem_r.at[m], pr, px))
        res = ab[y, x].astype(F32)
        for m in range(1, 16):
            ps[m - 1].wait_recv()
            res = res + rp[m].astype(F32)
        return res.astype(BF)

    sw[0] = reduce_planes(128, weights, mine1, sum1, rc1, ab1, rp1, c1_s, c1_r, p1_s, p1_r)
    yield "red1"
    swap(sw.at[0], sw.at[1], sx_s, sx_r)()
    yield "swap2"
    for n in (4, 5, 6):
        ins[n].wait()
    agg1 = sw[1]
    z_one = dot(agg1, w1[...])
    g2[z] = (z_one * jax.nn.sigmoid(z_one)).astype(BF)
    gather_z(g2, 64, 32, z2_s, z2_r)
    yield "gz2"
    for a in range(4):
        pk[a] = dot(oh[a], g2[4 * a:4 * a + 4].reshape(256, 256)).astype(BF)
    agg2 = reduce_planes(256, lambda k: None, mine2, sum2, rc2, ab2, rp2, c2_s, c2_r, p2_s, p2_r)
    yield "red2"

    z_two = dot(agg2, w2[...])
    dz2 = (cot[mine, :].astype(F32) * silu_slope(z_two)).astype(BF)
    bk[y, core, mine, :] = dot(dz2, w2[...], 1, 1).astype(BF)
    bcopies = []
    for m in range(1, 16):
        py, px, pr = peer(m)
        bcopies.append(send(bk.at[y, core, mine], bk.at[y, core, mine], bp_s.at[m], bp_r.at[m], pr, px))
    out[mine, :] = (z_two * jax.nn.sigmoid(z_two)).astype(BF)
    ocopies = []
    for m in range(1, 4):
        ocopies.append(send(out.at[mine], out.at[mine], ox_s.at[m], ox_r.at[m], r, lax.rem(x + m, 4)))

    def reduce_all(ga, rc, gs, gp, gz, gt, c_s, c_r, p_s, p_r, z_s, z_r, t_s, t_r, d_s, d_r):
        c = to_core(ga.at[other], rc, c_s, c_r)
        yield
        c.wait_recv()
        gs[...] = ga[core] + rc[...]
        ps = []
        for m in range(1, 16):
            py, px, pr = peer(m)
            ps.append(send(gs.at[py * 4 + px], gp.at[m], p_s.at[m], p_r.at[m], pr, px))
        yield
        total = gs[q]
        for m in range(1, 16):
            ps[m - 1].wait_recv()
            total = total + gp[m]
        gz[0] = total
        zs = []
        for m in (8, 7, 9, 6, 10, 5, 11, 4, 12, 3, 13, 2, 14, 1, 15):
            zs.append(send(gz.at[0], gz.at[m], z_s.at[m], z_r.at[m], zpeer(m), x))
        yield
        for c in zs:
            c.wait_recv()
        total = jnp.zeros_like(total)
        for k in range(16):
            total = total + gz[lax.rem(z - k + 16, 16)]
        gt[core, q] = total
        ts = []
        for m in range(1, 16):
            py, px, pr = peer(m)
            ts.append(send(gt.at[core, q], gt.at[core, q], t_s.at[m], t_r.at[m], pr, px))
        yield
        for c in ts:
            c.wait_recv()
        c = to_core(gt.at[core], gt.at[core], d_s, d_r)
        yield
        c.wait_recv()
        yield

    half = len(sums) // 2
    ga2, ga1 = sums[0], sums[half]
    reduce2, reduce1 = reduce_all(*sums[:half]), reduce_all(*sums[half:])
    ga2[...] = dot(agg2, dz2, 0, 0).reshape(2, 16, 8, 256)
    next(reduce2)

    for a in range(4):
        oht[a] = dot(eye, oh[a], 1, 1).astype(BF)
    for c in bcopies:
        c.wait_recv()
    cc = [to_core(bk.at[j, core], bk.at[j, core], bc_s.at[j], bc_r.at[j]) for j in range(4)]
    next(reduce2)

    def slot_terms(k):
        got = dot(wb[k], bk[lax.div(k, 2), lax.rem(k, 2)]).astype(BF)
        tt[:, pl.ds(pl.multiple_of(k * 64, 64), 64), :] = got.reshape(4, 64, 256)

    for j in range(4):
        slot_terms(j * 2 + core)
    for j in range(4):
        cc[j].wait_recv()
        slot_terms(j * 2 + other)
    yield "bwait"
    for a in range(4):
        pb[4 * a:4 * a + 4] = dot(oht[a], tt[a]).astype(BF).reshape(4, 64, 256)

    full, parts = pl.ds(0, 64), (pl.ds(0, 32), pl.ds(32, 32))
    fars, nears = {}, {}
    for m in (4, 3, 2, 1):
        for d in range(2):
            sign = 1 if d == 0 else -1
            part = parts[d] if m == 4 else full
            fars[d, m] = send(pb.at[zat(sign * (4 + m)), part], fr.at[d, m, part], fr_s.at[d, m], fr_r.at[d, m],
                              zpeer(sign * m), x)
    for m in (3, 2, 1):
        for d in range(2):
            sign = 1 if d == 0 else -1
            nears[d, m] = send(pb.at[zat(sign * m)], nr.at[d, m], nr_s.at[d, m], nr_r.at[d, m], zpeer(sign * m), x)
    next(reduce2)
    for d in range(2):
        sign = 1 if d == 0 else -1
        acc = pb[zat(sign * 4)].astype(F32)
        for m in (1, 2, 3):
            fars[d, m].wait_recv()
            acc = acc + fr[d, m].astype(F32)
        fars[d, 4].wait_recv()
        cb[d] = acc.astype(BF)
        lo = 0 if d == 0 else 32
        cb[d, lo:lo + 32, :] = (acc[lo:lo + 32] + fr[d, 4, lo:lo + 32, :].astype(F32)).astype(BF)
        nears[d, 4] = send(cb.at[d], nr.at[d, 4], nr_s.at[d, 4], nr_r.at[d, 4], zpeer(sign * 4), x)
    next(reduce2)
    dh = pb[z].astype(F32)
    for m in (1, 2, 3, 4):
        for d in range(2):
            nears[d, m].wait_recv()
            dh = dh + nr[d, m].astype(F32)
    yield "rsz"
    dz1 = (dh * silu_slope(z_one)).astype(BF)
    grad1 = dot(agg1, dz1, 0, 0).reshape(2, 8, 8, 256)
    for b in range(2):
        ga1[:, :, b] = grad1[:, :, :, b * 128:(b + 1) * 128]
    ga1 = ga1.reshape(2, 16, 8, 128)
    reduce1 = reduce_all(ga1, *sums[half + 1:])
    next(reduce1)
    next(reduce2)
    yield "arc"
    next(reduce1)
    next(reduce2)
    gr2[...] = sums[5][...].reshape(256, 256)
    yield "arp"
    next(reduce1)
    yield "arz"
    next(reduce1)
    yield "art"
    next(reduce1)
    next(reduce1)
    gt1 = sums[half + 5]
    for b in range(2):
        for k in range(8):
            gr1[:, k, :, b * 128:(b + 1) * 128] = gt1[:, 2 * k + b]
    for c in ocopies:
        c.wait_recv()


def kernel(*refs):
    pending = []
    for _ in body(pending, *refs):
        pass
    for wait in pending:
        wait()


def local(feats, edge_w, send_rows, counts, w_one, w_two, cotangent):
    idxt = jnp.transpose(send_rows[0])
    vm = pl.BlockSpec(memory_space=pltpu.VMEM)
    hbm = pl.BlockSpec(memory_space=pl.ANY)
    args = (feats, idxt, counts, edge_w, w_one, w_two, cotangent)
    dma = pltpu.SemaphoreType.DMA

    def vmem(kind, *shape):
        return pltpu.VMEM(shape, kind)

    scratch = [pltpu.VMEM(a.shape, a.dtype) for a in args] + [
        vmem(BF, 4, 32, 16, 256),
        vmem(BF, 8, 4, 4, 16, 256),
        vmem(BF, 8, 256, 256),
        vmem(BF, 8, 256, 256),
        vmem(BF, 80, 128),
        vmem(BF, 16, 80, 128),
        vmem(BF, 4, 512, 256),
        vmem(BF, 4, 256, 512),
        vmem(BF, 4, 512, 256),
        vmem(BF, 2, 4, 256, 128),
        vmem(F32, 4, 256, 128),
        vmem(BF, 4, 256, 128),
        vmem(BF, 4, 4, 64, 128),
        vmem(BF, 16, 64, 128),
        vmem(BF, 2, 64, 128),
        vmem(BF, 16, 64, 256),
        vmem(BF, 2, 4, 256, 256),
        vmem(F32, 4, 256, 256),
        vmem(BF, 4, 256, 256),
        vmem(BF, 4, 4, 64, 256),
        vmem(BF, 16, 64, 256),
        vmem(BF, 4, 2, 256, 256),
        vmem(BF, 4, 512, 256),
        vmem(BF, 16, 64, 256),
        vmem(BF, 2, 5, 64, 256),
        vmem(BF, 2, 5, 64, 256),
        vmem(BF, 2, 64, 256),
        dma((7,)), dma(()), dma(()), dma((32,)), dma((32,)), dma((2, 9)), dma((2, 9)),
        dma((4,)), dma((4,)), dma((16,)), dma((16,)), dma(()), dma(()), dma((2, 9)), dma((2, 9)),
        dma((4,)), dma((4,)), dma((16,)), dma((16,)), dma((4,)), dma((4,)), dma((16,)), dma((16,)),
        dma((4,)), dma((4,)), dma((2, 5)), dma((2, 5)), dma((2, 5)), dma((2, 5)),
    ]
    for width, first in ((256, (2, 16, 8, 256)), (128, (2, 8, 2, 8, 128))):
        scratch += [
            vmem(F32, *first),
            vmem(F32, 16, 8, width),
            vmem(F32, 16, 8, width),
            vmem(F32, 16, 8, width),
            vmem(F32, 16, 8, width),
            vmem(F32, 2, 16, 8, width),
            dma(()), dma(()), dma((16,)), dma((16,)), dma((16,)), dma((16,)), dma((16,)), dma((16,)), dma(()), dma(()),
        ]
    out, gr1, gr2 = pl.pallas_call(
        kernel,
        out_shape=(
            jax.ShapeDtypeStruct((256, 256), BF),
            jax.ShapeDtypeStruct((2, 8, 8, 256), F32),
            jax.ShapeDtypeStruct((256, 256), F32),
        ),
        in_specs=[hbm] * 7,
        out_specs=(vm, vm, vm),
        scratch_shapes=scratch,
        compiler_params=pltpu.CompilerParams(
            collective_id=0, has_side_effects=True, vmem_limit_bytes=56 * 1024 * 1024
        ),
    )(*args)
    return out, gr1.reshape(128, 256), gr2


def solution(mesh):
    in_specs = (
        P("rows", None),
        P("rows", "rep"),
        P("rows", None, "rep"),
        P("rows", None),
        P(),
        P(),
        P("rows", None),
    )
    out_specs = (P("rows", None), P(), P())
    return jax.shard_map(local, mesh=mesh, in_specs=in_specs, out_specs=out_specs, check_vma=False)
```

```python
import jax
import jax.numpy as jnp
from jax import lax
from jax.experimental import pallas as pl
from jax.experimental.pallas import tpu as pltpu
from jax.sharding import PartitionSpec as P

MESH = pl.DeviceIdType.MESH
BF = jnp.bfloat16
F32 = jnp.float32


def dot(a, b, ca=1, cb=0):
    return lax.dot_general(a, b, (((ca,), (cb,)), ((), ())), preferred_element_type=F32)


def silu_slope(values):
    sigma = jax.nn.sigmoid(values)
    return sigma * (1.0 + values * (1.0 - sigma))


def iota(shape, dim):
    return lax.broadcasted_iota(jnp.int32, shape, dim)


def one_hot(hit):
    return jnp.where(hit, 1.0, 0.0).astype(BF)


def body(
    pending,
    feats_h, idxt_h, cnt_h, w_h, w1_h, w2_h, cot_h,
    out, gr1, gr2,
    feats, idxt, cnt, w, w1, w2, cot,
    wtb, wr, wb, wf, stage, g1, oh, oht, pk, mine1, rc1, ab1, rp1, sw, g2,
    mine2, rc2, ab2, rp2, bk, tt, pb, fr, nr, cb,
    in_s, sw_s, sw_r, wx_s, wx_r, z1_s, z1_r, c1_s, c1_r, p1_s, p1_r, sx_s, sx_r, z2_s, z2_r,
    c2_s, c2_r, p2_s, p2_r, ox_s, ox_r, bp_s, bp_r, bc_s, bc_r, fr_s, fr_r, nr_s, nr_r,
    *sums,
):
    r = lax.axis_index("rows")
    x = lax.axis_index("rep")
    core = lax.rem(r, 2)
    z = lax.rem(lax.div(r, 2), 16)
    y = lax.div(r, 32)
    za = lax.div(z, 4)
    zb = lax.rem(z, 4)
    q = y * 4 + x
    other = 1 - core

    def rid(yy, zz, cc):
        return (yy * 16 + zz) * 2 + cc

    def peer(m):
        pq = lax.rem(q + m, 16)
        py, px = lax.div(pq, 4), lax.rem(pq, 4)
        return py, px, rid(py, z, core)

    def zat(m):
        return lax.rem(z + m + 16, 16)

    def zpeer(m):
        return rid(y, zat(m), core)

    def copy(src, dst, ssem, rsem, rows, rep):
        return pltpu.make_async_remote_copy(
            src_ref=src, dst_ref=dst, send_sem=ssem, recv_sem=rsem,
            device_id={"rows": rows, "rep": rep}, device_id_type=MESH,
        )

    def send(src, dst, ssem, rsem, rows, rep):
        c = copy(src, dst, ssem, rsem, rows, rep)
        c.start()
        pending.append(c.wait_send)
        return c

    def to_core(src, dst, ssem, rsem):
        return send(src, dst, ssem, rsem, rid(y, z, other), x)

    barrier = pltpu.get_barrier_semaphore()

    def greet(rows, rep):
        pl.semaphore_signal(barrier, inc=1, device_id={"rows": rows, "rep": rep}, device_id_type=MESH)

    ins = []
    for n, (a, b) in enumerate(
        [(feats_h, feats), (idxt_h, idxt), (cnt_h, cnt), (w_h, w), (w1_h, w1), (w2_h, w2), (cot_h, cot)]
    ):
        c = pltpu.make_async_copy(a, b, in_s.at[n])
        c.start()
        ins.append(c)

    alone = x == zb
    swap_r, swap_x = rid(y, za * 4 + x, core), zb
    for m in (1, 2, 3, 4, 12, 13, 14, 15):
        greet(zpeer(m), x)
    for m in range(1, 16):
        py, px, pr = peer(m)
        greet(pr, px)
        greet(rid(py, z, other), px)
    greet(rid(y, z, other), x)

    @pl.when(jnp.logical_not(alone))
    def _():
        greet(swap_r, swap_x)

    mine = pl.ds(pl.multiple_of(x * 64, 64), 64)
    ins[0].wait()
    ins[1].wait()
    stage[0:64, :] = feats[mine, :]
    stage[64:80, :] = idxt[...].astype(F32).astype(BF)

    ins[2].wait()
    ins[3].wait()
    row = iota((512, 1), 0)
    plane, rest = row >> 4, row & 15
    source = ((rest >> 2) << 7) + ((plane >> 3) << 5) + ((rest & 3) << 3) + (plane & 7)
    order = one_hot(source == iota((512, 512), 1))
    for sq in range(4):
        alive = [one_hot(cnt[...] > x * 16 + sq * 4 + s4) for s4 in range(4)]
        live = w[:, sq * 512:(sq + 1) * 512] * jnp.concatenate(alive, axis=1)
        wtb[sq] = dot(order, live, 1, 1).astype(BF).reshape(32, 16, 256)

    pl.semaphore_wait(barrier, 40 - alone.astype(jnp.int32))

    def swap(src, dst, ssem, rsem):
        c = copy(src, dst, ssem, rsem, swap_r, swap_x)

        @pl.when(alone)
        def _():
            dst[...] = src[...]

        @pl.when(jnp.logical_not(alone))
        def _():
            c.start()

        def finish():
            @pl.when(jnp.logical_not(alone))
            def _():
                c.wait_recv()

        def sent():
            @pl.when(jnp.logical_not(alone))
            def _():
                c.wait_send()

        pending.append(sent)
        return finish

    swap_done = swap(stage, g1.at[za * 4 + x], sw_s, sw_r)

    wcopies = []
    me8 = y * 2 + core
    for m in range(1, 16):
        py, px, pr = peer(m)
        for h, hr in ((core, pr), (other, rid(py, z, other))):
            n = 2 * m + (0 if h is core else 1)
            wcopies.append(send(wtb.at[:, (py * 4 + px) * 2 + h], wr.at[me8, x], wx_s.at[n], wx_r.at[n], hr, px))
    wcopies.append(to_core(wtb.at[:, q * 2 + other], wr.at[me8, x], wx_s.at[1], wx_r.at[1]))
    wr[me8, x] = wtb[:, q * 2 + core]
    yield "prep"

    row, col = iota((256, 1), 0), iota((256, 256), 1)
    regroup = one_hot(((row & 63) << 2) + (row >> 6) == col)
    eye = one_hot(row == col)
    swap_done()
    yield "swap1"

    def gather_z(g, rows, cut, ssem, rsem, work):
        full, parts = pl.ds(0, rows), (pl.ds(0, cut), pl.ds(cut, rows - cut))

        def move(d, dist):
            sign = 1 if d == 0 else -1
            far = dist > 4
            part = parts[d] if dist == 8 else full
            slot = zat(-sign * 4) if far else z
            return copy(g.at[slot, part], g.at[slot, part], ssem.at[d, dist], rsem.at[d, dist],
                        zpeer(sign * (dist - 4 if far else dist)), x)

        moves = {}
        for dist in (4, 3, 2, 1):
            for d in range(2):
                moves[d, dist] = move(d, dist)
                moves[d, dist].start()
                pending.append(moves[d, dist].wait_send)
        work()
        for d in range(2):
            moves[d, 4].wait_recv()
            for dist in (8, 7, 6, 5):
                moves[d, dist] = move(d, dist)
                moves[d, dist].start()
                pending.append(moves[d, dist].wait_send)
        for dist in (1, 2, 3, 5, 6, 7, 8):
            for d in range(2):
                moves[d, dist].wait_recv()

    gather_z(g1, 80, 48, z1_s, z1_r, lambda: None)
    yield "gz1"

    ids = g1[:, 64:80, :].reshape(256, 128)
    lane = iota((256, 256), 1).astype(F32)
    for k in range(8):
        at = ((k // 2) * 16 + z) * 2 + k % 2
        rows = dot(ids, one_hot(iota((128, 256), 0) == at))
        oh[:, k * 64:(k + 1) * 64, :] = one_hot(rows == lane).reshape(4, 64, 256)
    for a in range(4):
        pk[a, :, 0:128] = dot(oh[a], g1[4 * a:4 * a + 4, 0:64, :].reshape(256, 128)).astype(BF)

    yield "picks1"
    for c in wcopies:
        c.wait_recv()
    yield "wwait"


    def weights(k):
        wb[k] = dot(regroup, wr[k].reshape(256, 256)).astype(BF)
        wf[k] = dot(eye, wb[k], 1, 1).astype(BF)

    def reduce_planes(width, prepare, own, rc, ab, rp, csem_s, csem_r, psem_s, psem_r):
        def partial(k):
            prepare(k)
            picked = pk[:, pl.ds(pl.multiple_of(k * 64, 64), 64), 0:width].reshape(256, width)
            return dot(wf[k], picked)

        near = (2, 1, 3, 0)
        cs = []
        for off in near:
            j = lax.rem(y + off, 4)
            own[j] = partial(j * 2 + other).astype(BF)
            cs.append(to_core(own.at[j], rc.at[j], csem_s.at[off], csem_r.at[off]))
        ps = []
        for n, off in enumerate(near):
            j = lax.rem(y + off, 4)
            mine_j = partial(j * 2 + core)
            cs[n].wait_recv()
            ab[j] = (mine_j + rc[j].astype(F32)).astype(BF).reshape(4, 64, width)
            for mx in near:
                m = off * 4 + mx
                if m:
                    px = lax.rem(x + mx, 4)
                    ps.append((m, send(ab.at[j, px], rp.at[m], psem_s.at[m], psem_r.at[m], rid(j, z, core), px)))
        res = ab[y, x].astype(F32)
        for m, c in ps[::-1]:
            c.wait_recv()
            res = res + rp[m].astype(F32)
        return res.astype(BF)

    sw[0] = reduce_planes(128, weights, mine1, rc1, ab1, rp1, c1_s, c1_r, p1_s, p1_r)
    yield "red1"
    swap(sw.at[0], sw.at[1], sx_s, sx_r)()
    yield "swap2"
    for n in (4, 5, 6):
        ins[n].wait()
    agg1 = sw[1]
    z_one = dot(agg1, w1[...])
    g2[z] = (z_one * jax.nn.sigmoid(z_one)).astype(BF)

    def turn_picks():
        for a in range(4):
            oht[a] = dot(eye, oh[a], 1, 1).astype(BF)

    gather_z(g2, 64, 32, z2_s, z2_r, turn_picks)
    yield "gz2"
    for a in range(4):
        pk[a] = dot(oh[a], g2[4 * a:4 * a + 4].reshape(256, 256)).astype(BF)
    agg2 = reduce_planes(256, lambda k: None, mine2, rc2, ab2, rp2, c2_s, c2_r, p2_s, p2_r)
    yield "red2"

    z_two = dot(agg2, w2[...])
    dz2 = (cot[mine, :].astype(F32) * silu_slope(z_two)).astype(BF)
    bk[y, core, mine, :] = dot(dz2, w2[...], 1, 1).astype(BF)
    bcopies = {}
    for off in (2, 1, 3, 0):
        for mx in (2, 1, 3, 0):
            m = off * 4 + mx
            if m:
                py, px = lax.rem(y + off, 4), lax.rem(x + mx, 4)
                bcopies[m] = send(bk.at[y, core, mine], bk.at[y, core, mine], bp_s.at[m], bp_r.at[m],
                                  rid(py, z, core), px)
    out[mine, :] = (z_two * jax.nn.sigmoid(z_two)).astype(BF)
    ocopies = []
    for m in range(1, 4):
        ocopies.append(send(out.at[mine], out.at[mine], ox_s.at[m], ox_r.at[m], r, lax.rem(x + m, 4)))

    def reduce_all(ga, rc, gs, gp, gz, gt, c_s, c_r, p_s, p_r, z_s, z_r, t_s, t_r, d_s, d_r):
        c = to_core(ga.at[other], rc, c_s, c_r)
        yield
        c.wait_recv()
        gs[...] = ga[core] + rc[...]
        ps = []
        for m in range(1, 16):
            py, px, pr = peer(m)
            ps.append(send(gs.at[py * 4 + px], gp.at[m], p_s.at[m], p_r.at[m], pr, px))
        yield
        total = gs[q]
        for m in range(1, 16):
            ps[m - 1].wait_recv()
            total = total + gp[m]
        wide = gz.dtype == BF
        gz[0] = jnp.concatenate([total[:, :128], total[:, 128:]], axis=0).astype(BF) if wide else total
        zs = []
        for m in (8, 7, 9, 6, 10, 5, 11, 4, 12, 3, 13, 2, 14, 1, 15):
            zs.append(send(gz.at[0], gz.at[m], z_s.at[m], z_r.at[m], zpeer(m), x))
        yield
        for c in zs:
            c.wait_recv()
        total = gz[z].astype(F32)
        for k in range(1, 16):
            total = total + gz[lax.rem(z - k + 16, 16)].astype(F32)
        gt[core, q] = jnp.concatenate([total[:8], total[8:]], axis=1) if wide else total
        ts = []
        for m in range(1, 16):
            py, px, pr = peer(m)
            ts.append(send(gt.at[core, q], gt.at[core, q], t_s.at[m], t_r.at[m], pr, px))
        yield
        for c in ts:
            c.wait_recv()
        c = to_core(gt.at[core], gt.at[core], d_s, d_r)
        yield
        c.wait_recv()
        yield

    half = len(sums) // 2
    ga2, ga1 = sums[0], sums[half]
    reduce2, reduce1 = reduce_all(*sums[:half]), reduce_all(*sums[half:])
    ga2[...] = dot(agg2, dz2, 0, 0).reshape(2, 16, 8, 256)
    next(reduce2)


    def slot_terms(k):
        got = dot(wb[k], bk[lax.div(k, 2), lax.rem(k, 2)]).astype(BF)
        tt[:, pl.ds(pl.multiple_of(k * 64, 64), 64), :] = got.reshape(4, 64, 256)

    next(reduce2)
    cc = {}
    for off in (0, 1, 3, 2):
        j = lax.rem(y - off + 4, 4)
        for mx in range(4):
            if off * 4 + mx:
                bcopies[off * 4 + mx].wait_recv()
        cc[off] = to_core(bk.at[j, core], bk.at[j, core], bc_s.at[off], bc_r.at[off])
        slot_terms(j * 2 + core)
    next(reduce2)
    for off in (0, 1, 3, 2):
        cc[off].wait_recv()
        slot_terms(lax.rem(y - off + 4, 4) * 2 + other)
    yield "bwait"
    for a in range(4):
        pb[4 * a:4 * a + 4] = dot(oht[a], tt[a]).astype(BF).reshape(4, 64, 256)

    full, parts = pl.ds(0, 64), (pl.ds(0, 32), pl.ds(32, 32))
    fars, nears = {}, {}
    for m in (4, 3, 2, 1):
        for d in range(2):
            sign = 1 if d == 0 else -1
            part = parts[d] if m == 4 else full
            fars[d, m] = send(pb.at[zat(sign * (4 + m)), part], fr.at[d, m, part], fr_s.at[d, m], fr_r.at[d, m],
                              zpeer(sign * m), x)
    for m in (3, 2, 1):
        for d in range(2):
            sign = 1 if d == 0 else -1
            nears[d, m] = send(pb.at[zat(sign * m)], nr.at[d, m], nr_s.at[d, m], nr_r.at[d, m], zpeer(sign * m), x)
    for d in range(2):
        sign = 1 if d == 0 else -1
        acc = pb[zat(sign * 4)].astype(F32)
        for m in (1, 2, 3):
            fars[d, m].wait_recv()
            acc = acc + fr[d, m].astype(F32)
        fars[d, 4].wait_recv()
        cb[d] = acc.astype(BF)
        lo = 0 if d == 0 else 32
        cb[d, lo:lo + 32, :] = (acc[lo:lo + 32] + fr[d, 4, lo:lo + 32, :].astype(F32)).astype(BF)
        nears[d, 4] = send(cb.at[d], nr.at[d, 4], nr_s.at[d, 4], nr_r.at[d, 4], zpeer(sign * 4), x)
    next(reduce2)
    dh = pb[z].astype(F32)
    for m in (1, 2, 3, 4):
        for d in range(2):
            nears[d, m].wait_recv()
            dh = dh + nr[d, m].astype(F32)
    yield "rsz"
    dz1 = (dh * silu_slope(z_one)).astype(BF)
    grad1 = dot(agg1, dz1, 0, 0).reshape(2, 8, 8, 256)
    for b in range(2):
        ga1[:, :, b] = grad1[:, :, :, b * 128:(b + 1) * 128]
    ga1 = ga1.reshape(2, 16, 8, 128)
    reduce1 = reduce_all(ga1, *sums[half + 1:])
    next(reduce1)
    next(reduce2)
    yield "arc"
    next(reduce1)
    next(reduce2)
    gr2[...] = sums[5][...].reshape(256, 256)
    yield "arp"
    next(reduce1)
    yield "arz"
    next(reduce1)
    yield "art"
    next(reduce1)
    next(reduce1)
    gt1 = sums[half + 5]
    for b in range(2):
        for k in range(8):
            gr1[:, k, :, b * 128:(b + 1) * 128] = gt1[:, 2 * k + b]
    for c in ocopies:
        c.wait_recv()


def kernel(*refs):
    pending = []
    for _ in body(pending, *refs):
        pass
    for wait in pending:
        wait()


def local(feats, edge_w, send_rows, counts, w_one, w_two, cotangent):
    idxt = jnp.transpose(send_rows[0])
    vm = pl.BlockSpec(memory_space=pltpu.VMEM)
    hbm = pl.BlockSpec(memory_space=pl.ANY)
    args = (feats, idxt, counts, edge_w, w_one, w_two, cotangent)
    dma = pltpu.SemaphoreType.DMA

    def vmem(kind, *shape):
        return pltpu.VMEM(shape, kind)

    scratch = [pltpu.VMEM(a.shape, a.dtype) for a in args] + [
        vmem(BF, 4, 32, 16, 256),
        vmem(BF, 8, 4, 4, 16, 256),
        vmem(BF, 8, 256, 256),
        vmem(BF, 8, 256, 256),
        vmem(BF, 80, 128),
        vmem(BF, 16, 80, 128),
        vmem(BF, 4, 512, 256),
        vmem(BF, 4, 256, 512),
        vmem(BF, 4, 512, 256),
        vmem(BF, 4, 256, 128),
        vmem(BF, 4, 256, 128),
        vmem(BF, 4, 4, 64, 128),
        vmem(BF, 16, 64, 128),
        vmem(BF, 2, 64, 128),
        vmem(BF, 16, 64, 256),
        vmem(BF, 4, 256, 256),
        vmem(BF, 4, 256, 256),
        vmem(BF, 4, 4, 64, 256),
        vmem(BF, 16, 64, 256),
        vmem(BF, 4, 2, 256, 256),
        vmem(BF, 4, 512, 256),
        vmem(BF, 16, 64, 256),
        vmem(BF, 2, 5, 64, 256),
        vmem(BF, 2, 5, 64, 256),
        vmem(BF, 2, 64, 256),
        dma((7,)), dma(()), dma(()), dma((32,)), dma((32,)), dma((2, 9)), dma((2, 9)),
        dma((4,)), dma((4,)), dma((16,)), dma((16,)), dma(()), dma(()), dma((2, 9)), dma((2, 9)),
        dma((4,)), dma((4,)), dma((16,)), dma((16,)), dma((4,)), dma((4,)), dma((16,)), dma((16,)),
        dma((4,)), dma((4,)), dma((2, 5)), dma((2, 5)), dma((2, 5)), dma((2, 5)),
    ]
    for width, first in ((256, (2, 16, 8, 256)), (128, (2, 8, 2, 8, 128))):
        scratch += [
            vmem(F32, *first),
            vmem(F32, 16, 8, width),
            vmem(F32, 16, 8, width),
            vmem(F32, 16, 8, width),
            vmem(BF, 16, 16, 128) if width == 256 else vmem(F32, 16, 8, width),
            vmem(F32, 2, 16, 8, width),
            dma(()), dma(()), dma((16,)), dma((16,)), dma((16,)), dma((16,)), dma((16,)), dma((16,)), dma(()), dma(()),
        ]
    out, gr1, gr2 = pl.pallas_call(
        kernel,
        out_shape=(
            jax.ShapeDtypeStruct((256, 256), BF),
            jax.ShapeDtypeStruct((2, 8, 8, 256), F32),
            jax.ShapeDtypeStruct((256, 256), F32),
        ),
        in_specs=[hbm] * 7,
        out_specs=(vm, vm, vm),
        scratch_shapes=scratch,
        compiler_params=pltpu.CompilerParams(
            collective_id=0, has_side_effects=True, vmem_limit_bytes=56 * 1024 * 1024
        ),
    )(*args)
    return out, gr1.reshape(128, 256), gr2


def solution(mesh):
    in_specs = (
        P("rows", None),
        P("rows", "rep"),
        P("rows", None, "rep"),
        P("rows", None),
        P(),
        P(),
        P("rows", None),
    )
    out_specs = (P("rows", None), P(), P())
    return jax.shard_map(local, mesh=mesh, in_specs=in_specs, out_specs=out_specs, check_vma=False)
```

```python
import jax
import jax.numpy as jnp
from jax import lax
from jax.experimental import pallas as pl
from jax.experimental.pallas import tpu as pltpu
from jax.sharding import PartitionSpec as P

MESH = pl.DeviceIdType.MESH
BF = jnp.bfloat16
F32 = jnp.float32


def dot(a, b, ca=1, cb=0):
    return lax.dot_general(a, b, (((ca,), (cb,)), ((), ())), preferred_element_type=F32)


def silu_slope(values):
    sigma = jax.nn.sigmoid(values)
    return sigma * (1.0 + values * (1.0 - sigma))


def iota(shape, dim):
    return lax.broadcasted_iota(jnp.int32, shape, dim)


def one_hot(hit):
    return jnp.where(hit, 1.0, 0.0).astype(BF)


def body(
    pending,
    feats_h, idxt_h, cnt_h, w_h, w1_h, w2_h, cot_h,
    out, gr1, gr2,
    feats, idxt, cnt, w, w1, w2, cot,
    wtb, wr, wb, wf, stage, g1, oh, oht, pk, mine1, rc1, ab1, rp1, sw, g2,
    mine2, rc2, ab2, rp2, bk, tt, pb, fr, nr, cb,
    in_s, sw_s, sw_r, wx_s, wx_r, z1_s, z1_r, c1_s, c1_r, p1_s, p1_r, sx_s, sx_r, z2_s, z2_r,
    c2_s, c2_r, p2_s, p2_r, ox_s, ox_r, bp_s, bp_r, bc_s, bc_r, fr_s, fr_r,
    *sums,
):
    r = lax.axis_index("rows")
    x = lax.axis_index("rep")
    core = lax.rem(r, 2)
    z = lax.rem(lax.div(r, 2), 16)
    y = lax.div(r, 32)
    za = lax.div(z, 4)
    zb = lax.rem(z, 4)
    q = y * 4 + x
    other = 1 - core

    def rid(yy, zz, cc):
        return (yy * 16 + zz) * 2 + cc

    def peer(m):
        pq = lax.rem(q + m, 16)
        py, px = lax.div(pq, 4), lax.rem(pq, 4)
        return py, px, rid(py, z, core)

    def zat(m):
        return lax.rem(z + m + 16, 16)

    def zpeer(m):
        return rid(y, zat(m), core)

    def copy(src, dst, ssem, rsem, rows, rep):
        return pltpu.make_async_remote_copy(
            src_ref=src, dst_ref=dst, send_sem=ssem, recv_sem=rsem,
            device_id={"rows": rows, "rep": rep}, device_id_type=MESH,
        )

    def send(src, dst, ssem, rsem, rows, rep):
        c = copy(src, dst, ssem, rsem, rows, rep)
        c.start()
        pending.append(c.wait_send)
        return c

    def to_core(src, dst, ssem, rsem):
        return send(src, dst, ssem, rsem, rid(y, z, other), x)

    barrier = pltpu.get_barrier_semaphore()

    def greet(rows, rep):
        pl.semaphore_signal(barrier, inc=1, device_id={"rows": rows, "rep": rep}, device_id_type=MESH)

    ins = []
    for n, (a, b) in enumerate(
        [(feats_h, feats), (idxt_h, idxt), (cnt_h, cnt), (w_h, w), (w1_h, w1), (w2_h, w2), (cot_h, cot)]
    ):
        c = pltpu.make_async_copy(a, b, in_s.at[n])
        c.start()
        ins.append(c)

    alone = x == zb
    swap_r, swap_x = rid(y, za * 4 + x, core), zb
    for m in (1, 2, 3, 4, 12, 13, 14, 15):
        greet(zpeer(m), x)
    for m in range(1, 16):
        py, px, pr = peer(m)
        greet(pr, px)
        greet(rid(py, z, other), px)
    greet(rid(y, z, other), x)

    @pl.when(jnp.logical_not(alone))
    def _():
        greet(swap_r, swap_x)

    mine = pl.ds(pl.multiple_of(x * 64, 64), 64)
    ins[0].wait()
    ins[1].wait()
    stage[0:64, :] = feats[mine, :]
    stage[64:80, :] = idxt[...].astype(F32).astype(BF)

    ins[2].wait()
    ins[3].wait()
    row = iota((512, 1), 0)
    plane, rest = row >> 4, row & 15
    source = ((rest >> 2) << 7) + ((plane >> 3) << 5) + ((rest & 3) << 3) + (plane & 7)
    order = one_hot(source == iota((512, 512), 1))
    for sq in range(4):
        alive = [one_hot(cnt[...] > x * 16 + sq * 4 + s4) for s4 in range(4)]
        live = w[:, sq * 512:(sq + 1) * 512] * jnp.concatenate(alive, axis=1)
        wtb[:, sq] = dot(order, live, 1, 1).astype(BF).reshape(32, 16, 256)

    pl.semaphore_wait(barrier, 40 - alone.astype(jnp.int32))

    def swap(src, dst, ssem, rsem):
        c = copy(src, dst, ssem, rsem, swap_r, swap_x)

        @pl.when(alone)
        def _():
            dst[...] = src[...]

        @pl.when(jnp.logical_not(alone))
        def _():
            c.start()

        def finish():
            @pl.when(jnp.logical_not(alone))
            def _():
                c.wait_recv()

        def sent():
            @pl.when(jnp.logical_not(alone))
            def _():
                c.wait_send()

        pending.append(sent)
        return finish

    swap_done = swap(stage, g1.at[za * 4 + x], sw_s, sw_r)

    wcopies = {}
    me8 = y * 2 + core
    for off in (2, 1, 3, 0):
        for mx in (2, 1, 3, 0):
            py, px = lax.rem(y + off, 4), lax.rem(x + mx, 4)
            for n, h in enumerate((core, other)):
                m = (off * 4 + mx) * 2 + n
                if m:
                    wcopies[m] = send(wtb.at[(py * 4 + px) * 2 + h], wr.at[me8, x], wx_s.at[m], wx_r.at[m],
                                      rid(py, z, h), px)
    wr[me8, x] = wtb[q * 2 + core]
    yield "prep"

    row, col = iota((256, 1), 0), iota((256, 256), 1)
    regroup = one_hot(((row & 63) << 2) + (row >> 6) == col)
    eye = one_hot(row == col)
    swap_done()
    yield "swap1"

    def gather_z(g, rows, cut, ssem, rsem, work):
        full, parts = pl.ds(0, rows), (pl.ds(0, cut), pl.ds(cut, rows - cut))

        moves = {}

        def move(dist, via):
            for d in range(2):
                sign = 1 if d == 0 else -1
                if via:
                    moves[d, via].wait_recv()
                part = parts[d] if dist == 8 else full
                piece = g.at[zat(-sign * via), part]
                moves[d, dist] = send(piece, piece, ssem.at[d, dist], rsem.at[d, dist], zpeer(sign * (dist - via)), x)
                for more in (8, 5) if dist == 6 else ():
                    part = parts[d] if more == 8 else full
                    piece = g.at[zat(-sign * via), part]
                    moves[d, more] = send(piece, piece, ssem.at[d, more], rsem.at[d, more],
                                          zpeer(sign * (more - via)), x)

        for dist in (4, 2, 1):
            move(dist, 0)
        work()
        move(3, 2)
        move(6, 4)
        move(7, 6)
        for dist in (1, 3, 5, 8, 7):
            for d in range(2):
                moves[d, dist].wait_recv()

    gather_z(g1, 80, 48, z1_s, z1_r, lambda: None)
    yield "gz1"

    ids = g1[:, 64:80, :].reshape(256, 128)
    lane = iota((256, 256), 1).astype(F32)
    for k in range(8):
        at = ((k // 2) * 16 + z) * 2 + k % 2
        rows = dot(ids, one_hot(iota((128, 256), 0) == at))
        oh[:, k * 64:(k + 1) * 64, :] = one_hot(rows == lane).reshape(4, 64, 256)
    for a in range(4):
        pk[a, :, 0:128] = dot(oh[a], g1[4 * a:4 * a + 4, 0:64, :].reshape(256, 128)).astype(BF)

    yield "picks1"


    def weights(k, off, n):
        for mx in range(4):
            m = ((4 - off) % 4 * 4 + mx) * 2 + n
            if m:
                wcopies[m].wait_recv()
        wb[k] = dot(regroup, wr[k].reshape(256, 256)).astype(BF)
        wf[k] = dot(eye, wb[k], 1, 1).astype(BF)

    def reduce_planes(width, prepare, own, rc, ab, rp, csem_s, csem_r, psem_s, psem_r):
        def partial(j, off, n):
            k = j * 2 + (other if n else core)
            prepare(k, off, n)
            picked = pk[:, pl.ds(pl.multiple_of(k * 64, 64), 64), 0:width].reshape(256, width)
            return dot(wf[k], picked)

        near = (2, 1, 3, 0)
        cs = []
        for off in near:
            j = lax.rem(y + off, 4)
            own[j] = partial(j, off, 1).astype(BF)
            cs.append(to_core(own.at[j], rc.at[j], csem_s.at[off], csem_r.at[off]))
        ps = []
        for n, off in enumerate(near):
            j = lax.rem(y + off, 4)
            mine_j = partial(j, off, 0)
            cs[n].wait_recv()
            ab[j] = (mine_j + rc[j].astype(F32)).astype(BF).reshape(4, 64, width)
            for mx in near:
                m = off * 4 + mx
                if m:
                    px = lax.rem(x + mx, 4)
                    ps.append((m, send(ab.at[j, px], rp.at[m], psem_s.at[m], psem_r.at[m], rid(j, z, core), px)))
        res = ab[y, x].astype(F32)
        for m, c in ps[::-1]:
            c.wait_recv()
            res = res + rp[m].astype(F32)
        return res.astype(BF)

    sw[0] = reduce_planes(128, weights, mine1, rc1, ab1, rp1, c1_s, c1_r, p1_s, p1_r)
    yield "red1"
    swap(sw.at[0], sw.at[1], sx_s, sx_r)()
    yield "swap2"
    for n in (4, 5, 6):
        ins[n].wait()
    agg1 = sw[1]
    z_one = dot(agg1, w1[...])
    g2[z] = (z_one * jax.nn.sigmoid(z_one)).astype(BF)

    def turn_picks():
        for a in range(4):
            oht[a] = dot(eye, oh[a], 1, 1).astype(BF)

    gather_z(g2, 64, 32, z2_s, z2_r, turn_picks)
    yield "gz2"
    for a in range(4):
        pk[a] = dot(oh[a], g2[4 * a:4 * a + 4].reshape(256, 256)).astype(BF)
    agg2 = reduce_planes(256, lambda k, off, n: None, mine2, rc2, ab2, rp2, c2_s, c2_r, p2_s, p2_r)
    yield "red2"

    z_two = dot(agg2, w2[...])
    dz2 = (cot[mine, :].astype(F32) * silu_slope(z_two)).astype(BF)
    bk[y, core, mine, :] = dot(dz2, w2[...], 1, 1).astype(BF)
    bcopies = {}
    for off in (2, 1, 3, 0):
        for mx in (2, 1, 3, 0):
            m = off * 4 + mx
            if m:
                py, px = lax.rem(y + off, 4), lax.rem(x + mx, 4)
                bcopies[m] = send(bk.at[y, core, mine], bk.at[y, core, mine], bp_s.at[m], bp_r.at[m],
                                  rid(py, z, core), px)
    out[mine, :] = (z_two * jax.nn.sigmoid(z_two)).astype(BF)
    ocopies = []
    for m in range(1, 4):
        ocopies.append(send(out.at[mine], out.at[mine], ox_s.at[m], ox_r.at[m], r, lax.rem(x + m, 4)))

    def reduce_all(ga, rc, gs, gp, gz, gt, c_s, c_r, p_s, p_r, z_s, z_r, t_s, t_r, d_s, d_r):
        c = to_core(ga.at[other], rc, c_s, c_r)
        yield
        c.wait_recv()
        gs[...] = ga[core] + rc[...]
        ps = []
        for m in range(1, 16):
            py, px, pr = peer(m)
            ps.append(send(gs.at[py * 4 + px], gp.at[m], p_s.at[m], p_r.at[m], pr, px))
        yield
        total = gs[q]
        for m in range(1, 16):
            ps[m - 1].wait_recv()
            total = total + gp[m]
        wide = gz.dtype == BF
        gz[0] = jnp.concatenate([total[:, :128], total[:, 128:]], axis=0).astype(BF) if wide else total
        zs = []
        for m in (8, 7, 9, 6, 10, 5, 11, 4, 12, 3, 13, 2, 14, 1, 15):
            zs.append(send(gz.at[0], gz.at[m], z_s.at[m], z_r.at[m], zpeer(m), x))
        yield
        for c in zs:
            c.wait_recv()
        total = gz[z].astype(F32)
        for k in range(1, 16):
            total = total + gz[lax.rem(z - k + 16, 16)].astype(F32)
        gt[core, q] = jnp.concatenate([total[:8], total[8:]], axis=1) if wide else total
        ts = []
        for m in range(1, 16):
            py, px, pr = peer(m)
            ts.append(send(gt.at[core, q], gt.at[core, q], t_s.at[m], t_r.at[m], pr, px))
        yield
        for c in ts:
            c.wait_recv()
        c = to_core(gt.at[core], gt.at[core], d_s, d_r)
        yield
        c.wait_recv()
        yield

    half = len(sums) // 2
    ga2, ga1 = sums[0], sums[half]
    reduce2, reduce1 = reduce_all(*sums[:half]), reduce_all(*sums[half:])
    ga2[...] = dot(agg2, dz2, 0, 0).reshape(2, 16, 8, 256)
    next(reduce2)


    def slot_terms(k):
        got = dot(wb[k], bk[lax.div(k, 2), lax.rem(k, 2)]).astype(BF)
        tt[:, pl.ds(pl.multiple_of(k * 64, 64), 64), :] = got.reshape(4, 64, 256)

    next(reduce2)
    cc = {}
    for off in (0, 1, 3, 2):
        j = lax.rem(y - off + 4, 4)
        for mx in range(4):
            if off * 4 + mx:
                bcopies[off * 4 + mx].wait_recv()
        cc[off] = to_core(bk.at[j, core], bk.at[j, core], bc_s.at[off], bc_r.at[off])
        slot_terms(j * 2 + core)
    next(reduce2)
    for off in (0, 1, 3, 2):
        cc[off].wait_recv()
        slot_terms(lax.rem(y - off + 4, 4) * 2 + other)
    yield "bwait"
    for a in range(4):
        pb[4 * a:4 * a + 4] = dot(oht[a], tt[a]).astype(BF).reshape(4, 64, 256)

    full, parts = pl.ds(0, 64), (pl.ds(0, 32), pl.ds(32, 32))
    ways = ((0, 1), (1, -1))
    moves = {}

    def pass_on(d, sign, dist, src, slot, hop, part=full):
        dst = fr.at[d, slot, part] if slot < 5 else nr.at[d, slot - 5]
        moves[d, dist] = send(src, dst, fr_s.at[d, dist], fr_r.at[d, dist], zpeer(sign * hop), x)

    for dist, slot, hop in ((7, 0, 1), (8, 3, 4), (5, 1, 1), (3, 4, 1), (1, 5, 1)):
        for d, sign in ways:
            part = parts[d] if dist == 8 else full
            pass_on(d, sign, dist, pb.at[zat(sign * dist), part], slot, hop, part)
    for dist, via, slot, out_slot in ((6, 7, 0, 2), (2, 3, 4, 6)):
        for d, sign in ways:
            moves[d, via].wait_recv()
            cb[d, dist // 2] = (pb[zat(sign * dist)].astype(F32) + fr[d, slot].astype(F32)).astype(BF)
            pass_on(d, sign, dist, cb.at[d, dist // 2], out_slot, 2)
    for d, sign in ways:
        moves[d, 5].wait_recv()
        moves[d, 6].wait_recv()
        acc = pb[zat(sign * 4)].astype(F32) + fr[d, 1].astype(F32) + fr[d, 2].astype(F32)
        moves[d, 8].wait_recv()
        cb[d, 2] = acc.astype(BF)
        lo = 0 if d == 0 else 32
        cb[d, 2, lo:lo + 32, :] = (acc[lo:lo + 32] + fr[d, 3, lo:lo + 32, :].astype(F32)).astype(BF)
        pass_on(d, sign, 4, cb.at[d, 2], 7, 4)
    next(reduce2)
    dh = pb[z].astype(F32)
    for dist, slot in ((1, 0), (2, 1), (4, 2)):
        for d in range(2):
            moves[d, dist].wait_recv()
            dh = dh + nr[d, slot].astype(F32)
    yield "rsz"
    dz1 = (dh * silu_slope(z_one)).astype(BF)
    grad1 = dot(agg1, dz1, 0, 0).reshape(2, 8, 8, 256)
    for b in range(2):
        ga1[:, :, b] = grad1[:, :, :, b * 128:(b + 1) * 128]
    ga1 = ga1.reshape(2, 16, 8, 128)
    reduce1 = reduce_all(ga1, *sums[half + 1:])
    next(reduce1)
    next(reduce2)
    yield "arc"
    next(reduce1)
    next(reduce2)
    gr2[...] = sums[5][...].reshape(256, 256)
    yield "arp"
    next(reduce1)
    yield "arz"
    next(reduce1)
    yield "art"
    next(reduce1)
    next(reduce1)
    gt1 = sums[half + 5]
    for b in range(2):
        for k in range(8):
            gr1[:, k, :, b * 128:(b + 1) * 128] = gt1[:, 2 * k + b]
    for c in ocopies:
        c.wait_recv()


def kernel(*refs):
    pending = []
    for _ in body(pending, *refs):
        pass
    for wait in pending:
        wait()


def place(*refs):
    copies = [pltpu.make_async_copy(refs[n], refs[3 + n], refs[6].at[n]) for n in range(3)]
    for c in copies:
        c.start()
    for c in copies:
        c.wait()


def local(feats, edge_w, send_rows, counts, w_one, w_two, cotangent):
    idxt = jnp.transpose(send_rows[0])
    vm = pl.BlockSpec(memory_space=pltpu.VMEM)
    hbm = pl.BlockSpec(memory_space=pl.ANY)
    args = (feats, idxt, counts, edge_w, w_one, w_two, cotangent)
    dma = pltpu.SemaphoreType.DMA

    def vmem(kind, *shape):
        return pltpu.VMEM(shape, kind)

    scratch = [pltpu.VMEM(a.shape, a.dtype) for a in args] + [
        vmem(BF, 32, 4, 16, 256),
        vmem(BF, 8, 4, 4, 16, 256),
        vmem(BF, 8, 256, 256),
        vmem(BF, 8, 256, 256),
        vmem(BF, 80, 128),
        vmem(BF, 16, 80, 128),
        vmem(BF, 4, 512, 256),
        vmem(BF, 4, 256, 512),
        vmem(BF, 4, 512, 256),
        vmem(BF, 4, 256, 128),
        vmem(BF, 4, 256, 128),
        vmem(BF, 4, 4, 64, 128),
        vmem(BF, 16, 64, 128),
        vmem(BF, 2, 64, 128),
        vmem(BF, 16, 64, 256),
        vmem(BF, 4, 256, 256),
        vmem(BF, 4, 256, 256),
        vmem(BF, 4, 4, 64, 256),
        vmem(BF, 16, 64, 256),
        vmem(BF, 4, 2, 256, 256),
        vmem(BF, 4, 512, 256),
        vmem(BF, 16, 64, 256),
        vmem(BF, 2, 5, 64, 256),
        vmem(BF, 2, 3, 64, 256),
        vmem(BF, 2, 4, 64, 256),
        dma((7,)), dma(()), dma(()), dma((32,)), dma((32,)), dma((2, 9)), dma((2, 9)),
        dma((4,)), dma((4,)), dma((16,)), dma((16,)), dma(()), dma(()), dma((2, 9)), dma((2, 9)),
        dma((4,)), dma((4,)), dma((16,)), dma((16,)), dma((4,)), dma((4,)), dma((16,)), dma((16,)),
        dma((4,)), dma((4,)), dma((2, 9)), dma((2, 9)),
    ]
    for width, first in ((256, (2, 16, 8, 256)), (128, (2, 8, 2, 8, 128))):
        scratch += [
            vmem(F32, *first),
            vmem(F32, 16, 8, width),
            vmem(F32, 16, 8, width),
            vmem(F32, 16, 8, width),
            vmem(BF, 16, 16, 128) if width == 256 else vmem(F32, 16, 8, width),
            vmem(F32, 2, 16, 8, width),
            dma(()), dma(()), dma((16,)), dma((16,)), dma((16,)), dma((16,)), dma((16,)), dma((16,)), dma(()), dma(()),
        ]
    out, gr1, gr2 = pl.pallas_call(
        kernel,
        out_shape=(
            jax.ShapeDtypeStruct((256, 256), BF),
            jax.ShapeDtypeStruct((2, 8, 8, 256), F32),
            jax.ShapeDtypeStruct((256, 256), F32),
        ),
        in_specs=[hbm] * 7,
        out_specs=(vm, vm, vm),
        scratch_shapes=scratch,
        compiler_params=pltpu.CompilerParams(
            collective_id=0, has_side_effects=True, vmem_limit_bytes=56 * 1024 * 1024
        ),
    )(*args)
    return pl.pallas_call(
        place,
        out_shape=(
            jax.ShapeDtypeStruct((256, 256), BF),
            jax.ShapeDtypeStruct((128, 256), F32),
            jax.ShapeDtypeStruct((256, 256), F32),
        ),
        in_specs=[hbm] * 3,
        out_specs=(hbm, hbm, hbm),
        scratch_shapes=[dma((3,))],
    )(out, gr1.reshape(128, 256), gr2)


def solution(mesh):
    in_specs = (
        P("rows", None),
        P("rows", "rep"),
        P("rows", None, "rep"),
        P("rows", None),
        P(),
        P(),
        P("rows", None),
    )
    out_specs = (P("rows", None), P(), P())
    return jax.shard_map(local, mesh=mesh, in_specs=in_specs, out_specs=out_specs, check_vma=False)
```

```python
import jax
import jax.numpy as jnp
from jax import lax
from jax.experimental import pallas as pl
from jax.experimental.pallas import tpu as pltpu
from jax.sharding import PartitionSpec as P

MESH = pl.DeviceIdType.MESH
BF = jnp.bfloat16
F32 = jnp.float32


def dot(a, b, ca=1, cb=0):
    return lax.dot_general(a, b, (((ca,), (cb,)), ((), ())), preferred_element_type=F32)


def silu_slope(values):
    sigma = jax.nn.sigmoid(values)
    return sigma * (1.0 + values * (1.0 - sigma))


def iota(shape, dim):
    return lax.broadcasted_iota(jnp.int32, shape, dim)


def each(lo, hi, fn):
    def step(n, carry):
        fn(n)
        return carry

    lax.fori_loop(lo, hi, step, 0)


def one_hot(hit):
    return jnp.where(hit, 1.0, 0.0).astype(BF)


def body(
    pending,
    feats_h, idxt_h, cnt_h, w_h, w1_h, w2_h, cot_h,
    out, gr1, gr2,
    feats, idxt, cnt, w, w1, w2, cot,
    wtb, wr, wb, wf, stage, g1, oh, oht, pk, mine1, rc1, ab1, rp1, sw, g2,
    mine2, rc2, ab2, rp2, bk, tt, pb, fr, nr, cb,
    in_s, sw_s, sw_r, wx_s, wx_r, z1_s, z1_r, c1_s, c1_r, p1_s, p1_r, sx_s, sx_r, z2_s, z2_r,
    c2_s, c2_r, p2_s, p2_r, ox_s, ox_r, bp_s, bp_r, bc_s, bc_r, fr_s, fr_r, nr_s, nr_r,
    *sums,
):
    r = lax.axis_index("rows")
    x = lax.axis_index("rep")
    core = lax.rem(r, 2)
    z = lax.rem(lax.div(r, 2), 16)
    y = lax.div(r, 32)
    za = lax.div(z, 4)
    zb = lax.rem(z, 4)
    q = y * 4 + x
    other = 1 - core

    def rid(yy, zz, cc):
        return (yy * 16 + zz) * 2 + cc

    def peer(m):
        pq = lax.rem(q + m, 16)
        py, px = lax.div(pq, 4), lax.rem(pq, 4)
        return py, px, rid(py, z, core)

    def zat(m):
        return lax.rem(z + m + 16, 16)

    def zpeer(m):
        return rid(y, zat(m), core)

    def copy(src, dst, ssem, rsem, rows, rep):
        return pltpu.make_async_remote_copy(
            src_ref=src, dst_ref=dst, send_sem=ssem, recv_sem=rsem,
            device_id={"rows": rows, "rep": rep}, device_id_type=MESH,
        )

    def send(src, dst, ssem, rsem, rows, rep):
        c = copy(src, dst, ssem, rsem, rows, rep)
        c.start()
        pending.append(c.wait_send)
        return c

    def start_all(lo, hi, make):
        each(lo, hi, lambda m: make(m).start())
        pending.append(lambda: each(lo, hi, lambda m: make(m).wait_send()))

    def rel(m):
        return lax.rem(y + lax.div(m, 4), 4), lax.rem(x + lax.rem(m, 4), 4)

    def to_core(src, dst, ssem, rsem):
        return send(src, dst, ssem, rsem, rid(y, z, other), x)

    barrier = pltpu.get_barrier_semaphore()

    def greet(rows, rep):
        pl.semaphore_signal(barrier, inc=1, device_id={"rows": rows, "rep": rep}, device_id_type=MESH)

    ins = []
    for n, (a, b) in enumerate(
        [(feats_h, feats), (idxt_h, idxt), (cnt_h, cnt), (w_h, w), (w1_h, w1), (w2_h, w2), (cot_h, cot)]
    ):
        c = pltpu.make_async_copy(a, b, in_s.at[n])
        c.start()
        ins.append(c)

    alone = x == zb
    swap_r, swap_x = rid(y, za * 4 + x, core), zb
    for m in (1, 2, 3, 4, 12, 13, 14, 15):
        greet(zpeer(m), x)
    for m in range(1, 16):
        py, px, pr = peer(m)
        greet(pr, px)
        greet(rid(py, z, other), px)
    greet(rid(y, z, other), x)

    @pl.when(jnp.logical_not(alone))
    def _():
        greet(swap_r, swap_x)

    mine = pl.ds(pl.multiple_of(x * 64, 64), 64)
    ins[0].wait()
    ins[1].wait()
    stage[0:64, :] = feats[mine, :]
    stage[64:80, :] = idxt[...].astype(F32).astype(BF)

    ins[2].wait()
    ins[3].wait()
    row = iota((512, 1), 0)
    plane, rest = row >> 4, row & 15
    source = ((rest >> 2) << 7) + ((plane >> 3) << 5) + ((rest & 3) << 3) + (plane & 7)
    order = one_hot(source == iota((512, 512), 1))
    def regroup_weights(sq):
        alive = [one_hot(cnt[...] > x * 16 + sq * 4 + s4) for s4 in range(4)]
        live = w[:, pl.ds(pl.multiple_of(sq * 512, 512), 512)] * jnp.concatenate(alive, axis=1)
        wtb[:, sq] = dot(order, live, 1, 1).astype(BF).reshape(32, 16, 256)

    each(0, 4, regroup_weights)
    pl.semaphore_wait(barrier, 40 - alone.astype(jnp.int32))

    def swap(src, dst, ssem, rsem):
        c = copy(src, dst, ssem, rsem, swap_r, swap_x)

        @pl.when(alone)
        def _():
            dst[...] = src[...]

        @pl.when(jnp.logical_not(alone))
        def _():
            c.start()

        def finish():
            @pl.when(jnp.logical_not(alone))
            def _():
                c.wait_recv()

        def sent():
            @pl.when(jnp.logical_not(alone))
            def _():
                c.wait_send()

        pending.append(sent)
        return finish

    swap_done = swap(stage, g1.at[za * 4 + x], sw_s, sw_r)

    me8 = y * 2 + core

    def weight_copy(m):
        py, px = rel(lax.div(m, 2))
        h = lax.rem(core + lax.rem(m, 2), 2)
        return copy(wtb.at[(py * 4 + px) * 2 + h], wr.at[me8, x], wx_s.at[m], wx_r.at[m], rid(py, z, h), px)

    start_all(1, 32, weight_copy)
    wr[me8, x] = wtb[q * 2 + core]
    yield "prep"

    row, col = iota((256, 1), 0), iota((256, 256), 1)
    regroup = one_hot(((row & 63) << 2) + (row >> 6) == col)
    eye = one_hot(row == col)
    swap_done()
    yield "swap1"

    def gather_z(g, rows, cut, ssem, rsem, work):
        full, parts = pl.ds(0, rows), (pl.ds(0, cut), pl.ds(cut, rows - cut))

        moves = {}

        def move(dist, via):
            for d in range(2):
                sign = 1 if d == 0 else -1
                if via:
                    moves[d, via].wait_recv()
                part = parts[d] if dist == 8 else full
                piece = g.at[zat(-sign * via), part]
                moves[d, dist] = send(piece, piece, ssem.at[d, dist], rsem.at[d, dist], zpeer(sign * (dist - via)), x)
                for more in (8, 5) if dist == 6 else ():
                    part = parts[d] if more == 8 else full
                    piece = g.at[zat(-sign * via), part]
                    moves[d, more] = send(piece, piece, ssem.at[d, more], rsem.at[d, more],
                                          zpeer(sign * (more - via)), x)

        for dist in (4, 2, 1):
            move(dist, 0)
        work()
        move(3, 2)
        move(6, 4)
        move(7, 6)
        for dist in (1, 3, 5, 8, 7):
            for d in range(2):
                moves[d, dist].wait_recv()

    gather_z(g1, 80, 48, z1_s, z1_r, lambda: None)
    yield "gz1"

    ids = g1[:, 64:80, :].reshape(256, 128)
    lane = iota((256, 256), 1).astype(F32)

    def pick_rows(k):
        at = (lax.div(k, 2) * 16 + z) * 2 + lax.rem(k, 2)
        rows = dot(ids, one_hot(iota((128, 256), 0) == at))
        oh[:, pl.ds(pl.multiple_of(k * 64, 64), 64), :] = one_hot(rows == lane).reshape(4, 64, 256)

    each(0, 8, pick_rows)

    def pick1(a):
        pk[a, :, 0:128] = dot(oh[a], g1[pl.ds(a * 4, 4), 0:64, :].reshape(256, 128)).astype(BF)

    each(0, 4, pick1)
    yield "picks1"


    def weights(k, off, n):
        def arrived(mx):
            m = (lax.rem(4 - off, 4) * 4 + mx) * 2 + n

            @pl.when(m > 0)
            def _():
                weight_copy(m).wait_recv()

        each(0, 4, arrived)
        wb[k] = dot(regroup, wr[k].reshape(256, 256)).astype(BF)
        wf[k] = dot(eye, wb[k], 1, 1).astype(BF)

    def reduce_planes(width, prepare, own, rc, ab, rp, csem_s, csem_r, psem_s, psem_r):
        def partial(j, off, n):
            k = j * 2 + (other if n else core)
            prepare(k, off, n)
            picked = pk[:, pl.ds(pl.multiple_of(k * 64, 64), 64), 0:width].reshape(256, width)
            return dot(wf[k], picked)

        def swap_half(n):
            off = lax.rem(n + 2, 4)
            j = lax.rem(y + off, 4)
            return off, j, copy(own.at[j], rc.at[j], csem_s.at[off], csem_r.at[off], rid(y, z, other), x)

        def other_half(n):
            off, j, c = swap_half(n)
            own[j] = partial(j, off, 1).astype(BF)
            c.start()

        each(0, 4, other_half)
        pending.append(lambda: each(0, 4, lambda n: swap_half(n)[2].wait_send()))

        def piece(m):
            py, px = rel(m)
            return copy(ab.at[py, px], rp.at[m], psem_s.at[m], psem_r.at[m], rid(py, z, core), px)

        def own_half(n):
            off, j, c = swap_half(n)
            mine_j = partial(j, off, 0)
            c.wait_recv()
            ab[j] = (mine_j + rc[j].astype(F32)).astype(BF).reshape(4, 64, width)
            for mx in (2, 1, 3):
                piece(off * 4 + mx).start()

            @pl.when(off > 0)
            def _():
                piece(off * 4).start()

        each(0, 4, own_half)
        pending.append(lambda: each(1, 16, lambda m: piece(m).wait_send()))

        def add(m, res):
            piece(m).wait_recv()
            return res + rp[m].astype(F32)

        return lax.fori_loop(1, 16, add, ab[y, x].astype(F32)).astype(BF)

    sw[0] = reduce_planes(128, weights, mine1, rc1, ab1, rp1, c1_s, c1_r, p1_s, p1_r)
    yield "red1"
    swap(sw.at[0], sw.at[1], sx_s, sx_r)()
    yield "swap2"
    for n in (4, 5, 6):
        ins[n].wait()
    agg1 = sw[1]
    z_one = dot(agg1, w1[...])
    g2[z] = (z_one * jax.nn.sigmoid(z_one)).astype(BF)

    def turn_picks():
        def turn(a):
            oht[a] = dot(eye, oh[a], 1, 1).astype(BF)

        each(0, 4, turn)

    gather_z(g2, 64, 32, z2_s, z2_r, turn_picks)
    yield "gz2"

    def pick2(a):
        pk[a] = dot(oh[a], g2[pl.ds(a * 4, 4)].reshape(256, 256)).astype(BF)

    each(0, 4, pick2)
    agg2 = reduce_planes(256, lambda k, off, n: None, mine2, rc2, ab2, rp2, c2_s, c2_r, p2_s, p2_r)
    yield "red2"

    z_two = dot(agg2, w2[...])
    dz2 = (cot[mine, :].astype(F32) * silu_slope(z_two)).astype(BF)
    bk[y, core, mine, :] = dot(dz2, w2[...], 1, 1).astype(BF)

    def back_copy(m):
        py, px = rel(m)
        return copy(bk.at[y, core, mine], bk.at[y, core, mine], bp_s.at[m], bp_r.at[m], rid(py, z, core), px)

    start_all(1, 16, back_copy)
    out[mine, :] = (z_two * jax.nn.sigmoid(z_two)).astype(BF)
    ocopies = []
    for m in range(1, 4):
        ocopies.append(send(out.at[mine], out.at[mine], ox_s.at[m], ox_r.at[m], r, lax.rem(x + m, 4)))

    def reduce_all(ga, rc, gs, gp, gz, gt, c_s, c_r, p_s, p_r, z_s, z_r, t_s, t_r, d_s, d_r):
        c = to_core(ga.at[other], rc, c_s, c_r)
        yield
        c.wait_recv()
        gs[...] = ga[core] + rc[...]

        def part(m):
            py, px = rel(m)
            return copy(gs.at[py * 4 + px], gp.at[m], p_s.at[m], p_r.at[m], rid(py, z, core), px)

        start_all(1, 16, part)
        yield

        def add(m, total):
            part(m).wait_recv()
            return total + gp[m]

        total = lax.fori_loop(1, 16, add, gs[q])
        wide = gz.dtype == BF
        gz[0] = jnp.concatenate([total[:, :128], total[:, 128:]], axis=0).astype(BF) if wide else total

        def along_z(n):
            m = lax.rem(8 + (1 - 2 * lax.rem(n, 2)) * lax.div(n + 1, 2), 16)
            return copy(gz.at[0], gz.at[m], z_s.at[m], z_r.at[m], zpeer(m), x)

        start_all(0, 15, along_z)
        yield
        each(0, 15, lambda n: along_z(n).wait_recv())
        total = lax.fori_loop(
            1, 16, lambda k, t: t + gz[lax.rem(z - k + 16, 16)].astype(F32), gz[z].astype(F32)
        )
        gt[core, q] = jnp.concatenate([total[:8], total[8:]], axis=1) if wide else total

        def whole(m):
            py, px = rel(m)
            return copy(gt.at[core, q], gt.at[core, q], t_s.at[m], t_r.at[m], rid(py, z, core), px)

        start_all(1, 16, whole)
        yield
        each(1, 16, lambda m: whole(m).wait_recv())
        c = to_core(gt.at[core], gt.at[core], d_s, d_r)
        yield
        c.wait_recv()
        yield

    half = len(sums) // 2
    ga2, ga1 = sums[0], sums[half]
    reduce2, reduce1 = reduce_all(*sums[:half]), reduce_all(*sums[half:])
    ga2[...] = dot(agg2, dz2, 0, 0).reshape(2, 16, 8, 256)
    next(reduce2)


    def slot_terms(k):
        got = dot(wb[k], bk[lax.div(k, 2), lax.rem(k, 2)]).astype(BF)
        tt[:, pl.ds(pl.multiple_of(k * 64, 64), 64), :] = got.reshape(4, 64, 256)

    next(reduce2)

    def block_copy(off):
        j = lax.rem(y - off + 4, 4)
        return j, copy(bk.at[j, core], bk.at[j, core], bc_s.at[off], bc_r.at[off], rid(y, z, other), x)

    def own_block(off):
        j, c = block_copy(off)

        def arrived(mx):
            @pl.when(off * 4 + mx > 0)
            def _():
                back_copy(off * 4 + mx).wait_recv()

        each(0, 4, arrived)
        c.start()
        slot_terms(j * 2 + core)

    def other_block(off):
        j, c = block_copy(off)
        c.wait_recv()
        slot_terms(j * 2 + other)

    each(0, 4, own_block)
    pending.append(lambda: each(0, 4, lambda off: block_copy(off)[1].wait_send()))
    next(reduce2)
    each(0, 4, other_block)
    yield "bwait"

    def row_terms(a):
        pb[pl.ds(a * 4, 4)] = dot(oht[a], tt[a]).astype(BF).reshape(4, 64, 256)

    each(0, 4, row_terms)

    full, parts = pl.ds(0, 64), (pl.ds(0, 32), pl.ds(32, 32))
    fars, nears = {}, {}
    for m in (4, 3, 2, 1):
        for d in range(2):
            sign = 1 if d == 0 else -1
            part = parts[d] if m == 4 else full
            fars[d, m] = send(pb.at[zat(sign * (4 + m)), part], fr.at[d, m, part], fr_s.at[d, m], fr_r.at[d, m],
                              zpeer(sign * m), x)
    for m in (3, 2, 1):
        for d in range(2):
            sign = 1 if d == 0 else -1
            nears[d, m] = send(pb.at[zat(sign * m)], nr.at[d, m], nr_s.at[d, m], nr_r.at[d, m], zpeer(sign * m), x)
    for d in range(2):
        sign = 1 if d == 0 else -1
        acc = pb[zat(sign * 4)].astype(F32)
        for m in (1, 2, 3):
            fars[d, m].wait_recv()
            acc = acc + fr[d, m].astype(F32)
        fars[d, 4].wait_recv()
        cb[d] = acc.astype(BF)
        lo = 0 if d == 0 else 32
        cb[d, lo:lo + 32, :] = (acc[lo:lo + 32] + fr[d, 4, lo:lo + 32, :].astype(F32)).astype(BF)
        nears[d, 4] = send(cb.at[d], nr.at[d, 4], nr_s.at[d, 4], nr_r.at[d, 4], zpeer(sign * 4), x)
    next(reduce2)
    dh = pb[z].astype(F32)
    for m in (1, 2, 3, 4):
        for d in range(2):
            nears[d, m].wait_recv()
            dh = dh + nr[d, m].astype(F32)
    yield "rsz"
    dz1 = (dh * silu_slope(z_one)).astype(BF)
    grad1 = dot(agg1, dz1, 0, 0).reshape(2, 8, 8, 256)
    for b in range(2):
        ga1[:, :, b] = grad1[:, :, :, b * 128:(b + 1) * 128]
    ga1 = ga1.reshape(2, 16, 8, 128)
    reduce1 = reduce_all(ga1, *sums[half + 1:])
    next(reduce1)
    next(reduce2)
    yield "arc"
    next(reduce1)
    next(reduce2)
    gr2[...] = sums[5][...].reshape(256, 256)
    yield "arp"
    next(reduce1)
    yield "arz"
    next(reduce1)
    yield "art"
    next(reduce1)
    next(reduce1)
    gt1 = sums[half + 5]
    for b in range(2):
        for k in range(8):
            gr1[:, k, :, b * 128:(b + 1) * 128] = gt1[:, 2 * k + b]
    for c in ocopies:
        c.wait_recv()


def kernel(*refs):
    pending = []
    for _ in body(pending, *refs):
        pass
    for wait in pending:
        wait()


def local(feats, edge_w, send_rows, counts, w_one, w_two, cotangent):
    idxt = jnp.transpose(send_rows[0])
    vm = pl.BlockSpec(memory_space=pltpu.VMEM)
    hbm = pl.BlockSpec(memory_space=pl.ANY)
    args = (feats, idxt, counts, edge_w, w_one, w_two, cotangent)
    dma = pltpu.SemaphoreType.DMA

    def vmem(kind, *shape):
        return pltpu.VMEM(shape, kind)

    scratch = [pltpu.VMEM(a.shape, a.dtype) for a in args] + [
        vmem(BF, 32, 4, 16, 256),
        vmem(BF, 8, 4, 4, 16, 256),
        vmem(BF, 8, 256, 256),
        vmem(BF, 8, 256, 256),
        vmem(BF, 80, 128),
        vmem(BF, 16, 80, 128),
        vmem(BF, 4, 512, 256),
        vmem(BF, 4, 256, 512),
        vmem(BF, 4, 512, 256),
        vmem(BF, 4, 256, 128),
        vmem(BF, 4, 256, 128),
        vmem(BF, 4, 4, 64, 128),
        vmem(BF, 16, 64, 128),
        vmem(BF, 2, 64, 128),
        vmem(BF, 16, 64, 256),
        vmem(BF, 4, 256, 256),
        vmem(BF, 4, 256, 256),
        vmem(BF, 4, 4, 64, 256),
        vmem(BF, 16, 64, 256),
        vmem(BF, 4, 2, 256, 256),
        vmem(BF, 4, 512, 256),
        vmem(BF, 16, 64, 256),
        vmem(BF, 2, 5, 64, 256),
        vmem(BF, 2, 5, 64, 256),
        vmem(BF, 2, 64, 256),
        dma((7,)), dma(()), dma(()), dma((32,)), dma((32,)), dma((2, 9)), dma((2, 9)),
        dma((4,)), dma((4,)), dma((16,)), dma((16,)), dma(()), dma(()), dma((2, 9)), dma((2, 9)),
        dma((4,)), dma((4,)), dma((16,)), dma((16,)), dma((4,)), dma((4,)), dma((16,)), dma((16,)),
        dma((4,)), dma((4,)), dma((2, 5)), dma((2, 5)), dma((2, 5)), dma((2, 5)),
    ]
    for width, first in ((256, (2, 16, 8, 256)), (128, (2, 8, 2, 8, 128))):
        scratch += [
            vmem(F32, *first),
            vmem(F32, 16, 8, width),
            vmem(F32, 16, 8, width),
            vmem(F32, 16, 8, width),
            vmem(BF, 16, 16, 128) if width == 256 else vmem(F32, 16, 8, width),
            vmem(F32, 2, 16, 8, width),
            dma(()), dma(()), dma((16,)), dma((16,)), dma((16,)), dma((16,)), dma((16,)), dma((16,)), dma(()), dma(()),
        ]
    out, gr1, gr2 = pl.pallas_call(
        kernel,
        out_shape=(
            jax.ShapeDtypeStruct((256, 256), BF),
            jax.ShapeDtypeStruct((2, 8, 8, 256), F32),
            jax.ShapeDtypeStruct((256, 256), F32),
        ),
        in_specs=[hbm] * 7,
        out_specs=(vm, vm, vm),
        scratch_shapes=scratch,
        compiler_params=pltpu.CompilerParams(
            collective_id=0, has_side_effects=True, vmem_limit_bytes=56 * 1024 * 1024
        ),
    )(*args)
    return out, gr1.reshape(128, 256), gr2


def solution(mesh):
    in_specs = (
        P("rows", None),
        P("rows", "rep"),
        P("rows", None, "rep"),
        P("rows", None),
        P(),
        P(),
        P("rows", None),
    )
    out_specs = (P("rows", None), P(), P())
    return jax.shard_map(local, mesh=mesh, in_specs=in_specs, out_specs=out_specs, check_vma=False)
```

```python
import jax
import jax.numpy as jnp
from jax import lax
from jax.experimental import pallas as pl
from jax.experimental.pallas import tpu as pltpu
from jax.sharding import PartitionSpec as P

MESH = pl.DeviceIdType.MESH
BF = jnp.bfloat16
F32 = jnp.float32


def dot(a, b, ca=1, cb=0):
    return lax.dot_general(a, b, (((ca,), (cb,)), ((), ())), preferred_element_type=F32)


def silu_slope(values):
    sigma = jax.nn.sigmoid(values)
    return sigma * (1.0 + values * (1.0 - sigma))


def iota(shape, dim):
    return lax.broadcasted_iota(jnp.int32, shape, dim)


def one_hot(hit):
    return jnp.where(hit, 1.0, 0.0).astype(BF)


def body(
    pending,
    feats_h, idxt_h, cnt_h, w_h, w1_h, w2_h, cot_h,
    out, gr1, gr2,
    feats, idxt, cnt, w, w1, w2, cot,
    wtb, wr, wb, wf, stage, g1, oh, oht, pk, mine1, rc1, ab1, rp1, sw, g2,
    mine2, rc2, ab2, rp2, bk, tt, pb, fr, nr, cb,
    in_s, sw_s, sw_r, wx_s, wx_r, z1_s, z1_r, c1_s, c1_r, p1_s, p1_r, sx_s, sx_r, z2_s, z2_r,
    c2_s, c2_r, p2_s, p2_r, ox_s, ox_r, bp_s, bp_r, bc_s, bc_r, fr_s, fr_r, nr_r,
    *sums,
):
    r = lax.axis_index("rows")
    x = lax.axis_index("rep")
    core = lax.rem(r, 2)
    z = lax.rem(lax.div(r, 2), 16)
    y = lax.div(r, 32)
    za = lax.div(z, 4)
    zb = lax.rem(z, 4)
    q = y * 4 + x
    other = 1 - core

    def rid(yy, zz, cc):
        return (yy * 16 + zz) * 2 + cc

    def peer(m):
        pq = lax.rem(q + m, 16)
        py, px = lax.div(pq, 4), lax.rem(pq, 4)
        return py, px, rid(py, z, core)

    def zat(m):
        return lax.rem(z + m + 16, 16)

    def zpeer(m):
        return rid(y, zat(m), core)

    def copy(src, dst, ssem, rsem, rows, rep):
        return pltpu.make_async_remote_copy(
            src_ref=src, dst_ref=dst, send_sem=ssem, recv_sem=rsem,
            device_id={"rows": rows, "rep": rep}, device_id_type=MESH,
        )

    def send(src, dst, ssem, rsem, rows, rep):
        c = copy(src, dst, ssem, rsem, rows, rep)
        c.start()
        return c

    def sent(ref, sem):
        pending.append(copy(ref, ref, sem, sem, rid(y, z, other), x).wait_send)

    def received(ref, sem):
        copy(ref, ref, sem, sem, rid(y, z, other), x).wait_recv()

    def to_core(src, dst, ssem, rsem):
        return send(src, dst, ssem, rsem, rid(y, z, other), x)

    barrier = pltpu.get_barrier_semaphore()

    def greet(rows, rep):
        pl.semaphore_signal(barrier, inc=1, device_id={"rows": rows, "rep": rep}, device_id_type=MESH)

    alone = x == zb
    swap_r, swap_x = rid(y, za * 4 + x, core), zb
    for m in (1, 2, 3, 4, 12, 13, 14, 15):
        greet(zpeer(m), x)
    for m in range(1, 16):
        py, px, pr = peer(m)
        greet(pr, px)
        greet(rid(py, z, other), px)
    greet(rid(y, z, other), x)

    @pl.when(jnp.logical_not(alone))
    def _():
        greet(swap_r, swap_x)

    ins = []
    for n, (a, b) in enumerate(
        [(feats_h, feats), (idxt_h, idxt), (cnt_h, cnt), (w_h, w), (w1_h, w1), (w2_h, w2), (cot_h, cot)]
    ):
        c = pltpu.make_async_copy(a, b, in_s.at[n])
        c.start()
        ins.append(c)

    mine = pl.ds(pl.multiple_of(x * 64, 64), 64)
    ins[0].wait()
    ins[1].wait()
    stage[0:64, :] = feats[mine, :]
    stage[64:80, :] = idxt[...].astype(F32).astype(BF)

    ins[2].wait()
    ins[3].wait()
    row = iota((512, 1), 0)
    plane, rest = row >> 4, row & 15
    source = ((rest >> 2) << 7) + ((plane >> 3) << 5) + ((rest & 3) << 3) + (plane & 7)
    order = one_hot(source == iota((512, 512), 1))
    for sq in range(4):
        alive = [one_hot(cnt[...] > x * 16 + sq * 4 + s4) for s4 in range(4)]
        live = w[:, sq * 512:(sq + 1) * 512] * jnp.concatenate(alive, axis=1)
        wtb[:, sq] = dot(order, live, 1, 1).astype(BF).reshape(32, 16, 256)

    pl.semaphore_wait(barrier, 40 - alone.astype(jnp.int32))

    def swap(src, dst, ssem, rsem):
        c = copy(src, dst, ssem, rsem, swap_r, swap_x)

        @pl.when(alone)
        def _():
            dst[...] = src[...]

        @pl.when(jnp.logical_not(alone))
        def _():
            c.start()

        def finish():
            @pl.when(jnp.logical_not(alone))
            def _():
                c.wait_recv()

        def sent():
            @pl.when(jnp.logical_not(alone))
            def _():
                c.wait_send()

        pending.append(sent)
        return finish

    swap_done = swap(stage, g1.at[za * 4 + x], sw_s, sw_r)

    me8 = y * 2 + core
    for off in (2, 1, 3, 0):
        for mx in (2, 1, 3, 0):
            py, px = lax.rem(y + off, 4), lax.rem(x + mx, 4)
            for n, h in enumerate((core, other)):
                if off + mx + n:
                    send(wtb.at[(py * 4 + px) * 2 + h], wr.at[me8 * 4 + x], wx_s, wx_r, rid(py, z, h), px)
    sent(wtb.at[pl.ds(0, 31)], wx_s)
    wr[me8 * 4 + x] = wtb[q * 2 + core]
    yield "prep"

    row, col = iota((256, 1), 0), iota((256, 256), 1)
    regroup = one_hot(((row & 63) << 2) + (row >> 6) == col)
    eye = one_hot(row == col)
    swap_done()
    yield "swap1"

    def gather_z(g, rows, cut, ssem, rsem, work):
        full, parts = pl.ds(0, rows), (pl.ds(0, cut), pl.ds(cut, rows - cut))

        relay = {}

        def move(dist, via):
            for d in range(2):
                sign = 1 if d == 0 else -1
                if via:
                    relay[d, via].wait_recv()
                for there in (6, 8, 5) if dist == 6 else (dist,):
                    piece = g.at[zat(-sign * via), parts[d] if there == 8 else full]
                    sem = rsem.at[d * 3 + there // 2 - 1] if there in (2, 4, 6) else rsem.at[6]
                    relay[d, there] = send(piece, piece, ssem, sem, zpeer(sign * (there - via)), x)

        for dist in (4, 2, 1):
            move(dist, 0)
        work()
        move(3, 2)
        move(6, 4)
        move(7, 6)
        sent(g.at[pl.ds(0, 15)], ssem)
        received(g.at[pl.ds(0, 9)], rsem.at[6])

    gather_z(g1, 80, 48, z1_s, z1_r, lambda: None)
    yield "gz1"

    ids = g1[:, 64:80, :].reshape(256, 128)
    lane = iota((256, 256), 1).astype(F32)
    for k in range(8):
        at = ((k // 2) * 16 + z) * 2 + k % 2
        rows = dot(ids, one_hot(iota((128, 256), 0) == at))
        oh[:, k * 64:(k + 1) * 64, :] = one_hot(rows == lane).reshape(4, 64, 256)
    for a in range(4):
        pk[a, :, 0:128] = dot(oh[a], g1[4 * a:4 * a + 4, 0:64, :].reshape(256, 128)).astype(BF)

    yield "picks1"


    received(wr.at[pl.ds(0, 31)], wx_r)

    def weights(k):
        wb[k] = dot(regroup, wr[pl.ds(k * 4, 4)].reshape(256, 256)).astype(BF)
        wf[k] = dot(eye, wb[k], 1, 1).astype(BF)

    def reduce_planes(width, prepare, own, rc, ab, rp, csem_s, csem_r, psem_s, psem_r):
        def partial(k):
            prepare(k)
            picked = pk[:, pl.ds(pl.multiple_of(k * 64, 64), 64), 0:width].reshape(256, width)
            return dot(wf[k], picked)

        near = (2, 1, 3, 0)
        cs = []
        for off in near:
            j = lax.rem(y + off, 4)
            own[j] = partial(j * 2 + other).astype(BF)
            cs.append(to_core(own.at[j], rc.at[j], csem_s, csem_r.at[off]))
        sent(own, csem_s)
        for n, off in enumerate(near):
            j = lax.rem(y + off, 4)
            mine_j = partial(j * 2 + core)
            cs[n].wait_recv()
            ab[j] = (mine_j + rc[j].astype(F32)).astype(BF).reshape(4, 64, width)
            for mx in near:
                m = off * 4 + mx
                if m:
                    px = lax.rem(x + mx, 4)
                    send(ab.at[j, px], rp.at[m], psem_s, psem_r, rid(j, z, core), px)
        sent(rp.at[pl.ds(1, 15)], psem_s)
        received(rp.at[pl.ds(1, 15)], psem_r)
        res = ab[y, x].astype(F32)
        for m in range(1, 16):
            res = res + rp[m].astype(F32)
        return res.astype(BF)

    sw[0] = reduce_planes(128, weights, mine1, rc1, ab1, rp1, c1_s, c1_r, p1_s, p1_r)
    yield "red1"
    swap(sw.at[0], sw.at[1], sx_s, sx_r)()
    yield "swap2"
    for n in (4, 5, 6):
        ins[n].wait()
    agg1 = sw[1]
    z_one = dot(agg1, w1[...])
    g2[z] = (z_one * jax.nn.sigmoid(z_one)).astype(BF)

    def turn_picks():
        for a in range(4):
            oht[a] = dot(eye, oh[a], 1, 1).astype(BF)

    gather_z(g2, 64, 32, z2_s, z2_r, turn_picks)
    yield "gz2"
    for a in range(4):
        pk[a] = dot(oh[a], g2[4 * a:4 * a + 4].reshape(256, 256)).astype(BF)
    agg2 = reduce_planes(256, lambda k: None, mine2, rc2, ab2, rp2, c2_s, c2_r, p2_s, p2_r)
    yield "red2"

    z_two = dot(agg2, w2[...])
    dz2 = (cot[mine, :].astype(F32) * silu_slope(z_two)).astype(BF)
    bk[y, core, mine, :] = dot(dz2, w2[...], 1, 1).astype(BF)
    for off in (2, 1, 3, 0):
        for mx in (2, 1, 3, 0):
            m = off * 4 + mx
            if m:
                py, px = lax.rem(y + off, 4), lax.rem(x + mx, 4)
                send(bk.at[y, core, mine], bk.at[y, core, mine], bp_s, bp_r.at[off], rid(py, z, core), px)
    sent(pb.at[pl.ds(0, 15)], bp_s)
    out[mine, :] = (z_two * jax.nn.sigmoid(z_two)).astype(BF)
    for m in range(1, 4):
        send(out.at[mine], out.at[mine], ox_s, ox_r, r, lax.rem(x + m, 4))
    sent(out.at[pl.ds(0, 192)], ox_s)

    def reduce_all(ga, rc, gs, gp, gz, gt, c_s, c_r, p_s, p_r, z_s, z_r, t_s, t_r, d_s, d_r):
        c = to_core(ga.at[other], rc, c_s, c_r)
        sent(rc, c_s)
        yield
        c.wait_recv()
        gs[...] = ga[core] + rc[...]
        for m in range(1, 16):
            py, px, pr = peer(m)
            send(gs.at[py * 4 + px], gp.at[m], p_s, p_r, pr, px)
        sent(gp.at[pl.ds(1, 15)], p_s)
        yield
        received(gp.at[pl.ds(1, 15)], p_r)
        total = gs[q]
        for m in range(1, 16):
            total = total + gp[m]
        wide = gz.dtype == BF
        gz[0] = jnp.concatenate([total[:, :128], total[:, 128:]], axis=0).astype(BF) if wide else total
        for m in (8, 7, 9, 6, 10, 5, 11, 4, 12, 3, 13, 2, 14, 1, 15):
            send(gz.at[0], gz.at[m], z_s, z_r, zpeer(m), x)
        sent(gz.at[pl.ds(1, 15)], z_s)
        yield
        received(gz.at[pl.ds(1, 15)], z_r)
        total = gz[z].astype(F32)
        for k in range(1, 16):
            total = total + gz[lax.rem(z - k + 16, 16)].astype(F32)
        gt[core, q] = jnp.concatenate([total[:8], total[8:]], axis=1) if wide else total
        for m in range(1, 16):
            py, px, pr = peer(m)
            send(gt.at[core, q], gt.at[core, q], t_s, t_r, pr, px)
        sent(gt.at[core, pl.ds(0, 15)], t_s)
        yield
        received(gt.at[core, pl.ds(0, 15)], t_r)
        c = to_core(gt.at[core], gt.at[core], d_s, d_r)
        sent(gt.at[core], d_s)
        yield
        c.wait_recv()
        yield

    half = len(sums) // 2
    ga2, ga1 = sums[0], sums[half]
    reduce2, reduce1 = reduce_all(*sums[:half]), reduce_all(*sums[half:])
    ga2[...] = dot(agg2, dz2, 0, 0).reshape(2, 16, 8, 256)
    next(reduce2)


    def slot_terms(k):
        got = dot(wb[k], bk[lax.div(k, 2), lax.rem(k, 2)]).astype(BF)
        tt[:, pl.ds(pl.multiple_of(k * 64, 64), 64), :] = got.reshape(4, 64, 256)

    next(reduce2)
    cc = {}
    for off in (0, 1, 3, 2):
        j = lax.rem(y - off + 4, 4)
        received(bk.at[j, core] if off else bk.at[j, core, pl.ds(0, 192)], bp_r.at[off])
        cc[off] = to_core(bk.at[j, core], bk.at[j, core], bc_s, bc_r.at[off])
        slot_terms(j * 2 + core)
    sent(bk.at[:, 0], bc_s)
    next(reduce2)
    for off in (0, 1, 3, 2):
        cc[off].wait_recv()
        slot_terms(lax.rem(y - off + 4, 4) * 2 + other)
    yield "bwait"
    for a in range(4):
        pb[4 * a:4 * a + 4] = dot(oht[a], tt[a]).astype(BF).reshape(4, 64, 256)

    full, parts = pl.ds(0, 64), (pl.ds(0, 32), pl.ds(32, 32))
    fars, nears = {}, {}
    for m in (4, 3, 2, 1):
        for d in range(2):
            sign = 1 if d == 0 else -1
            part = parts[d] if m == 4 else full
            fars[d, m] = send(pb.at[zat(sign * (4 + m)), part], fr.at[d, m, part], fr_s, fr_r.at[d, 1 if m == 4 else 0],
                              zpeer(sign * m), x)
    for m in (3, 2, 1):
        for d in range(2):
            sign = 1 if d == 0 else -1
            nears[d, m] = send(pb.at[zat(sign * m)], nr.at[d, m], fr_s, nr_r.at[d], zpeer(sign * m), x)
    for d in range(2):
        sign = 1 if d == 0 else -1
        acc = pb[zat(sign * 4)].astype(F32)
        received(fr.at[d, pl.ds(1, 3)], fr_r.at[d, 0])
        for m in (1, 2, 3):
            acc = acc + fr[d, m].astype(F32)
        fars[d, 4].wait_recv()
        cb[d] = acc.astype(BF)
        lo = 0 if d == 0 else 32
        cb[d, lo:lo + 32, :] = (acc[lo:lo + 32] + fr[d, 4, lo:lo + 32, :].astype(F32)).astype(BF)
        nears[d, 4] = send(cb.at[d], nr.at[d, 4], fr_s, nr_r.at[d], zpeer(sign * 4), x)
    next(reduce2)
    dh = pb[z].astype(F32)
    sent(pb.at[pl.ds(0, 15)], fr_s)
    for d in range(2):
        received(nr.at[d, pl.ds(1, 4)], nr_r.at[d])
        for m in (1, 2, 3, 4):
            dh = dh + nr[d, m].astype(F32)
    yield "rsz"
    dz1 = (dh * silu_slope(z_one)).astype(BF)
    grad1 = dot(agg1, dz1, 0, 0).reshape(2, 8, 8, 256)
    for b in range(2):
        ga1[:, :, b] = grad1[:, :, :, b * 128:(b + 1) * 128]
    ga1 = ga1.reshape(2, 16, 8, 128)
    reduce1 = reduce_all(ga1, *sums[half + 1:])
    next(reduce1)
    next(reduce2)
    yield "arc"
    next(reduce1)
    next(reduce2)
    gr2[...] = sums[5][...].reshape(256, 256)
    yield "arp"
    next(reduce1)
    yield "arz"
    next(reduce1)
    yield "art"
    next(reduce1)
    next(reduce1)
    gt1 = sums[half + 5]
    for b in range(2):
        for k in range(8):
            gr1[:, k, :, b * 128:(b + 1) * 128] = gt1[:, 2 * k + b]
    received(out.at[pl.ds(0, 192)], ox_r)


def kernel(*refs):
    pending = []
    for _ in body(pending, *refs):
        pass
    for wait in pending:
        wait()


def local(feats, edge_w, send_rows, counts, w_one, w_two, cotangent):
    idxt = jnp.transpose(send_rows[0])
    vm = pl.BlockSpec(memory_space=pltpu.VMEM)
    hbm = pl.BlockSpec(memory_space=pl.ANY)
    args = (feats, idxt, counts, edge_w, w_one, w_two, cotangent)
    dma = pltpu.SemaphoreType.DMA

    def vmem(kind, *shape):
        return pltpu.VMEM(shape, kind)

    one = dma(())
    scratch = [pltpu.VMEM(a.shape, a.dtype) for a in args] + [
        vmem(BF, 32, 4, 16, 256),
        vmem(BF, 32, 4, 16, 256),
        vmem(BF, 8, 256, 256),
        vmem(BF, 8, 256, 256),
        vmem(BF, 80, 128),
        vmem(BF, 16, 80, 128),
        vmem(BF, 4, 512, 256),
        vmem(BF, 4, 256, 512),
        vmem(BF, 4, 512, 256),
        vmem(BF, 4, 256, 128),
        vmem(BF, 4, 256, 128),
        vmem(BF, 4, 4, 64, 128),
        vmem(BF, 16, 64, 128),
        vmem(BF, 2, 64, 128),
        vmem(BF, 16, 64, 256),
        vmem(BF, 4, 256, 256),
        vmem(BF, 4, 256, 256),
        vmem(BF, 4, 4, 64, 256),
        vmem(BF, 16, 64, 256),
        vmem(BF, 4, 2, 256, 256),
        vmem(BF, 4, 512, 256),
        vmem(BF, 16, 64, 256),
        vmem(BF, 2, 5, 64, 256),
        vmem(BF, 2, 5, 64, 256),
        vmem(BF, 2, 64, 256),
        dma((7,)), one, one, one, one, one, dma((7,)),
        one, dma((4,)), one, one, one, one, one, dma((7,)),
        one, dma((4,)), one, one, one, one, one, dma((4,)),
        one, dma((4,)), one, dma((2, 2)), dma((2,)),
    ]
    for width, first in ((256, (2, 16, 8, 256)), (128, (2, 8, 2, 8, 128))):
        scratch += [
            vmem(F32, *first),
            vmem(F32, 16, 8, width),
            vmem(F32, 16, 8, width),
            vmem(F32, 16, 8, width),
            vmem(BF, 16, 16, 128) if width == 256 else vmem(F32, 16, 8, width),
            vmem(F32, 2, 16, 8, width),
        ] + [one] * 10
    out, gr1, gr2 = pl.pallas_call(
        kernel,
        out_shape=(
            jax.ShapeDtypeStruct((256, 256), BF),
            jax.ShapeDtypeStruct((2, 8, 8, 256), F32),
            jax.ShapeDtypeStruct((256, 256), F32),
        ),
        in_specs=[hbm] * 7,
        out_specs=(vm, vm, vm),
        scratch_shapes=scratch,
        compiler_params=pltpu.CompilerParams(
            collective_id=0, has_side_effects=True, vmem_limit_bytes=56 * 1024 * 1024
        ),
    )(*args)
    return out, gr1.reshape(128, 256), gr2


def solution(mesh):
    in_specs = (
        P("rows", None),
        P("rows", "rep"),
        P("rows", None, "rep"),
        P("rows", None),
        P(),
        P(),
        P("rows", None),
    )
    out_specs = (P("rows", None), P(), P())
    return jax.shard_map(local, mesh=mesh, in_specs=in_specs, out_specs=out_specs, check_vma=False)
```

```python
import jax
import jax.numpy as jnp
from jax import lax
from jax.experimental import pallas as pl
from jax.experimental.pallas import tpu as pltpu
from jax.sharding import PartitionSpec as P

MESH = pl.DeviceIdType.MESH
BF = jnp.bfloat16
F32 = jnp.float32


def dot(a, b, ca=1, cb=0):
    return lax.dot_general(a, b, (((ca,), (cb,)), ((), ())), preferred_element_type=F32)


def silu_slope(values):
    sigma = jax.nn.sigmoid(values)
    return sigma * (1.0 + values * (1.0 - sigma))


def iota(shape, dim):
    return lax.broadcasted_iota(jnp.int32, shape, dim)


def one_hot(hit):
    return jnp.where(hit, 1.0, 0.0).astype(BF)


def body(
    pending,
    feats_h, idxt_h, cnt_h, w_h, w1_h, w2_h, cot_h,
    out, gr1, gr2,
    feats, idxt, cnt, w, w1, w2, cot,
    wtb, wr, wb, wf, stage, g1, oh, oht, pk, own, rc, ab, rp, sw, g2,
    bk, tt, pb, fr, nr, cb,
    in_s, sw_s, sw_r, wx_s, wx_r, z1_s, z1_r, c1_s, c1_r, p1_s, p1_r, sx_s, sx_r, z2_s, z2_r,
    c2_s, c2_r, p2_s, p2_r, ox_s, ox_r, bp_s, bp_r, bc_s, bc_r, fr_s, fr_r, nr_r,
    *sums,
):
    r = lax.axis_index("rows")
    x = lax.axis_index("rep")
    core = lax.rem(r, 2)
    z = lax.rem(lax.div(r, 2), 16)
    y = lax.div(r, 32)
    za = lax.div(z, 4)
    zb = lax.rem(z, 4)
    q = y * 4 + x
    other = 1 - core

    def rid(yy, zz, cc):
        return (yy * 16 + zz) * 2 + cc

    def peer(m):
        pq = lax.rem(q + m, 16)
        py, px = lax.div(pq, 4), lax.rem(pq, 4)
        return py, px, rid(py, z, core)

    def zat(m):
        return lax.rem(z + m + 16, 16)

    def zpeer(m):
        return rid(y, zat(m), core)

    def copy(src, dst, ssem, rsem, rows, rep):
        return pltpu.make_async_remote_copy(
            src_ref=src, dst_ref=dst, send_sem=ssem, recv_sem=rsem,
            device_id={"rows": rows, "rep": rep}, device_id_type=MESH,
        )

    def send(src, dst, ssem, rsem, rows, rep):
        c = copy(src, dst, ssem, rsem, rows, rep)
        c.start()
        return c

    def sent(ref, sem):
        pending.append(copy(ref, ref, sem, sem, rid(y, z, other), x).wait_send)

    def received(ref, sem):
        copy(ref, ref, sem, sem, rid(y, z, other), x).wait_recv()

    def to_core(src, dst, ssem, rsem):
        return send(src, dst, ssem, rsem, rid(y, z, other), x)

    barrier = pltpu.get_barrier_semaphore()

    def greet(rows, rep):
        pl.semaphore_signal(barrier, inc=1, device_id={"rows": rows, "rep": rep}, device_id_type=MESH)

    alone = x == zb
    swap_r, swap_x = rid(y, za * 4 + x, core), zb
    for m in (1, 2, 3, 4, 12, 13, 14, 15):
        greet(zpeer(m), x)
    for m in range(1, 16):
        py, px, pr = peer(m)
        greet(pr, px)
        greet(rid(py, z, other), px)
    greet(rid(y, z, other), x)

    @pl.when(jnp.logical_not(alone))
    def _():
        greet(swap_r, swap_x)

    ins = []
    for n, (a, b) in enumerate(
        [(feats_h, feats), (idxt_h, idxt), (cnt_h, cnt), (w_h, w), (w1_h, w1), (w2_h, w2), (cot_h, cot)]
    ):
        c = pltpu.make_async_copy(a, b, in_s.at[n])
        c.start()
        ins.append(c)

    mine = pl.ds(pl.multiple_of(x * 64, 64), 64)
    ins[0].wait()
    ins[1].wait()
    stage[0:64, :] = feats[mine, :]
    stage[64:80, :] = idxt[...].astype(F32).astype(BF)

    ins[2].wait()
    ins[3].wait()
    row = iota((512, 1), 0)
    plane, rest = row >> 4, row & 15
    source = ((rest >> 2) << 7) + ((plane >> 3) << 5) + ((rest & 3) << 3) + (plane & 7)
    order = one_hot(source == iota((512, 512), 1))
    for sq in range(4):
        alive = [one_hot(cnt[...] > x * 16 + sq * 4 + s4) for s4 in range(4)]
        live = w[:, sq * 512:(sq + 1) * 512] * jnp.concatenate(alive, axis=1)
        wtb[:, sq] = dot(order, live, 1, 1).astype(BF).reshape(32, 16, 256)

    pl.semaphore_wait(barrier, 40 - alone.astype(jnp.int32))

    def swap(src, dst, ssem, rsem):
        c = copy(src, dst, ssem, rsem, swap_r, swap_x)

        @pl.when(alone)
        def _():
            dst[...] = src[...]

        @pl.when(jnp.logical_not(alone))
        def _():
            c.start()

        def finish():
            @pl.when(jnp.logical_not(alone))
            def _():
                c.wait_recv()

        def sent():
            @pl.when(jnp.logical_not(alone))
            def _():
                c.wait_send()

        pending.append(sent)
        return finish

    swap_done = swap(stage, g1.at[za * 4 + x], sw_s, sw_r)

    me8 = y * 2 + core
    for off in (2, 1, 3, 0):
        for mx in (2, 1, 3, 0):
            py, px = lax.rem(y + off, 4), lax.rem(x + mx, 4)
            for n, h in enumerate((core, other)):
                if off + mx + n:
                    send(wtb.at[(py * 4 + px) * 2 + h], wr.at[me8 * 4 + x], wx_s, wx_r.at[off], rid(py, z, h), px)
    sent(wtb.at[pl.ds(0, 31)], wx_s)
    wr[me8 * 4 + x] = wtb[q * 2 + core]
    yield "prep"

    row, col = iota((256, 1), 0), iota((256, 256), 1)
    regroup = one_hot(((row & 63) << 2) + (row >> 6) == col)
    eye = one_hot(row == col)
    swap_done()
    yield "swap1"

    def gather_z(g, rows, cut, ssem, rsem):
        full, parts = pl.ds(0, rows), (pl.ds(0, cut), pl.ds(cut, rows - cut))
        relay = {}

        def move(dist, via):
            for d in range(2):
                sign = 1 if d == 0 else -1
                if via:
                    relay[d, via].wait_recv()
                for there in (6, 8, 5) if dist == 6 else (dist,):
                    piece = g.at[zat(-sign * via), parts[d] if there == 8 else full]
                    sem = rsem.at[d * 3 + there // 2 - 1] if there in (2, 4, 6) else rsem.at[6]
                    relay[d, there] = send(piece, piece, ssem, sem, zpeer(sign * (there - via)), x)

        for dist in (4, 2, 1):
            move(dist, 0)
        yield
        move(3, 2)
        move(6, 4)
        yield
        move(7, 6)
        sent(g.at[pl.ds(0, 15)], ssem)
        yield
        received(g.at[pl.ds(0, 9)], rsem.at[6])
        yield

    for _ in gather_z(g1, 80, 48, z1_s, z1_r):
        pass
    yield "gz1"

    ids = g1[:, 64:80, :].reshape(256, 128)
    lane = iota((256, 256), 1).astype(F32)
    for k in range(8):
        at = ((k // 2) * 16 + z) * 2 + k % 2
        rows = dot(ids, one_hot(iota((128, 256), 0) == at))
        oh[:, k * 64:(k + 1) * 64, :] = one_hot(rows == lane).reshape(4, 64, 256)
    for a in range(4):
        pk[0, a] = dot(oh[a], g1[4 * a:4 * a + 4, 0:64, :].reshape(256, 128)).astype(BF)

    yield "picks1"


    def weights(k):
        wb[k] = dot(regroup, wr[pl.ds(k * 4, 4)].reshape(256, 256)).astype(BF)
        wf[k] = dot(eye, wb[k], 1, 1).astype(BF)

    near = (2, 3, 1, 0)

    def reduce_send(t, prepare, csem_s, csem_r, psem_s, psem_r):
        def partial(k):
            if prepare:
                prepare(k)
            return dot(wf[k], pk[t, :, pl.ds(pl.multiple_of(k * 64, 64), 64), :].reshape(256, 128))

        cs, mine_j = [], []

        def first(off):
            if prepare is weights:
                received(wr.at[pl.ds(0, 8 if off else 7)], wx_r.at[(4 - off) % 4])
            j = lax.rem(y + off, 4)
            own[t, j] = partial(j * 2 + other).astype(BF)
            cs.append(to_core(own.at[t, j], rc.at[t, j], csem_s, csem_r.at[off]))
            mine_j.append(partial(j * 2 + core))

        def second(n):
            off = near[n]
            j = lax.rem(y + off, 4)
            cs[n].wait_recv()
            ab[t, j] = (mine_j[n] + rc[t, j].astype(F32)).astype(BF).reshape(4, 64, 128)
            for mx in (2, 1, 3, 0):
                if off + mx:
                    px = lax.rem(x + mx, 4)
                    send(ab.at[t, j, px], rp.at[t, off * 4 + mx], psem_s, psem_r, rid(j, z, core), px)

        first(near[0])
        for n in range(1, 4):
            first(near[n])
            second(n - 1)
        second(3)
        sent(own.at[t], csem_s)
        sent(rp.at[t, pl.ds(1, 15)], psem_s)

    def reduce_add(t, psem_r):
        received(rp.at[t, pl.ds(1, 15)], psem_r)
        res = ab[t, y, x].astype(F32)
        for m in range(1, 16):
            res = res + rp[t, m].astype(F32)
        return res.astype(BF)

    reduce_send(0, weights, c1_s, c1_r, p1_s, p1_r)
    sw[0] = reduce_add(0, p1_r)
    yield "red1"
    swap(sw.at[0], sw.at[1], sx_s, sx_r)()
    yield "swap2"
    for n in (4, 5, 6):
        ins[n].wait()
    agg1 = sw[1]
    z_one = dot(agg1, w1[...])
    hidden = (z_one * jax.nn.sigmoid(z_one)).astype(BF)
    halves = []
    for t in range(2):
        g2[t, z] = hidden[:, t * 128:(t + 1) * 128]
        halves.append(gather_z(g2.at[t], 64, 32, z2_s.at[t], z2_r.at[t]))
        next(halves[t])
    for a in range(4):
        oht[a] = dot(eye, oh[a], 1, 1).astype(BF)
    for stage in range(2):
        for t in range(2):
            next(halves[t])
    for t in range(2):
        next(halves[t])
        for a in range(4):
            pk[1 + t, a] = dot(oh[a], g2[t, 4 * a:4 * a + 4].reshape(256, 128)).astype(BF)
        reduce_send(1 + t, None, c2_s.at[t], c2_r.at[t], p2_s.at[t], p2_r.at[t])
    agg2 = jnp.concatenate([reduce_add(1 + t, p2_r.at[t]) for t in range(2)], axis=1)
    yield "red2"

    z_two = dot(agg2, w2[...])
    dz2 = (cot[mine, :].astype(F32) * silu_slope(z_two)).astype(BF)
    bk[y, core, mine, :] = dot(dz2, w2[...], 1, 1).astype(BF)
    for off in (2, 1, 3, 0):
        for mx in (2, 1, 3, 0):
            m = off * 4 + mx
            if m:
                py, px = lax.rem(y + off, 4), lax.rem(x + mx, 4)
                send(bk.at[y, core, mine], bk.at[y, core, mine], bp_s, bp_r.at[off], rid(py, z, core), px)
    sent(pb.at[pl.ds(0, 15)], bp_s)
    out[mine, :] = (z_two * jax.nn.sigmoid(z_two)).astype(BF)
    for m in range(1, 4):
        send(out.at[mine], out.at[mine], ox_s, ox_r, r, lax.rem(x + m, 4))
    sent(out.at[pl.ds(0, 192)], ox_s)

    def reduce_all(ga, gc, gs, gp, gz, gt, c_s, c_r, p_s, p_r, z_s, z_r, t_s, t_r, d_s, d_r):
        c = to_core(ga.at[other], gc, c_s, c_r)
        sent(gc, c_s)
        yield
        c.wait_recv()
        gs[...] = ga[core] + gc[...]
        for m in range(1, 16):
            py, px, pr = peer(m)
            send(gs.at[py * 4 + px], gp.at[m], p_s, p_r, pr, px)
        sent(gp.at[pl.ds(1, 15)], p_s)
        yield
        received(gp.at[pl.ds(1, 15)], p_r)
        total = gs[q]
        for m in range(1, 16):
            total = total + gp[m]
        wide = gz.dtype == BF
        gz[0] = jnp.concatenate([total[:, :128], total[:, 128:]], axis=0).astype(BF) if wide else total
        for m in (8, 7, 9, 6, 10, 5, 11, 4, 12, 3, 13, 2, 14, 1, 15):
            send(gz.at[0], gz.at[m], z_s, z_r, zpeer(m), x)
        sent(gz.at[pl.ds(1, 15)], z_s)
        yield
        received(gz.at[pl.ds(1, 15)], z_r)
        total = gz[z].astype(F32)
        for k in range(1, 16):
            total = total + gz[lax.rem(z - k + 16, 16)].astype(F32)
        gt[core, q] = jnp.concatenate([total[:8], total[8:]], axis=1) if wide else total
        for m in range(1, 16):
            py, px, pr = peer(m)
            send(gt.at[core, q], gt.at[core, q], t_s, t_r, pr, px)
        sent(gt.at[core, pl.ds(0, 15)], t_s)
        yield
        received(gt.at[core, pl.ds(0, 15)], t_r)
        c = to_core(gt.at[core], gt.at[core], d_s, d_r)
        sent(gt.at[core], d_s)
        yield
        c.wait_recv()
        yield

    half = len(sums) // 2
    ga2, ga1 = sums[0], sums[half]
    reduce2, reduce1 = reduce_all(*sums[:half]), reduce_all(*sums[half:])
    ga2[...] = dot(agg2, dz2, 0, 0).reshape(2, 16, 8, 256)
    next(reduce2)


    def slot_terms(k):
        got = dot(wb[k], bk[lax.div(k, 2), lax.rem(k, 2)]).astype(BF)
        tt[:, pl.ds(pl.multiple_of(k * 64, 64), 64), :] = got.reshape(4, 64, 256)

    next(reduce2)
    cc = {}
    for off in (0, 1, 3, 2):
        j = lax.rem(y - off + 4, 4)
        received(bk.at[j, core] if off else bk.at[j, core, pl.ds(0, 192)], bp_r.at[off])
        cc[off] = to_core(bk.at[j, core], bk.at[j, core], bc_s, bc_r.at[off])
        slot_terms(j * 2 + core)
    sent(bk.at[:, 0], bc_s)
    next(reduce2)
    for off in (0, 1, 3, 2):
        cc[off].wait_recv()
        slot_terms(lax.rem(y - off + 4, 4) * 2 + other)
    yield "bwait"
    for a in range(4):
        pb[4 * a:4 * a + 4] = dot(oht[a], tt[a]).astype(BF).reshape(4, 64, 256)

    full, parts = pl.ds(0, 64), (pl.ds(0, 32), pl.ds(32, 32))
    fars, nears = {}, {}
    for m in (4, 3, 2, 1):
        for d in range(2):
            sign = 1 if d == 0 else -1
            part = parts[d] if m == 4 else full
            fars[d, m] = send(pb.at[zat(sign * (4 + m)), part], fr.at[d, m, part], fr_s, fr_r.at[d, 1 if m == 4 else 0],
                              zpeer(sign * m), x)
    for m in (3, 2, 1):
        for d in range(2):
            sign = 1 if d == 0 else -1
            nears[d, m] = send(pb.at[zat(sign * m)], nr.at[d, m], fr_s, nr_r.at[d], zpeer(sign * m), x)
    for d in range(2):
        sign = 1 if d == 0 else -1
        acc = pb[zat(sign * 4)].astype(F32)
        received(fr.at[d, pl.ds(1, 3)], fr_r.at[d, 0])
        for m in (1, 2, 3):
            acc = acc + fr[d, m].astype(F32)
        fars[d, 4].wait_recv()
        cb[d] = acc.astype(BF)
        lo = 0 if d == 0 else 32
        cb[d, lo:lo + 32, :] = (acc[lo:lo + 32] + fr[d, 4, lo:lo + 32, :].astype(F32)).astype(BF)
        nears[d, 4] = send(cb.at[d], nr.at[d, 4], fr_s, nr_r.at[d], zpeer(sign * 4), x)
    next(reduce2)
    dh = pb[z].astype(F32)
    sent(pb.at[pl.ds(0, 15)], fr_s)
    for d in range(2):
        received(nr.at[d, pl.ds(1, 4)], nr_r.at[d])
        for m in (1, 2, 3, 4):
            dh = dh + nr[d, m].astype(F32)
    yield "rsz"
    dz1 = (dh * silu_slope(z_one)).astype(BF)
    grad1 = dot(agg1, dz1, 0, 0).reshape(2, 8, 8, 256)
    for b in range(2):
        ga1[:, :, b] = grad1[:, :, :, b * 128:(b + 1) * 128]
    ga1 = ga1.reshape(2, 16, 8, 128)
    reduce1 = reduce_all(ga1, *sums[half + 1:])
    next(reduce1)
    next(reduce2)
    yield "arc"
    next(reduce1)
    next(reduce2)
    gr2[...] = sums[5][...].reshape(256, 256)
    yield "arp"
    next(reduce1)
    yield "arz"
    next(reduce1)
    yield "art"
    next(reduce1)
    next(reduce1)
    gt1 = sums[half + 5]
    for b in range(2):
        for k in range(8):
            gr1[:, k, :, b * 128:(b + 1) * 128] = gt1[:, 2 * k + b]
    received(out.at[pl.ds(0, 192)], ox_r)


def kernel(*refs):
    pending = []
    for _ in body(pending, *refs):
        pass
    for wait in pending:
        wait()


def local(feats, edge_w, send_rows, counts, w_one, w_two, cotangent):
    idxt = jnp.transpose(send_rows[0])
    vm = pl.BlockSpec(memory_space=pltpu.VMEM)
    hbm = pl.BlockSpec(memory_space=pl.ANY)
    args = (feats, idxt, counts, edge_w, w_one, w_two, cotangent)
    dma = pltpu.SemaphoreType.DMA

    def vmem(kind, *shape):
        return pltpu.VMEM(shape, kind)

    one = dma(())
    scratch = [pltpu.VMEM(a.shape, a.dtype) for a in args] + [
        vmem(BF, 32, 4, 16, 256),
        vmem(BF, 32, 4, 16, 256),
        vmem(BF, 8, 256, 256),
        vmem(BF, 8, 256, 256),
        vmem(BF, 80, 128),
        vmem(BF, 16, 80, 128),
        vmem(BF, 4, 512, 256),
        vmem(BF, 4, 256, 512),
        vmem(BF, 3, 4, 512, 128),
        vmem(BF, 3, 4, 256, 128),
        vmem(BF, 3, 4, 256, 128),
        vmem(BF, 3, 4, 4, 64, 128),
        vmem(BF, 3, 16, 64, 128),
        vmem(BF, 2, 64, 128),
        vmem(BF, 2, 16, 64, 128),
        vmem(BF, 4, 2, 256, 256),
        vmem(BF, 4, 512, 256),
        vmem(BF, 16, 64, 256),
        vmem(BF, 2, 5, 64, 256),
        vmem(BF, 2, 5, 64, 256),
        vmem(BF, 2, 64, 256),
        dma((7,)), one, one, one, dma((4,)), one, dma((7,)),
        one, dma((4,)), one, one, one, one, dma((2,)), dma((2, 7)),
        dma((2,)), dma((2, 4)), dma((2,)), dma((2,)), one, one, one, dma((4,)),
        one, dma((4,)), one, dma((2, 2)), dma((2,)),
    ]
    for width, first in ((256, (2, 16, 8, 256)), (128, (2, 8, 2, 8, 128))):
        scratch += [
            vmem(F32, *first),
            vmem(F32, 16, 8, width),
            vmem(F32, 16, 8, width),
            vmem(F32, 16, 8, width),
            vmem(BF, 16, 16, 128) if width == 256 else vmem(F32, 16, 8, width),
            vmem(F32, 2, 16, 8, width),
        ] + [one] * 10
    out, gr1, gr2 = pl.pallas_call(
        kernel,
        out_shape=(
            jax.ShapeDtypeStruct((256, 256), BF),
            jax.ShapeDtypeStruct((2, 8, 8, 256), F32),
            jax.ShapeDtypeStruct((256, 256), F32),
        ),
        in_specs=[hbm] * 7,
        out_specs=(vm, vm, vm),
        scratch_shapes=scratch,
        compiler_params=pltpu.CompilerParams(
            collective_id=0, has_side_effects=True, vmem_limit_bytes=56 * 1024 * 1024
        ),
    )(*args)
    return out, gr1.reshape(128, 256), gr2


def solution(mesh):
    in_specs = (
        P("rows", None),
        P("rows", "rep"),
        P("rows", None, "rep"),
        P("rows", None),
        P(),
        P(),
        P("rows", None),
    )
    out_specs = (P("rows", None), P(), P())
    return jax.shard_map(local, mesh=mesh, in_specs=in_specs, out_specs=out_specs, check_vma=False)
```

```python
import jax
import jax.numpy as jnp
from jax import lax
from jax.experimental import pallas as pl
from jax.experimental.pallas import tpu as pltpu
from jax.sharding import PartitionSpec as P

MESH = pl.DeviceIdType.MESH
BF = jnp.bfloat16
F32 = jnp.float32


def dot(a, b, ca=1, cb=0):
    return lax.dot_general(a, b, (((ca,), (cb,)), ((), ())), preferred_element_type=F32)


def silu_slope(values):
    sigma = jax.nn.sigmoid(values)
    return sigma * (1.0 + values * (1.0 - sigma))


def iota(shape, dim):
    return lax.broadcasted_iota(jnp.int32, shape, dim)


def one_hot(hit):
    return jnp.where(hit, 1.0, 0.0).astype(BF)


def body(
    pending,
    feats_h, idxt_h, cnt_h, w_h, w1_h, w2_h, cot_h,
    out, gr1, gr2,
    feats, idxt, cnt, w, w1, w2, cot,
    wtb, wr, wb, wf, stage, g1, oh, oht, pk, own, rc, ab, rp, sw, g2,
    bk, tt, pb, fr, nr, cb,
    in_s, sw_s, sw_r, wx_s, wx_r, z1_s, z1_r, c1_s, c1_r, p1_s, p1_r, sx_s, sx_r, z2_s, z2_r,
    c2_s, c2_r, p2_s, p2_r, ox_s, ox_r, bp_s, bp_r, bc_s, bc_r, fr_s, fr_r, nr_r, n3_r,
    *sums,
):
    r = lax.axis_index("rows")
    x = lax.axis_index("rep")
    core = lax.rem(r, 2)
    z = lax.rem(lax.div(r, 2), 16)
    y = lax.div(r, 32)
    za = lax.div(z, 4)
    zb = lax.rem(z, 4)
    q = y * 4 + x
    other = 1 - core

    def rid(yy, zz, cc):
        return (yy * 16 + zz) * 2 + cc

    def peer(m):
        pq = lax.rem(q + m, 16)
        py, px = lax.div(pq, 4), lax.rem(pq, 4)
        return py, px, rid(py, z, core)

    def zat(m):
        return lax.rem(z + m + 16, 16)

    def zpeer(m):
        return rid(y, zat(m), core)

    def copy(src, dst, ssem, rsem, rows, rep):
        return pltpu.make_async_remote_copy(
            src_ref=src, dst_ref=dst, send_sem=ssem, recv_sem=rsem,
            device_id={"rows": rows, "rep": rep}, device_id_type=MESH,
        )

    def send(src, dst, ssem, rsem, rows, rep):
        c = copy(src, dst, ssem, rsem, rows, rep)
        c.start()
        return c

    def sent(ref, sem):
        pending.append(copy(ref, ref, sem, sem, rid(y, z, other), x).wait_send)

    def received(ref, sem):
        copy(ref, ref, sem, sem, rid(y, z, other), x).wait_recv()

    def to_core(src, dst, ssem, rsem):
        return send(src, dst, ssem, rsem, rid(y, z, other), x)

    barrier = pltpu.get_barrier_semaphore()

    def greet(rows, rep):
        pl.semaphore_signal(barrier, inc=1, device_id={"rows": rows, "rep": rep}, device_id_type=MESH)

    alone = x == zb
    swap_r, swap_x = rid(y, za * 4 + x, core), zb
    for m in (1, 2, 3, 4, 12, 13, 14, 15):
        greet(zpeer(m), x)
    for m in range(1, 16):
        py, px, pr = peer(m)
        greet(pr, px)
        greet(rid(py, z, other), px)
    greet(rid(y, z, other), x)

    @pl.when(jnp.logical_not(alone))
    def _():
        greet(swap_r, swap_x)

    ins = []
    for n, (a, b) in enumerate(
        [(feats_h, feats), (idxt_h, idxt), (cnt_h, cnt), (w_h, w), (w1_h, w1), (w2_h, w2), (cot_h, cot)]
    ):
        c = pltpu.make_async_copy(a, b, in_s.at[n])
        c.start()
        ins.append(c)

    mine = pl.ds(pl.multiple_of(x * 64, 64), 64)
    ins[0].wait()
    ins[1].wait()
    stage[0:64, :] = feats[mine, :]
    stage[64:80, :] = idxt[...].astype(F32).astype(BF)

    ins[2].wait()
    ins[3].wait()
    row = iota((512, 1), 0)
    plane, rest = row >> 4, row & 15
    source = ((rest >> 2) << 7) + ((plane >> 3) << 5) + ((rest & 3) << 3) + (plane & 7)
    order = one_hot(source == iota((512, 512), 1))
    for sq in range(4):
        alive = [one_hot(cnt[...] > x * 16 + sq * 4 + s4) for s4 in range(4)]
        live = w[:, sq * 512:(sq + 1) * 512] * jnp.concatenate(alive, axis=1)
        wtb[:, sq] = dot(order, live, 1, 1).astype(BF).reshape(32, 16, 256)

    pl.semaphore_wait(barrier, 40 - alone.astype(jnp.int32))

    def swap(src, dst, ssem, rsem):
        c = copy(src, dst, ssem, rsem, swap_r, swap_x)

        @pl.when(alone)
        def _():
            dst[...] = src[...]

        @pl.when(jnp.logical_not(alone))
        def _():
            c.start()

        def finish():
            @pl.when(jnp.logical_not(alone))
            def _():
                c.wait_recv()

        def sent():
            @pl.when(jnp.logical_not(alone))
            def _():
                c.wait_send()

        pending.append(sent)
        return finish

    swap_done = swap(stage, g1.at[za * 4 + x], sw_s, sw_r)

    me8 = y * 2 + core
    for off in (2, 1, 3, 0):
        for mx in (2, 1, 3, 0):
            py, px = lax.rem(y + off, 4), lax.rem(x + mx, 4)
            for n, h in enumerate((core, other)):
                if off + mx + n:
                    send(wtb.at[(py * 4 + px) * 2 + h], wr.at[me8 * 4 + x], wx_s, wx_r.at[off], rid(py, z, h), px)
    sent(wtb.at[pl.ds(0, 31)], wx_s)
    wr[me8 * 4 + x] = wtb[q * 2 + core]
    yield "prep"

    row, col = iota((256, 1), 0), iota((256, 256), 1)
    regroup = one_hot(((row & 63) << 2) + (row >> 6) == col)
    eye = one_hot(row == col)
    swap_done()
    yield "swap1"

    def gather_z(g, rows, cut, ssem, rsem):
        full, parts = pl.ds(0, rows), (pl.ds(0, cut), pl.ds(cut, rows - cut))
        relay = {}

        def move(dist, via):
            for d in range(2):
                sign = 1 if d == 0 else -1
                if via:
                    relay[d, via].wait_recv()
                for there in (6, 8, 5) if dist == 6 else (dist,):
                    piece = g.at[zat(-sign * via), parts[d] if there == 8 else full]
                    sem = rsem.at[d * 3 + there // 2 - 1] if there in (2, 4, 6) else rsem.at[6]
                    relay[d, there] = send(piece, piece, ssem, sem, zpeer(sign * (there - via)), x)

        for dist in (4, 2, 1):
            move(dist, 0)
        yield
        move(3, 2)
        move(6, 4)
        yield
        move(7, 6)
        sent(g.at[pl.ds(0, 15)], ssem)
        yield
        received(g.at[pl.ds(0, 9)], rsem.at[6])
        yield

    gather1 = gather_z(g1, 80, 48, z1_s, z1_r)
    for _ in range(3):
        next(gather1)

    def weights(k):
        wb[k] = dot(regroup, wr[pl.ds(k * 4, 4)].reshape(256, 256)).astype(BF)
        wf[k] = dot(eye, wb[k], 1, 1).astype(BF)

    for off in (2, 1, 3, 0):
        received(wr.at[pl.ds(0, 8 if off else 7)], wx_r.at[off])
        for h in range(2):
            weights(lax.rem(y - off + 4, 4) * 2 + h)
    next(gather1)
    yield "gz1"

    ids = g1[:, 64:80, :].reshape(256, 128)
    lane = iota((256, 256), 1).astype(F32)
    for k in range(8):
        at = ((k // 2) * 16 + z) * 2 + k % 2
        rows = dot(ids, one_hot(iota((128, 256), 0) == at))
        oh[:, k * 64:(k + 1) * 64, :] = one_hot(rows == lane).reshape(4, 64, 256)
    for a in range(4):
        pk[0, a] = dot(oh[a], g1[4 * a:4 * a + 4, 0:64, :].reshape(256, 128)).astype(BF)

    yield "picks1"


    near = (2, 3, 1, 0)

    def reduce_send(t, csem_s, csem_r, psem_s, psem_r):
        def partial(k):
            return dot(wf[k], pk[t, :, pl.ds(pl.multiple_of(k * 64, 64), 64), :].reshape(256, 128))

        cs, mine_j = [], []

        def first(off):
            j = lax.rem(y + off, 4)
            own[t, j] = partial(j * 2 + other).astype(BF)
            cs.append(to_core(own.at[t, j], rc.at[t, j], csem_s, csem_r.at[off]))
            mine_j.append(partial(j * 2 + core))

        def second(n):
            off = near[n]
            j = lax.rem(y + off, 4)
            cs[n].wait_recv()
            ab[t, j] = (mine_j[n] + rc[t, j].astype(F32)).astype(BF).reshape(4, 64, 128)
            for mx in (2, 1, 3, 0):
                if off + mx:
                    px = lax.rem(x + mx, 4)
                    send(ab.at[t, j, px], rp.at[t, off * 4 + mx], psem_s, psem_r, rid(j, z, core), px)

        first(near[0])
        for n in range(1, 4):
            first(near[n])
            second(n - 1)
        second(3)
        sent(own.at[t], csem_s)
        sent(rp.at[t, pl.ds(1, 15)], psem_s)

    def reduce_add(t, psem_r):
        received(rp.at[t, pl.ds(1, 15)], psem_r)
        res = ab[t, y, x].astype(F32)
        for m in range(1, 16):
            res = res + rp[t, m].astype(F32)
        return res.astype(BF)

    reduce_send(0, c1_s, c1_r, p1_s, p1_r)
    sw[0] = reduce_add(0, p1_r)
    yield "red1"
    swap(sw.at[0], sw.at[1], sx_s, sx_r)()
    yield "swap2"
    for n in (4, 5, 6):
        ins[n].wait()
    agg1 = sw[1]
    z_one = dot(agg1, w1[...])
    hidden = (z_one * jax.nn.sigmoid(z_one)).astype(BF)
    halves = []
    for t in range(2):
        g2[t, z] = hidden[:, t * 128:(t + 1) * 128]
        halves.append(gather_z(g2.at[t], 64, 32, z2_s.at[t], z2_r.at[t]))
        next(halves[t])
    for a in range(4):
        oht[a] = dot(eye, oh[a], 1, 1).astype(BF)
    for stage in range(2):
        for t in range(2):
            next(halves[t])
    for t in range(2):
        next(halves[t])
        for a in range(4):
            pk[1 + t, a] = dot(oh[a], g2[t, 4 * a:4 * a + 4].reshape(256, 128)).astype(BF)
        reduce_send(1 + t, c2_s.at[t], c2_r.at[t], p2_s.at[t], p2_r.at[t])
    agg2 = jnp.concatenate([reduce_add(1 + t, p2_r.at[t]) for t in range(2)], axis=1)
    yield "red2"

    z_two = dot(agg2, w2[...])
    dz2 = (cot[mine, :].astype(F32) * silu_slope(z_two)).astype(BF)
    back = dot(dz2, w2[...], 1, 1).astype(BF)
    for t in range(2):
        bk[t, y, core, mine, :] = back[:, t * 128:(t + 1) * 128]
        piece = bk.at[t, y, core, mine]
        for off in (2, 1, 3, 0):
            for mx in (2, 1, 3, 0):
                if off + mx:
                    py, px = lax.rem(y + off, 4), lax.rem(x + mx, 4)
                    send(piece, piece, bp_s.at[t], bp_r.at[t, off], rid(py, z, core), px)
        sent(pb.at[t, pl.ds(0, 15)], bp_s.at[t])
    out[mine, :] = (z_two * jax.nn.sigmoid(z_two)).astype(BF)
    for m in range(1, 4):
        send(out.at[mine], out.at[mine], ox_s, ox_r, r, lax.rem(x + m, 4))
    sent(out.at[pl.ds(0, 192)], ox_s)

    def reduce_all(ga, gc, gs, gp, gz, gt, c_s, c_r, p_s, p_r, z_s, z_r, t_s, t_r, d_s, d_r):
        c = to_core(ga.at[other], gc, c_s, c_r)
        sent(gc, c_s)
        yield
        c.wait_recv()
        gs[...] = ga[core] + gc[...]
        for m in range(1, 16):
            py, px, pr = peer(m)
            send(gs.at[py * 4 + px], gp.at[m], p_s, p_r, pr, px)
        sent(gp.at[pl.ds(1, 15)], p_s)
        yield
        received(gp.at[pl.ds(1, 15)], p_r)
        total = gs[q]
        for m in range(1, 16):
            total = total + gp[m]
        wide = gz.dtype == BF
        gz[0] = jnp.concatenate([total[:, :128], total[:, 128:]], axis=0).astype(BF) if wide else total
        for m in (8, 7, 9, 6, 10, 5, 11, 4, 12, 3, 13, 2, 14, 1, 15):
            send(gz.at[0], gz.at[m], z_s, z_r, zpeer(m), x)
        sent(gz.at[pl.ds(1, 15)], z_s)
        yield
        received(gz.at[pl.ds(1, 15)], z_r)
        total = gz[z].astype(F32)
        for k in range(1, 16):
            total = total + gz[lax.rem(z - k + 16, 16)].astype(F32)
        gt[core, q] = jnp.concatenate([total[:8], total[8:]], axis=1) if wide else total
        for m in range(1, 16):
            py, px, pr = peer(m)
            send(gt.at[core, q], gt.at[core, q], t_s, t_r, pr, px)
        sent(gt.at[core, pl.ds(0, 15)], t_s)
        yield
        received(gt.at[core, pl.ds(0, 15)], t_r)
        c = to_core(gt.at[core], gt.at[core], d_s, d_r)
        sent(gt.at[core], d_s)
        yield
        c.wait_recv()
        yield

    half = len(sums) // 2
    ga2, ga1 = sums[0], sums[half]
    reduce2, reduce1 = reduce_all(*sums[:half]), reduce_all(*sums[half:])
    ga2[...] = dot(agg2, dz2, 0, 0).reshape(2, 16, 8, 256)
    next(reduce2)

    def slot_terms(t, k):
        got = dot(wb[k], bk[t, lax.div(k, 2), lax.rem(k, 2)]).astype(BF)
        tt[t, :, pl.ds(pl.multiple_of(k * 64, 64), 64), :] = got.reshape(4, 64, 128)

    next(reduce2)
    cc = {}

    def own_blocks(t):
        for off in (0, 1, 3, 2):
            j = lax.rem(y - off + 4, 4)
            block = bk.at[t, j, core]
            received(block if off else bk.at[t, j, core, pl.ds(0, 192)], bp_r.at[t, off])
            cc[t, off] = to_core(block, block, bc_s.at[t], bc_r.at[t, off])
            slot_terms(t, j * 2 + core)
        sent(bk.at[t, :, 0], bc_s.at[t])

    def other_blocks(t):
        for off in (0, 1, 3, 2):
            cc[t, off].wait_recv()
            slot_terms(t, lax.rem(y - off + 4, 4) * 2 + other)
        for a in range(4):
            pb[t, 4 * a:4 * a + 4] = dot(oht[a], tt[t, a]).astype(BF).reshape(4, 64, 128)

    full, parts = pl.ds(0, 64), (pl.ds(0, 32), pl.ds(32, 32))
    ways = ((0, 1), (1, -1))
    halfway = {}

    def scatter(t):
        for m in (4, 3, 2, 1):
            for d, sign in ways:
                part = parts[d] if m == 4 else full
                c = send(pb.at[t, zat(sign * (4 + m)), part], fr.at[t, d, m, part], fr_s.at[t],
                         fr_r.at[t, d, 1 if m == 4 else 0], zpeer(sign * m), x)
                if m == 4:
                    halfway[t, d] = c
        for d, sign in ways:
            halfway[t, d, 3] = send(pb.at[t, zat(sign * 3)], fr.at[t, d, 0], fr_s.at[t], n3_r.at[t, d], zpeer(sign), x)
        for d, sign in ways:
            send(pb.at[t, zat(sign)], nr.at[t, d, 1], fr_s.at[t], nr_r.at[t, d], zpeer(sign), x)

    def pass_near(t):
        for d, sign in ways:
            halfway[t, d, 3].wait_recv()
            cb[t, d, 1] = (pb[t, zat(sign * 2)].astype(F32) + fr[t, d, 0].astype(F32)).astype(BF)
            send(cb.at[t, d, 1], nr.at[t, d, 2], fr_s.at[t], nr_r.at[t, d], zpeer(sign * 2), x)

    def pass_on(t):
        for d, sign in ways:
            acc = pb[t, zat(sign * 4)].astype(F32)
            received(fr.at[t, d, pl.ds(1, 3)], fr_r.at[t, d, 0])
            for m in (1, 2, 3):
                acc = acc + fr[t, d, m].astype(F32)
            halfway[t, d].wait_recv()
            lo = 0 if d == 0 else 32
            cb[t, d, 0] = acc.astype(BF)
            cb[t, d, 0, lo:lo + 32, :] = (acc[lo:lo + 32] + fr[t, d, 4, lo:lo + 32, :].astype(F32)).astype(BF)
            send(cb.at[t, d, 0], nr.at[t, d, 3], fr_s.at[t], nr_r.at[t, d], zpeer(sign * 4), x)
        sent(pb.at[t, pl.ds(0, 15)], fr_s.at[t])

    def collect(t):
        dh = pb[t, z].astype(F32)
        for d in range(2):
            received(nr.at[t, d, pl.ds(1, 3)], nr_r.at[t, d])
            for m in (1, 2, 3):
                dh = dh + nr[t, d, m].astype(F32)
        return dh

    own_blocks(0)
    next(reduce2)
    other_blocks(0)
    scatter(0)
    own_blocks(1)
    other_blocks(1)
    yield "bwait"
    scatter(1)
    pass_near(0)
    slope = silu_slope(z_one)
    pass_near(1)
    pass_on(0)
    pass_on(1)
    next(reduce2)
    for t in range(2):
        dz1 = (collect(t) * slope[:, t * 128:(t + 1) * 128]).astype(BF)
        ga1[:, :, t] = dot(agg1, dz1, 0, 0).reshape(2, 8, 8, 128)
    yield "rsz"
    ga1 = ga1.reshape(2, 16, 8, 128)
    reduce1 = reduce_all(ga1, *sums[half + 1:])
    next(reduce1)
    next(reduce2)
    yield "arc"
    next(reduce1)
    next(reduce2)
    gr2[...] = sums[5][...].reshape(256, 256)
    yield "arp"
    next(reduce1)
    yield "arz"
    next(reduce1)
    yield "art"
    next(reduce1)
    next(reduce1)
    gt1 = sums[half + 5]
    for b in range(2):
        for k in range(8):
            gr1[:, k, :, b * 128:(b + 1) * 128] = gt1[:, 2 * k + b]
    received(out.at[pl.ds(0, 192)], ox_r)


def kernel(*refs):
    pending = []
    for _ in body(pending, *refs):
        pass
    for wait in pending:
        wait()


def local(feats, edge_w, send_rows, counts, w_one, w_two, cotangent):
    idxt = jnp.transpose(send_rows[0])
    vm = pl.BlockSpec(memory_space=pltpu.VMEM)
    hbm = pl.BlockSpec(memory_space=pl.ANY)
    args = (feats, idxt, counts, edge_w, w_one, w_two, cotangent)
    dma = pltpu.SemaphoreType.DMA

    def vmem(kind, *shape):
        return pltpu.VMEM(shape, kind)

    one = dma(())
    scratch = [pltpu.VMEM(a.shape, a.dtype) for a in args] + [
        vmem(BF, 32, 4, 16, 256),
        vmem(BF, 32, 4, 16, 256),
        vmem(BF, 8, 256, 256),
        vmem(BF, 8, 256, 256),
        vmem(BF, 80, 128),
        vmem(BF, 16, 80, 128),
        vmem(BF, 4, 512, 256),
        vmem(BF, 4, 256, 512),
        vmem(BF, 3, 4, 512, 128),
        vmem(BF, 3, 4, 256, 128),
        vmem(BF, 3, 4, 256, 128),
        vmem(BF, 3, 4, 4, 64, 128),
        vmem(BF, 3, 16, 64, 128),
        vmem(BF, 2, 64, 128),
        vmem(BF, 2, 16, 64, 128),
        vmem(BF, 2, 4, 2, 256, 128),
        vmem(BF, 2, 4, 512, 128),
        vmem(BF, 2, 16, 64, 128),
        vmem(BF, 2, 2, 5, 64, 128),
        vmem(BF, 2, 2, 4, 64, 128),
        vmem(BF, 2, 2, 2, 64, 128),
        dma((7,)), one, one, one, dma((4,)), one, dma((7,)),
        one, dma((4,)), one, one, one, one, dma((2,)), dma((2, 7)),
        dma((2,)), dma((2, 4)), dma((2,)), dma((2,)), one, one, dma((2,)), dma((2, 4)),
        dma((2,)), dma((2, 4)), dma((2,)), dma((2, 2, 2)), dma((2, 2)), dma((2, 2)),
    ]
    for width, first in ((256, (2, 16, 8, 256)), (128, (2, 8, 2, 8, 128))):
        scratch += [
            vmem(F32, *first),
            vmem(F32, 16, 8, width),
            vmem(F32, 16, 8, width),
            vmem(F32, 16, 8, width),
            vmem(BF, 16, 16, 128) if width == 256 else vmem(F32, 16, 8, width),
            vmem(F32, 2, 16, 8, width),
        ] + [one] * 10
    out, gr1, gr2 = pl.pallas_call(
        kernel,
        out_shape=(
            jax.ShapeDtypeStruct((256, 256), BF),
            jax.ShapeDtypeStruct((2, 8, 8, 256), F32),
            jax.ShapeDtypeStruct((256, 256), F32),
        ),
        in_specs=[hbm] * 7,
        out_specs=(vm, vm, vm),
        scratch_shapes=scratch,
        compiler_params=pltpu.CompilerParams(
            collective_id=0, has_side_effects=True, vmem_limit_bytes=56 * 1024 * 1024
        ),
    )(*args)
    return out, gr1.reshape(128, 256), gr2


def solution(mesh):
    in_specs = (
        P("rows", None),
        P("rows", "rep"),
        P("rows", None, "rep"),
        P("rows", None),
        P(),
        P(),
        P("rows", None),
    )
    out_specs = (P("rows", None), P(), P())
    return jax.shard_map(local, mesh=mesh, in_specs=in_specs, out_specs=out_specs, check_vma=False)
```

```python
import jax
import jax.numpy as jnp
from jax import lax
from jax.experimental import pallas as pl
from jax.experimental.pallas import tpu as pltpu
from jax.sharding import PartitionSpec as P

MESH = pl.DeviceIdType.MESH
BF = jnp.bfloat16
F32 = jnp.float32


def dot(a, b, ca=1, cb=0):
    return lax.dot_general(a, b, (((ca,), (cb,)), ((), ())), preferred_element_type=F32)


def silu_slope(values):
    sigma = jax.nn.sigmoid(values)
    return sigma * (1.0 + values * (1.0 - sigma))


def iota(shape, dim):
    return lax.broadcasted_iota(jnp.int32, shape, dim)


def one_hot(hit):
    return jnp.where(hit, 1.0, 0.0).astype(BF)


def body(
    pending,
    feats_h, idxt_h, cnt_h, w_h, w1_h, w2_h, cot_h,
    out, gr1, gr2,
    feats, idxt, cnt, w, w1, w2, cot,
    wtb, wr, wb, wf, stage, g1, oh, oht, pk, own, rc, ab, rp, sw, g2,
    bk, tt, pb, fr, nr, cb,
    in_s, sw_s, sw_r, wx_s, wx_r, z1_s, z1_r, c1_s, c1_r, p1_s, p1_r, sx_s, sx_r, z2_s, z2_r,
    c2_s, c2_r, p2_s, p2_r, ox_s, ox_r, bp_s, bp_r, bc_s, bc_r, fr_s, fr_r, nr_r, n3_r,
    *sums,
):
    r = lax.axis_index("rows")
    x = lax.axis_index("rep")
    core = lax.rem(r, 2)
    z = lax.rem(lax.div(r, 2), 16)
    y = lax.div(r, 32)
    za = lax.div(z, 4)
    zb = lax.rem(z, 4)
    q = y * 4 + x
    other = 1 - core

    def rid(yy, zz, cc):
        return (yy * 16 + zz) * 2 + cc

    def peer(m):
        pq = lax.rem(q + m, 16)
        py, px = lax.div(pq, 4), lax.rem(pq, 4)
        return py, px, rid(py, z, core)

    def zat(m):
        return lax.rem(z + m + 16, 16)

    def zpeer(m):
        return rid(y, zat(m), core)

    def copy(src, dst, ssem, rsem, rows, rep):
        return pltpu.make_async_remote_copy(
            src_ref=src, dst_ref=dst, send_sem=ssem, recv_sem=rsem,
            device_id={"rows": rows, "rep": rep}, device_id_type=MESH,
        )

    def send(src, dst, ssem, rsem, rows, rep):
        c = copy(src, dst, ssem, rsem, rows, rep)
        c.start()
        return c

    def sent(ref, sem):
        pending.append(copy(ref, ref, sem, sem, rid(y, z, other), x).wait_send)

    def received(ref, sem):
        copy(ref, ref, sem, sem, rid(y, z, other), x).wait_recv()

    def to_core(src, dst, ssem, rsem):
        return send(src, dst, ssem, rsem, rid(y, z, other), x)

    barrier = pltpu.get_barrier_semaphore()

    def greet(rows, rep):
        pl.semaphore_signal(barrier, inc=1, device_id={"rows": rows, "rep": rep}, device_id_type=MESH)

    alone = x == zb
    swap_r, swap_x = rid(y, za * 4 + x, core), zb
    for m in (1, 2, 3, 4, 12, 13, 14, 15):
        greet(zpeer(m), x)
    for m in range(1, 16):
        py, px, pr = peer(m)
        greet(pr, px)
        greet(rid(py, z, other), px)
    greet(rid(y, z, other), x)

    @pl.when(jnp.logical_not(alone))
    def _():
        greet(swap_r, swap_x)

    ins = []
    for n, (a, b) in enumerate(
        [(feats_h, feats), (idxt_h, idxt), (cnt_h, cnt), (w_h, w), (w1_h, w1), (w2_h, w2), (cot_h, cot)]
    ):
        c = pltpu.make_async_copy(a, b, in_s.at[n])
        c.start()
        ins.append(c)

    mine = pl.ds(pl.multiple_of(x * 64, 64), 64)
    ins[0].wait()
    ins[1].wait()
    stage[0:64, :] = feats[mine, :]
    stage[64:80, :] = idxt[...].astype(F32).astype(BF)

    ins[2].wait()
    ins[3].wait()
    row = iota((512, 1), 0)
    plane, rest = row >> 4, row & 15
    source = ((rest >> 2) << 7) + ((plane >> 3) << 5) + ((rest & 3) << 3) + (plane & 7)
    order = one_hot(source == iota((512, 512), 1))
    def regroup_weights(sq):
        alive = [one_hot(cnt[...] > x * 16 + sq * 4 + s4) for s4 in range(4)]
        live = w[:, sq * 512:(sq + 1) * 512] * jnp.concatenate(alive, axis=1)
        wtb[:, sq] = dot(order, live, 1, 1).astype(BF).reshape(32, 16, 256)

    regroup_weights(0)
    regroup_weights(1)

    pl.semaphore_wait(barrier, 40 - alone.astype(jnp.int32))

    def swap(src, dst, ssem, rsem):
        c = copy(src, dst, ssem, rsem, swap_r, swap_x)

        @pl.when(alone)
        def _():
            dst[...] = src[...]

        @pl.when(jnp.logical_not(alone))
        def _():
            c.start()

        def finish():
            @pl.when(jnp.logical_not(alone))
            def _():
                c.wait_recv()

        def sent():
            @pl.when(jnp.logical_not(alone))
            def _():
                c.wait_send()

        pending.append(sent)
        return finish

    swap_done = swap(stage, g1.at[za * 4 + x], sw_s, sw_r)
    regroup_weights(2)
    regroup_weights(3)

    me8 = y * 2 + core
    for off in (2, 1, 3, 0):
        for mx in (2, 1, 3, 0):
            py, px = lax.rem(y + off, 4), lax.rem(x + mx, 4)
            for n, h in enumerate((core, other)):
                if off + mx + n:
                    send(wtb.at[(py * 4 + px) * 2 + h], wr.at[me8 * 4 + x], wx_s, wx_r.at[off], rid(py, z, h), px)
    sent(wtb.at[pl.ds(0, 31)], wx_s)
    wr[me8 * 4 + x] = wtb[q * 2 + core]
    yield "prep"

    row, col = iota((256, 1), 0), iota((256, 256), 1)
    regroup = one_hot(((row & 63) << 2) + (row >> 6) == col)
    eye = one_hot(row == col)
    swap_done()
    yield "swap1"

    def gather_z(g, rows, cut, ssem, rsem):
        full, parts = pl.ds(0, rows), (pl.ds(0, cut), pl.ds(cut, rows - cut))
        relay = {}

        def move(dist, via):
            for d in range(2):
                sign = 1 if d == 0 else -1
                if via:
                    relay[d, via].wait_recv()
                for there in (6, 8, 5) if dist == 6 else (dist,):
                    piece = g.at[zat(-sign * via), parts[d] if there == 8 else full]
                    sem = rsem.at[d * 3 + there // 2 - 1] if there in (2, 4, 6) else rsem.at[6]
                    relay[d, there] = send(piece, piece, ssem, sem, zpeer(sign * (there - via)), x)

        for dist in (4, 2, 1):
            move(dist, 0)
        yield
        move(3, 2)
        move(6, 4)
        yield
        move(7, 6)
        sent(g.at[pl.ds(0, 15)], ssem)
        yield
        received(g.at[pl.ds(0, 9)], rsem.at[6])
        yield

    gather1 = gather_z(g1, 80, 48, z1_s, z1_r)
    for _ in range(3):
        next(gather1)

    def weights(k):
        wb[k] = dot(regroup, wr[pl.ds(k * 4, 4)].reshape(256, 256)).astype(BF)
        wf[k] = dot(eye, wb[k], 1, 1).astype(BF)

    for off in (2, 1, 3, 0):
        received(wr.at[pl.ds(0, 8 if off else 7)], wx_r.at[off])
        for h in range(2):
            weights(lax.rem(y - off + 4, 4) * 2 + h)
    next(gather1)
    yield "gz1"

    ids = g1[:, 64:80, :].reshape(256, 128)
    lane = iota((256, 256), 1).astype(F32)
    for k in range(8):
        at = ((k // 2) * 16 + z) * 2 + k % 2
        rows = dot(ids, one_hot(iota((128, 256), 0) == at))
        oh[:, k * 64:(k + 1) * 64, :] = one_hot(rows == lane).reshape(4, 64, 256)
    for a in range(4):
        pk[0, a] = dot(oh[a], g1[4 * a:4 * a + 4, 0:64, :].reshape(256, 128)).astype(BF)

    yield "picks1"


    near = (2, 3, 1, 0)

    def reduce_send(t, csem_s, csem_r, psem_s, psem_r):
        def partial(k):
            return dot(wf[k], pk[t, :, pl.ds(pl.multiple_of(k * 64, 64), 64), :].reshape(256, 128))

        cs, mine_j = [], []

        def first(off):
            j = lax.rem(y + off, 4)
            own[t, j] = partial(j * 2 + other).astype(BF)
            cs.append(to_core(own.at[t, j], rc.at[t, j], csem_s, csem_r.at[off]))
            mine_j.append(partial(j * 2 + core))

        def second(n):
            off = near[n]
            j = lax.rem(y + off, 4)
            cs[n].wait_recv()
            ab[t, j] = (mine_j[n] + rc[t, j].astype(F32)).astype(BF).reshape(4, 64, 128)
            for mx in (2, 1, 3, 0):
                if off + mx:
                    px = lax.rem(x + mx, 4)
                    send(ab.at[t, j, px], rp.at[t, off * 4 + mx], psem_s, psem_r, rid(j, z, core), px)

        first(near[0])
        for n in range(1, 4):
            first(near[n])
            second(n - 1)
        second(3)
        sent(own.at[t], csem_s)
        sent(rp.at[t, pl.ds(1, 15)], psem_s)

    def reduce_add(t, psem_r):
        received(rp.at[t, pl.ds(1, 15)], psem_r)
        res = ab[t, y, x].astype(F32)
        for m in range(1, 16):
            res = res + rp[t, m].astype(F32)
        return res.astype(BF)

    reduce_send(0, c1_s, c1_r, p1_s, p1_r)
    sw[0] = reduce_add(0, p1_r)
    yield "red1"
    swap(sw.at[0], sw.at[1], sx_s, sx_r)()
    yield "swap2"
    for n in (4, 5, 6):
        ins[n].wait()
    agg1 = sw[1]
    z_one = dot(agg1, w1[...])
    hidden = (z_one * jax.nn.sigmoid(z_one)).astype(BF)
    halves = []
    for t in range(2):
        g2[t, z] = hidden[:, t * 128:(t + 1) * 128]
        halves.append(gather_z(g2.at[t], 64, 32, z2_s.at[t], z2_r.at[t]))
        next(halves[t])
    for a in range(4):
        oht[a] = dot(eye, oh[a], 1, 1).astype(BF)
    for stage in range(2):
        for t in range(2):
            next(halves[t])
    for t in range(2):
        next(halves[t])
        for a in range(4):
            pk[1 + t, a] = dot(oh[a], g2[t, 4 * a:4 * a + 4].reshape(256, 128)).astype(BF)
        reduce_send(1 + t, c2_s.at[t], c2_r.at[t], p2_s.at[t], p2_r.at[t])
    agg2 = jnp.concatenate([reduce_add(1 + t, p2_r.at[t]) for t in range(2)], axis=1)
    yield "red2"

    z_two = dot(agg2, w2[...])
    dz2 = (cot[mine, :].astype(F32) * silu_slope(z_two)).astype(BF)
    back = dot(dz2, w2[...], 1, 1).astype(BF)
    for t in range(2):
        bk[t, y, core, mine, :] = back[:, t * 128:(t + 1) * 128]
        piece = bk.at[t, y, core, mine]
        for off in (2, 1, 3, 0):
            for mx in (2, 1, 3, 0):
                if off + mx:
                    py, px = lax.rem(y + off, 4), lax.rem(x + mx, 4)
                    send(piece, piece, bp_s.at[t], bp_r.at[t, off], rid(py, z, core), px)
        sent(pb.at[t, pl.ds(0, 15)], bp_s.at[t])
    out[mine, :] = (z_two * jax.nn.sigmoid(z_two)).astype(BF)
    for m in range(1, 4):
        send(out.at[mine], out.at[mine], ox_s, ox_r, r, lax.rem(x + m, 4))
    sent(out.at[pl.ds(0, 192)], ox_s)

    def reduce_all(ga, gc, gs, gp, gz, gt, c_s, c_r, p_s, p_r, z_s, z_r, t_s, t_r, d_s, d_r):
        c = to_core(ga.at[other], gc, c_s, c_r)
        sent(gc, c_s)
        yield
        c.wait_recv()
        gs[...] = ga[core] + gc[...]
        for m in range(1, 16):
            py, px, pr = peer(m)
            send(gs.at[py * 4 + px], gp.at[m], p_s, p_r, pr, px)
        sent(gp.at[pl.ds(1, 15)], p_s)
        yield
        received(gp.at[pl.ds(1, 15)], p_r)
        total = gs[q]
        for m in range(1, 16):
            total = total + gp[m]
        wide = gz.dtype == BF
        gz[0] = jnp.concatenate([total[:, :128], total[:, 128:]], axis=0).astype(BF) if wide else total
        for m in (8, 7, 9, 6, 10, 5, 11, 4, 12, 3, 13, 2, 14, 1, 15):
            send(gz.at[0], gz.at[m], z_s, z_r, zpeer(m), x)
        sent(gz.at[pl.ds(1, 15)], z_s)
        yield
        received(gz.at[pl.ds(1, 15)], z_r)
        total = gz[z].astype(F32)
        for k in range(1, 16):
            total = total + gz[lax.rem(z - k + 16, 16)].astype(F32)
        gt[q, core] = jnp.concatenate([total[:8], total[8:]], axis=1) if wide else total
        c = to_core(gt.at[q, core], gt.at[q, core], d_s, d_r)
        sent(gt.at[q, core], d_s)
        yield
        c.wait_recv()
        for m in range(1, 16):
            py, px, pr = peer(m)
            send(gt.at[q], gt.at[q], t_s, t_r, pr, px)
        sent(gt.at[pl.ds(0, 15)], t_s)
        yield
        received(gt.at[pl.ds(0, 15)], t_r)
        yield

    half = len(sums) // 2
    ga2, ga1 = sums[0], sums[half]
    reduce2, reduce1 = reduce_all(*sums[:half]), reduce_all(*sums[half:])
    ga2[...] = dot(agg2, dz2, 0, 0).reshape(2, 16, 8, 256)
    next(reduce2)

    def slot_terms(t, k):
        got = dot(wb[k], bk[t, lax.div(k, 2), lax.rem(k, 2)]).astype(BF)
        tt[t, :, pl.ds(pl.multiple_of(k * 64, 64), 64), :] = got.reshape(4, 64, 128)

    next(reduce2)
    cc = {}

    def own_blocks(t):
        for off in (0, 1, 3, 2):
            j = lax.rem(y - off + 4, 4)
            block = bk.at[t, j, core]
            received(block if off else bk.at[t, j, core, pl.ds(0, 192)], bp_r.at[t, off])
            cc[t, off] = to_core(block, block, bc_s.at[t], bc_r.at[t, off])
            slot_terms(t, j * 2 + core)
        sent(bk.at[t, :, 0], bc_s.at[t])

    def other_blocks(t):
        for off in (0, 1, 3, 2):
            cc[t, off].wait_recv()
            slot_terms(t, lax.rem(y - off + 4, 4) * 2 + other)
        for a in range(4):
            pb[t, 4 * a:4 * a + 4] = dot(oht[a], tt[t, a]).astype(BF).reshape(4, 64, 128)

    full, parts = pl.ds(0, 64), (pl.ds(0, 32), pl.ds(32, 32))
    ways = ((0, 1), (1, -1))
    halfway = {}

    def scatter(t):
        for m in (4, 3, 2, 1):
            for d, sign in ways:
                part = parts[d] if m == 4 else full
                c = send(pb.at[t, zat(sign * (4 + m)), part], fr.at[t, d, m, part], fr_s.at[t],
                         fr_r.at[t, d, 1 if m == 4 else 0], zpeer(sign * m), x)
                if m == 4:
                    halfway[t, d] = c
        for d, sign in ways:
            halfway[t, d, 3] = send(pb.at[t, zat(sign * 3)], fr.at[t, d, 0], fr_s.at[t], n3_r.at[t, d], zpeer(sign), x)
        for d, sign in ways:
            send(pb.at[t, zat(sign)], nr.at[t, d, 1], fr_s.at[t], nr_r.at[t, d], zpeer(sign), x)

    def pass_near(t):
        for d, sign in ways:
            halfway[t, d, 3].wait_recv()
            cb[t, d, 1] = (pb[t, zat(sign * 2)].astype(F32) + fr[t, d, 0].astype(F32)).astype(BF)
            send(cb.at[t, d, 1], nr.at[t, d, 2], fr_s.at[t], nr_r.at[t, d], zpeer(sign * 2), x)

    def pass_on(t):
        for d, sign in ways:
            acc = pb[t, zat(sign * 4)].astype(F32)
            received(fr.at[t, d, pl.ds(1, 3)], fr_r.at[t, d, 0])
            for m in (1, 2, 3):
                acc = acc + fr[t, d, m].astype(F32)
            halfway[t, d].wait_recv()
            lo = 0 if d == 0 else 32
            cb[t, d, 0] = acc.astype(BF)
            cb[t, d, 0, lo:lo + 32, :] = (acc[lo:lo + 32] + fr[t, d, 4, lo:lo + 32, :].astype(F32)).astype(BF)
            send(cb.at[t, d, 0], nr.at[t, d, 3], fr_s.at[t], nr_r.at[t, d], zpeer(sign * 4), x)
        sent(pb.at[t, pl.ds(0, 15)], fr_s.at[t])

    def collect(t):
        dh = pb[t, z].astype(F32)
        for d in range(2):
            received(nr.at[t, d, pl.ds(1, 3)], nr_r.at[t, d])
            for m in (1, 2, 3):
                dh = dh + nr[t, d, m].astype(F32)
        return dh

    own_blocks(0)
    next(reduce2)
    other_blocks(0)
    scatter(0)
    own_blocks(1)
    other_blocks(1)
    yield "bwait"
    scatter(1)
    pass_near(0)
    slope = silu_slope(z_one)
    pass_near(1)
    pass_on(0)
    pass_on(1)
    next(reduce2)
    for t in range(2):
        dz1 = (collect(t) * slope[:, t * 128:(t + 1) * 128]).astype(BF)
        ga1[:, :, t] = dot(agg1, dz1, 0, 0).reshape(2, 8, 8, 128)
        if t == 0:
            next(reduce2)
    yield "rsz"
    ga1 = ga1.reshape(2, 16, 8, 128)
    reduce1 = reduce_all(ga1, *sums[half + 1:])
    next(reduce1)
    yield "arc"
    next(reduce1)
    next(reduce2)
    for n in range(2):
        gr2[n * 128:(n + 1) * 128, :] = sums[5][:, n].reshape(128, 256)
    yield "arp"
    next(reduce1)
    yield "arz"
    next(reduce1)
    yield "art"
    next(reduce1)
    next(reduce1)
    gt1 = sums[half + 5]
    for b in range(2):
        for k in range(8):
            gr1[:, k, :, b * 128:(b + 1) * 128] = gt1[2 * k + b]
    received(out.at[pl.ds(0, 192)], ox_r)


def kernel(*refs):
    pending = []
    for _ in body(pending, *refs):
        pass
    for wait in pending:
        wait()


def local(feats, edge_w, send_rows, counts, w_one, w_two, cotangent):
    idxt = jnp.transpose(send_rows[0])
    vm = pl.BlockSpec(memory_space=pltpu.VMEM)
    hbm = pl.BlockSpec(memory_space=pl.ANY)
    args = (feats, idxt, counts, edge_w, w_one, w_two, cotangent)
    dma = pltpu.SemaphoreType.DMA

    def vmem(kind, *shape):
        return pltpu.VMEM(shape, kind)

    one = dma(())
    scratch = [pltpu.VMEM(a.shape, a.dtype) for a in args] + [
        vmem(BF, 32, 4, 16, 256),
        vmem(BF, 32, 4, 16, 256),
        vmem(BF, 8, 256, 256),
        vmem(BF, 8, 256, 256),
        vmem(BF, 80, 128),
        vmem(BF, 16, 80, 128),
        vmem(BF, 4, 512, 256),
        vmem(BF, 4, 256, 512),
        vmem(BF, 3, 4, 512, 128),
        vmem(BF, 3, 4, 256, 128),
        vmem(BF, 3, 4, 256, 128),
        vmem(BF, 3, 4, 4, 64, 128),
        vmem(BF, 3, 16, 64, 128),
        vmem(BF, 2, 64, 128),
        vmem(BF, 2, 16, 64, 128),
        vmem(BF, 2, 4, 2, 256, 128),
        vmem(BF, 2, 4, 512, 128),
        vmem(BF, 2, 16, 64, 128),
        vmem(BF, 2, 2, 5, 64, 128),
        vmem(BF, 2, 2, 4, 64, 128),
        vmem(BF, 2, 2, 2, 64, 128),
        dma((7,)), one, one, one, dma((4,)), one, dma((7,)),
        one, dma((4,)), one, one, one, one, dma((2,)), dma((2, 7)),
        dma((2,)), dma((2, 4)), dma((2,)), dma((2,)), one, one, dma((2,)), dma((2, 4)),
        dma((2,)), dma((2, 4)), dma((2,)), dma((2, 2, 2)), dma((2, 2)), dma((2, 2)),
    ]
    for width, first in ((256, (2, 16, 8, 256)), (128, (2, 8, 2, 8, 128))):
        scratch += [
            vmem(F32, *first),
            vmem(F32, 16, 8, width),
            vmem(F32, 16, 8, width),
            vmem(F32, 16, 8, width),
            vmem(BF, 16, 16, 128) if width == 256 else vmem(F32, 16, 8, width),
            vmem(F32, 16, 2, 8, width),
        ] + [one] * 10
    out, gr1, gr2 = pl.pallas_call(
        kernel,
        out_shape=(
            jax.ShapeDtypeStruct((256, 256), BF),
            jax.ShapeDtypeStruct((2, 8, 8, 256), F32),
            jax.ShapeDtypeStruct((256, 256), F32),
        ),
        in_specs=[hbm] * 7,
        out_specs=(vm, vm, vm),
        scratch_shapes=scratch,
        compiler_params=pltpu.CompilerParams(
            collective_id=0, has_side_effects=True, vmem_limit_bytes=56 * 1024 * 1024
        ),
    )(*args)
    return out, gr1.reshape(128, 256), gr2


def solution(mesh):
    in_specs = (
        P("rows", None),
        P("rows", "rep"),
        P("rows", None, "rep"),
        P("rows", None),
        P(),
        P(),
        P("rows", None),
    )
    out_specs = (P("rows", None), P(), P())
    return jax.shard_map(local, mesh=mesh, in_specs=in_specs, out_specs=out_specs, check_vma=False)
```

```python
import jax
import jax.numpy as jnp
from jax import lax
from jax.experimental import pallas as pl
from jax.experimental.pallas import tpu as pltpu
from jax.sharding import PartitionSpec as P

MESH = pl.DeviceIdType.MESH
BF = jnp.bfloat16
F32 = jnp.float32


def dot(a, b, ca=1, cb=0):
    return lax.dot_general(a, b, (((ca,), (cb,)), ((), ())), preferred_element_type=F32)


def silu_slope(values):
    sigma = jax.nn.sigmoid(values)
    return sigma * (1.0 + values * (1.0 - sigma))


def iota(shape, dim):
    return lax.broadcasted_iota(jnp.int32, shape, dim)


def one_hot(hit):
    return jnp.where(hit, 1.0, 0.0).astype(BF)


def body(
    pending,
    feats_h, idxt_h, cnt_h, w_h, w1_h, w2_h, cot_h,
    out, gr1, gr2,
    feats, idxt, cnt, w, w1, w2, cot,
    wtb, wr, wb, wf, stage, g1, oh, oht, pk, own, rc, ab, rp, sw, g2,
    bk, tt, pb, fr, nr, cb,
    in_s, sw_s, sw_r, wx_s, wx_r, z1_s, z1_r, c1_s, c1_r, p1_s, p1_r, sx_s, sx_r, z2_s, z2_r,
    c2_s, c2_r, p2_s, p2_r, ox_s, ox_r, bp_s, bp_r, bc_s, bc_r, fr_s, fr_r, nr_r, n3_r,
    *sums,
):
    r = lax.axis_index("rows")
    x = lax.axis_index("rep")
    core = lax.rem(r, 2)
    z = lax.rem(lax.div(r, 2), 16)
    y = lax.div(r, 32)
    za = lax.div(z, 4)
    zb = lax.rem(z, 4)
    q = y * 4 + x
    other = 1 - core

    def rid(yy, zz, cc):
        return (yy * 16 + zz) * 2 + cc

    def peer(m):
        pq = lax.rem(q + m, 16)
        py, px = lax.div(pq, 4), lax.rem(pq, 4)
        return py, px, rid(py, z, core)

    def zat(m):
        return lax.rem(z + m + 16, 16)

    def zpeer(m):
        return rid(y, zat(m), core)

    def copy(src, dst, ssem, rsem, rows, rep):
        return pltpu.make_async_remote_copy(
            src_ref=src, dst_ref=dst, send_sem=ssem, recv_sem=rsem,
            device_id={"rows": rows, "rep": rep}, device_id_type=MESH,
        )

    def send(src, dst, ssem, rsem, rows, rep):
        c = copy(src, dst, ssem, rsem, rows, rep)
        c.start()
        return c

    def sent(ref, sem):
        pending.append(copy(ref, ref, sem, sem, rid(y, z, other), x).wait_send)

    def received(ref, sem):
        copy(ref, ref, sem, sem, rid(y, z, other), x).wait_recv()

    def to_core(src, dst, ssem, rsem):
        return send(src, dst, ssem, rsem, rid(y, z, other), x)

    barrier = pltpu.get_barrier_semaphore()

    def greet(rows, rep):
        pl.semaphore_signal(barrier, inc=1, device_id={"rows": rows, "rep": rep}, device_id_type=MESH)

    alone = x == zb
    swap_r, swap_x = rid(y, za * 4 + x, core), zb
    for m in (1, 2, 3, 4, 12, 13, 14, 15):
        greet(zpeer(m), x)
    for m in range(1, 16):
        py, px, pr = peer(m)
        greet(pr, px)
        greet(rid(py, z, other), px)
    greet(rid(y, z, other), x)

    @pl.when(jnp.logical_not(alone))
    def _():
        greet(swap_r, swap_x)

    ins = []
    for n, (a, b) in enumerate(
        [(feats_h, feats), (idxt_h, idxt), (cnt_h, cnt), (w_h, w), (w1_h, w1), (w2_h, w2), (cot_h, cot)]
    ):
        c = pltpu.make_async_copy(a, b, in_s.at[n])
        c.start()
        ins.append(c)

    mine = pl.ds(pl.multiple_of(x * 64, 64), 64)
    ins[0].wait()
    ins[1].wait()
    stage[0:64, :] = feats[mine, :]
    stage[64:80, :] = idxt[...].astype(F32).astype(BF)

    ins[2].wait()
    ins[3].wait()
    row = iota((512, 1), 0)
    plane, rest = row >> 4, row & 15
    source = ((rest >> 2) << 7) + ((plane >> 3) << 5) + ((rest & 3) << 3) + (plane & 7)
    order = one_hot(source == iota((512, 512), 1))
    for sq in range(4):
        alive = [one_hot(cnt[...] > x * 16 + sq * 4 + s4) for s4 in range(4)]
        live = w[:, sq * 512:(sq + 1) * 512] * jnp.concatenate(alive, axis=1)
        wtb[:, sq] = dot(order, live, 1, 1).astype(BF).reshape(32, 16, 256)

    pl.semaphore_wait(barrier, 40 - alone.astype(jnp.int32))

    def swap(src, dst, ssem, rsem):
        c = copy(src, dst, ssem, rsem, swap_r, swap_x)

        @pl.when(alone)
        def _():
            dst[...] = src[...]

        @pl.when(jnp.logical_not(alone))
        def _():
            c.start()

        def finish():
            @pl.when(jnp.logical_not(alone))
            def _():
                c.wait_recv()

        def sent():
            @pl.when(jnp.logical_not(alone))
            def _():
                c.wait_send()

        pending.append(sent)
        return finish

    swap_done = swap(stage, g1.at[za * 4 + x], sw_s, sw_r)

    me8 = y * 2 + core
    for off in (2, 1, 3, 0):
        for mx in (2, 1, 3, 0):
            py, px = lax.rem(y + off, 4), lax.rem(x + mx, 4)
            for n, h in enumerate((core, other)):
                if off + mx + n:
                    send(wtb.at[(py * 4 + px) * 2 + h], wr.at[me8 * 4 + x], wx_s, wx_r.at[off], rid(py, z, h), px)
    sent(wtb.at[pl.ds(0, 31)], wx_s)
    wr[me8 * 4 + x] = wtb[q * 2 + core]
    yield "prep"

    row, col = iota((256, 1), 0), iota((256, 256), 1)
    regroup = one_hot(((row & 63) << 2) + (row >> 6) == col)
    eye = one_hot(row == col)
    swap_done()
    yield "swap1"

    def gather_z(g, rows, cut, ssem, rsem):
        full, parts = pl.ds(0, rows), (pl.ds(0, cut), pl.ds(cut, rows - cut))
        relay = {}

        def move(dist, via):
            for d in range(2):
                sign = 1 if d == 0 else -1
                if via:
                    relay[d, via].wait_recv()
                for there in (6, 8, 5) if dist == 6 else (dist,):
                    piece = g.at[zat(-sign * via), parts[d] if there == 8 else full]
                    sem = rsem.at[d * 3 + there // 2 - 1] if there in (2, 4, 6) else rsem.at[6]
                    relay[d, there] = send(piece, piece, ssem, sem, zpeer(sign * (there - via)), x)

        for dist in (4, 2, 1):
            move(dist, 0)
        yield
        move(3, 2)
        move(6, 4)
        yield
        move(7, 6)
        sent(g.at[pl.ds(0, 15)], ssem)
        yield
        received(g.at[pl.ds(0, 9)], rsem.at[6])
        yield

    gather1 = gather_z(g1, 80, 48, z1_s, z1_r)
    for _ in range(3):
        next(gather1)

    def weights(k):
        wb[k] = dot(regroup, wr[pl.ds(k * 4, 4)].reshape(256, 256)).astype(BF)
        wf[k] = dot(eye, wb[k], 1, 1).astype(BF)

    for off in (2, 1, 3, 0):
        received(wr.at[pl.ds(0, 8 if off else 7)], wx_r.at[off])
        for h in range(2):
            weights(lax.rem(y - off + 4, 4) * 2 + h)
    next(gather1)
    yield "gz1"

    ids = g1[:, 64:80, :].reshape(256, 128)
    lane = iota((256, 256), 1).astype(F32)
    for k in range(8):
        at = ((k // 2) * 16 + z) * 2 + k % 2
        rows = dot(ids, one_hot(iota((128, 256), 0) == at))
        oh[:, k * 64:(k + 1) * 64, :] = one_hot(rows == lane).reshape(4, 64, 256)
    for a in range(4):
        pk[0, a] = dot(oh[a], g1[4 * a:4 * a + 4, 0:64, :].reshape(256, 128)).astype(BF)

    yield "picks1"


    near = (2, 3, 1, 0)

    def reduce_send(t, csem_s, csem_r, psem_s, psem_r):
        def partial(k):
            return dot(wf[k], pk[t, :, pl.ds(pl.multiple_of(k * 64, 64), 64), :].reshape(256, 128))

        cs, mine_j = [], []

        def first(off):
            j = lax.rem(y + off, 4)
            own[t, j] = partial(j * 2 + other).astype(BF)
            cs.append(to_core(own.at[t, j], rc.at[t, j], csem_s, csem_r.at[off]))
            mine_j.append(partial(j * 2 + core))

        def second(n):
            off = near[n]
            j = lax.rem(y + off, 4)
            cs[n].wait_recv()
            ab[t, j] = (mine_j[n] + rc[t, j].astype(F32)).astype(BF).reshape(4, 64, 128)
            for mx in (2, 1, 3, 0):
                if off + mx:
                    px = lax.rem(x + mx, 4)
                    send(ab.at[t, j, px], rp.at[t, off * 4 + mx], psem_s, psem_r, rid(j, z, core), px)

        first(near[0])
        for n in range(1, 4):
            first(near[n])
            second(n - 1)
        second(3)
        sent(own.at[t], csem_s)
        sent(rp.at[t, pl.ds(1, 15)], psem_s)

    def reduce_add(t, psem_r):
        received(rp.at[t, pl.ds(1, 15)], psem_r)
        res = ab[t, y, x].astype(F32)
        for m in range(1, 16):
            res = res + rp[t, m].astype(F32)
        return res.astype(BF)

    reduce_send(0, c1_s, c1_r, p1_s, p1_r)
    sw[0] = reduce_add(0, p1_r)
    yield "red1"
    swap(sw.at[0], sw.at[1], sx_s, sx_r)()
    yield "swap2"
    for n in (4, 5, 6):
        ins[n].wait()
    agg1 = sw[1]
    z_one = dot(agg1, w1[...])
    hidden = (z_one * jax.nn.sigmoid(z_one)).astype(BF)
    halves = []
    for t in range(2):
        g2[t, z] = hidden[:, t * 128:(t + 1) * 128]
        halves.append(gather_z(g2.at[t], 64, 32, z2_s.at[t], z2_r.at[t]))
        next(halves[t])
    for a in range(4):
        oht[a] = dot(eye, oh[a], 1, 1).astype(BF)
    for stage in range(2):
        for t in range(2):
            next(halves[t])
    for t in range(2):
        next(halves[t])
        for a in range(4):
            pk[1 + t, a] = dot(oh[a], g2[t, 4 * a:4 * a + 4].reshape(256, 128)).astype(BF)
        reduce_send(1 + t, c2_s.at[t], c2_r.at[t], p2_s.at[t], p2_r.at[t])
    agg2 = jnp.concatenate([reduce_add(1 + t, p2_r.at[t]) for t in range(2)], axis=1)
    yield "red2"

    z_two = dot(agg2, w2[...])
    dz2 = (cot[mine, :].astype(F32) * silu_slope(z_two)).astype(BF)
    back = dot(dz2, w2[...], 1, 1).astype(BF)
    for t in range(2):
        bk[t, y, core, mine, :] = back[:, t * 128:(t + 1) * 128]
        piece = bk.at[t, y, core, mine]
        for off in (2, 1, 3, 0):
            for mx in (2, 1, 3, 0):
                if off + mx:
                    py, px = lax.rem(y + off, 4), lax.rem(x + mx, 4)
                    send(piece, piece, bp_s.at[t], bp_r.at[t, off], rid(py, z, core), px)
        sent(pb.at[t, pl.ds(0, 15)], bp_s.at[t])
    out[mine, :] = (z_two * jax.nn.sigmoid(z_two)).astype(BF)
    for m in range(1, 4):
        send(out.at[mine], out.at[mine], ox_s, ox_r, r, lax.rem(x + m, 4))
    sent(out.at[pl.ds(0, 192)], ox_s)

    def reduce_all(ga, gc, gs, gp, gz, gt, c_s, c_r, p_s, p_r, z_s, z_r, t_s, t_r, d_s, d_r):
        c = to_core(ga.at[other], gc, c_s, c_r)
        sent(gc, c_s)
        yield
        c.wait_recv()
        gs[...] = ga[core] + gc[...]
        for m in range(1, 16):
            py, px, pr = peer(m)
            send(gs.at[py * 4 + px], gp.at[m], p_s, p_r, pr, px)
        sent(gp.at[pl.ds(1, 15)], p_s)
        yield
        received(gp.at[pl.ds(1, 15)], p_r)
        total = gs[q]
        for m in range(1, 16):
            total = total + gp[m]
        wide = gz.dtype == BF
        gz[0] = jnp.concatenate([total[:, :128], total[:, 128:]], axis=0).astype(BF) if wide else total
        for m in (8, 7, 9, 6, 10, 5, 11, 4, 12, 3, 13, 2, 14, 1, 15):
            send(gz.at[0], gz.at[m], z_s, z_r, zpeer(m), x)
        sent(gz.at[pl.ds(1, 15)], z_s)
        yield
        received(gz.at[pl.ds(1, 15)], z_r)
        total = gz[z].astype(F32)
        for k in range(1, 16):
            total = total + gz[lax.rem(z - k + 16, 16)].astype(F32)
        gt[core, q] = jnp.concatenate([total[:8], total[8:]], axis=1) if wide else total
        for m in range(1, 16):
            py, px, pr = peer(m)
            send(gt.at[core, q], gt.at[core, q], t_s, t_r, pr, px)
        sent(gt.at[core, pl.ds(0, 15)], t_s)
        yield
        received(gt.at[core, pl.ds(0, 15)], t_r)
        c = to_core(gt.at[core], gt.at[core], d_s, d_r)
        sent(gt.at[core], d_s)
        yield
        c.wait_recv()
        yield

    half = len(sums) // 2
    ga2, ga1 = sums[0], sums[half]
    reduce2, reduce1 = reduce_all(*sums[:half]), reduce_all(*sums[half:])
    ga2[...] = dot(agg2, dz2, 0, 0).reshape(2, 16, 8, 256)
    next(reduce2)

    def slot_terms(t, k):
        got = dot(wb[k], bk[t, lax.div(k, 2), lax.rem(k, 2)]).astype(BF)
        tt[t, :, pl.ds(pl.multiple_of(k * 64, 64), 64), :] = got.reshape(4, 64, 128)

    next(reduce2)
    cc = {}

    def own_blocks(t):
        for off in (0, 1, 3, 2):
            j = lax.rem(y - off + 4, 4)
            block = bk.at[t, j, core]
            received(block if off else bk.at[t, j, core, pl.ds(0, 192)], bp_r.at[t, off])
            cc[t, off] = to_core(block, block, bc_s.at[t], bc_r.at[t, off])
            slot_terms(t, j * 2 + core)
        sent(bk.at[t, :, 0], bc_s.at[t])

    def other_blocks(t):
        for off in (0, 1, 3, 2):
            cc[t, off].wait_recv()
            slot_terms(t, lax.rem(y - off + 4, 4) * 2 + other)
        for a in range(4):
            pb[t, 4 * a:4 * a + 4] = dot(oht[a], tt[t, a]).astype(BF).reshape(4, 64, 128)

    full, parts = pl.ds(0, 64), (pl.ds(0, 32), pl.ds(32, 32))
    ways = ((0, 1), (1, -1))
    halfway = {}

    def scatter(t):
        for m in (4, 3, 2, 1):
            for d, sign in ways:
                part = parts[d] if m == 4 else full
                c = send(pb.at[t, zat(sign * (4 + m)), part], fr.at[t, d, m, part], fr_s.at[t],
                         fr_r.at[t, d, 1 if m == 4 else 0], zpeer(sign * m), x)
                if m == 4:
                    halfway[t, d] = c
        for d, sign in ways:
            halfway[t, d, 3] = send(pb.at[t, zat(sign * 3)], fr.at[t, d, 0], fr_s.at[t], n3_r.at[t, d], zpeer(sign), x)
        for d, sign in ways:
            send(pb.at[t, zat(sign)], nr.at[t, d, 1], fr_s.at[t], nr_r.at[t, d], zpeer(sign), x)

    def pass_near(t):
        for d, sign in ways:
            halfway[t, d, 3].wait_recv()
            cb[t, d, 1] = (pb[t, zat(sign * 2)].astype(F32) + fr[t, d, 0].astype(F32)).astype(BF)
            send(cb.at[t, d, 1], nr.at[t, d, 2], fr_s.at[t], nr_r.at[t, d], zpeer(sign * 2), x)

    def pass_on(t):
        for d, sign in ways:
            acc = pb[t, zat(sign * 4)].astype(F32)
            received(fr.at[t, d, pl.ds(1, 3)], fr_r.at[t, d, 0])
            for m in (1, 2, 3):
                acc = acc + fr[t, d, m].astype(F32)
            halfway[t, d].wait_recv()
            lo = 0 if d == 0 else 32
            cb[t, d, 0] = acc.astype(BF)
            cb[t, d, 0, lo:lo + 32, :] = (acc[lo:lo + 32] + fr[t, d, 4, lo:lo + 32, :].astype(F32)).astype(BF)
            send(cb.at[t, d, 0], nr.at[t, d, 3], fr_s.at[t], nr_r.at[t, d], zpeer(sign * 4), x)
        sent(pb.at[t, pl.ds(0, 15)], fr_s.at[t])

    def collect(t):
        dh = pb[t, z].astype(F32)
        for d in range(2):
            received(nr.at[t, d, pl.ds(1, 3)], nr_r.at[t, d])
            for m in (1, 2, 3):
                dh = dh + nr[t, d, m].astype(F32)
        return dh

    own_blocks(0)
    other_blocks(0)
    scatter(0)
    own_blocks(1)
    other_blocks(1)
    yield "bwait"
    scatter(1)
    pass_near(0)
    slope = silu_slope(z_one)
    pass_near(1)
    pass_on(0)
    pass_on(1)
    next(reduce2)
    for t in range(2):
        dz1 = (collect(t) * slope[:, t * 128:(t + 1) * 128]).astype(BF)
        ga1[:, :, t] = dot(agg1, dz1, 0, 0).reshape(2, 8, 8, 128)
    yield "rsz"
    ga1 = ga1.reshape(2, 16, 8, 128)
    reduce1 = reduce_all(ga1, *sums[half + 1:])
    next(reduce1)
    yield "arc"
    next(reduce1)
    next(reduce2)
    yield "arp"
    next(reduce1)
    next(reduce2)
    yield "arz"
    next(reduce1)
    next(reduce2)
    gr2[...] = sums[5][...].reshape(256, 256)
    yield "art"
    next(reduce1)
    next(reduce1)
    gt1 = sums[half + 5]
    for b in range(2):
        for k in range(8):
            gr1[:, k, :, b * 128:(b + 1) * 128] = gt1[:, 2 * k + b]
    received(out.at[pl.ds(0, 192)], ox_r)


def kernel(*refs):
    pending = []
    for _ in body(pending, *refs):
        pass
    for wait in pending:
        wait()


def local(feats, edge_w, send_rows, counts, w_one, w_two, cotangent):
    idxt = jnp.transpose(send_rows[0])
    vm = pl.BlockSpec(memory_space=pltpu.VMEM)
    hbm = pl.BlockSpec(memory_space=pl.ANY)
    args = (feats, idxt, counts, edge_w, w_one, w_two, cotangent)
    dma = pltpu.SemaphoreType.DMA

    def vmem(kind, *shape):
        return pltpu.VMEM(shape, kind)

    one = dma(())
    scratch = [pltpu.VMEM(a.shape, a.dtype) for a in args] + [
        vmem(BF, 32, 4, 16, 256),
        vmem(BF, 32, 4, 16, 256),
        vmem(BF, 8, 256, 256),
        vmem(BF, 8, 256, 256),
        vmem(BF, 80, 128),
        vmem(BF, 16, 80, 128),
        vmem(BF, 4, 512, 256),
        vmem(BF, 4, 256, 512),
        vmem(BF, 3, 4, 512, 128),
        vmem(BF, 3, 4, 256, 128),
        vmem(BF, 3, 4, 256, 128),
        vmem(BF, 3, 4, 4, 64, 128),
        vmem(BF, 3, 16, 64, 128),
        vmem(BF, 2, 64, 128),
        vmem(BF, 2, 16, 64, 128),
        vmem(BF, 2, 4, 2, 256, 128),
        vmem(BF, 2, 4, 512, 128),
        vmem(BF, 2, 16, 64, 128),
        vmem(BF, 2, 2, 5, 64, 128),
        vmem(BF, 2, 2, 4, 64, 128),
        vmem(BF, 2, 2, 2, 64, 128),
        dma((7,)), one, one, one, dma((4,)), one, dma((7,)),
        one, dma((4,)), one, one, one, one, dma((2,)), dma((2, 7)),
        dma((2,)), dma((2, 4)), dma((2,)), dma((2,)), one, one, dma((2,)), dma((2, 4)),
        dma((2,)), dma((2, 4)), dma((2,)), dma((2, 2, 2)), dma((2, 2)), dma((2, 2)),
    ]
    for width, first in ((256, (2, 16, 8, 256)), (128, (2, 8, 2, 8, 128))):
        scratch += [
            vmem(F32, *first),
            vmem(F32, 16, 8, width),
            vmem(F32, 16, 8, width),
            vmem(F32, 16, 8, width),
            vmem(BF, 16, 16, 128) if width == 256 else vmem(F32, 16, 8, width),
            vmem(F32, 2, 16, 8, width),
        ] + [one] * 10
    out, gr1, gr2 = pl.pallas_call(
        kernel,
        out_shape=(
            jax.ShapeDtypeStruct((256, 256), BF),
            jax.ShapeDtypeStruct((2, 8, 8, 256), F32),
            jax.ShapeDtypeStruct((256, 256), F32),
        ),
        in_specs=[hbm] * 7,
        out_specs=(vm, vm, vm),
        scratch_shapes=scratch,
        compiler_params=pltpu.CompilerParams(
            collective_id=0, has_side_effects=True, vmem_limit_bytes=56 * 1024 * 1024
        ),
    )(*args)
    return out, gr1.reshape(128, 256), gr2


def solution(mesh):
    in_specs = (
        P("rows", None),
        P("rows", "rep"),
        P("rows", None, "rep"),
        P("rows", None),
        P(),
        P(),
        P("rows", None),
    )
    out_specs = (P("rows", None), P(), P())
    return jax.shard_map(local, mesh=mesh, in_specs=in_specs, out_specs=out_specs, check_vma=False)
```
